32 devices in a mesh: dp: 4 (over z), fsdp: 8 (over y, x, core).
Axes of the slice: x: 2, y: 2, z: 4, core: 2. Of those that a mesh axis runs over, the one named last changes fastest.
Arguments:
- tokens: bfloat16 [4, 4096, 2048], P('dp', 'fsdp'), may hold values from -6 to 6
- summaries: bfloat16 [4, 150, 2048], P('dp', None, 'fsdp'), may hold values from -6 to 6
- segment_lengths: int32 [4, 4], P('dp'), may hold values from 0 to 2048, as said below
- pad_lengths: int32 [4], P('dp'), may hold values from 0 to 511
- output_grad: bfloat16 [4, 4096, 2048], P('dp', 'fsdp'), may hold values from -6 to 6
- norm1_gain: bfloat16 [2048], P(('dp', 'fsdp')), may hold values from 0.5 to 1.5
- norm1_bias: bfloat16 [2048], P(('dp', 'fsdp')), may hold values from -1.5 to 1.5
- query_weight: bfloat16 [2048, 2048], P(('dp', 'fsdp')), may hold values from -0.125 to 0.125
- query_bias: bfloat16 [2048], P(('dp', 'fsdp')), may hold values from -1.5 to 1.5
- key_weight: bfloat16 [2048, 2048], P(('dp', 'fsdp')), may hold values from -0.125 to 0.125
- value_weight: bfloat16 [2048, 2048], P(('dp', 'fsdp')), may hold values from -0.125 to 0.125
- value_bias: bfloat16 [2048], P(('dp', 'fsdp')), may hold values from -1.5 to 1.5
- out_weight: bfloat16 [2048, 2048], P(('dp', 'fsdp')), may hold values from -1 to 1
- out_bias: bfloat16 [2048], P(('dp', 'fsdp')), may hold values from -1.5 to 1.5
- norm2_gain: bfloat16 [2048], P(('dp', 'fsdp')), may hold values from 0.5 to 1.5
- norm2_bias: bfloat16 [2048], P(('dp', 'fsdp')), may hold values from -1.5 to 1.5
- up_weight: bfloat16 [2048, 8192], P(('dp', 'fsdp')), may hold values from -0.125 to 0.125
- up_bias: bfloat16 [8192], P(('dp', 'fsdp')), may hold values from -1.5 to 1.5
- down_weight: bfloat16 [8192, 2048], P(('dp', 'fsdp')), may hold values from -0.0625 to 0.0625
- down_bias: bfloat16 [2048], P(('dp', 'fsdp')), may hold values from -1.5 to 1.5
Outputs:
- output: bfloat16 [4, 4096, 2048], P('dp', 'fsdp')
- tokens_grad: float32 [4, 4096, 2048], P('dp', 'fsdp')
- summaries_grad: float32 [4, 150, 2048], P('dp', None, 'fsdp')
- norm1_gain_grad: float32 [2048], P(('dp', 'fsdp'))
- norm1_bias_grad: float32 [2048], P(('dp', 'fsdp'))
- query_weight_grad: float32 [2048, 2048], P(('dp', 'fsdp'))
- query_bias_grad: float32 [2048], P(('dp', 'fsdp'))
- key_weight_grad: float32 [2048, 2048], P(('dp', 'fsdp'))
- value_weight_grad: float32 [2048, 2048], P(('dp', 'fsdp'))
- value_bias_grad: float32 [2048], P(('dp', 'fsdp'))
- out_weight_grad: float32 [2048, 2048], P(('dp', 'fsdp'))
- out_bias_grad: float32 [2048], P(('dp', 'fsdp'))
- norm2_gain_grad: float32 [2048], P(('dp', 'fsdp'))
- norm2_bias_grad: float32 [2048], P(('dp', 'fsdp'))
- up_weight_grad: float32 [2048, 8192], P(('dp', 'fsdp'))
- up_bias_grad: float32 [8192], P(('dp', 'fsdp'))
- down_weight_grad: float32 [8192, 2048], P(('dp', 'fsdp'))
- down_bias_grad: float32 [2048], P(('dp', 'fsdp'))
The draws below stay inside these ranges and needn't reach their ends.
Inputs may be any that keep to these rules, and one draw needn't show every extreme that they name: `segment_lengths`: each row lists its item's segment lengths in order, each from 1024 to 2048, summing to 4096, followed by zeros; every row has two or more segments, one of them of exactly 2048 tokens. Summary rows of segments past an item's last but one are read by no query. `pad_lengths`: an item's last tokens, as many as its entry, are padding; they lie in its last segment.
All inputs are finite; a program needn't handle non-finite values.
Results may differ from the reference program's by a relative error of at most 0.012.
Values may be sent and summed in bfloat16 or wider, within the bound.
No kernel may reach another device: no remote copies, remote signals or barrier semaphores. Data moves between devices by JAX's collectives and lax.ppermute only.
A program may use at most 512 MiB of HBM per device.

```python
import math
import jax
import jax.numpy as jnp
from jax import lax

D = 2048
HEADS = 32
HEAD = 64
FF = 8192
SUMM = 50
SEG_MIN = 1024
ITEM_LEN = 4096
SEG_MAX = 2048
SEGS = 4
NSUM = 150
ITEMS = 4


def one_item(item_key):
    first_key, second_key, third_key = jax.random.split(item_key, 3)
    fewest = (ITEM_LEN + 2 * SEG_MIN - 1) // (2 * SEG_MIN)
    most_count = max(ITEM_LEN // SEG_MIN - 1, fewest)
    count = jax.random.randint(first_key, (), fewest, most_count + 1).astype(jnp.int32)
    spare = ITEM_LEN - count * SEG_MIN - SEG_MIN
    slot_keys = jax.random.split(second_key, SEGS)

    def settle(remain, inputs):
        index, slot_key = inputs
        others_left = count - 1 - index
        living = index < count - 1
        lower = jnp.maximum(0, remain - (others_left - 1) * SEG_MIN)
        upper = jnp.minimum(SEG_MIN, remain)
        extra = jax.random.randint(slot_key, (), lower, upper + 1).astype(jnp.int32)
        extra = jnp.where(living, extra, 0)
        return (remain - extra, jnp.where(living, SEG_MIN + extra, 0).astype(jnp.int32))
    _, others = lax.scan(settle, spare.astype(jnp.int32), (jnp.arange(SEGS, dtype=jnp.int32), slot_keys))
    full_place = jax.random.randint(third_key, (), 0, count).astype(jnp.int32)
    slots = jnp.arange(SEGS, dtype=jnp.int32)
    shifted = jnp.concatenate([jnp.zeros((1,), jnp.int32), others[:-1]])
    lengths = jnp.where(slots < full_place, others, jnp.where(slots == full_place, SEG_MAX, shifted))
    return lengths.astype(jnp.int32)


def draw_segment_lengths(key, part):
    item_keys = jax.random.split(jax.random.fold_in(key, 17), ITEMS)
    return jax.vmap(one_item)(item_keys)


def with_ends(drawn, own_key, least, top_value):
    longest = drawn.shape.index(max(drawn.shape))
    spots = []
    for shift in (0, 1):
        where = [jax.random.randint(jax.random.fold_in(own_key, axis), (), 0, length) for axis, length in enumerate(drawn.shape)]
        where[longest] = (where[longest] + shift) % drawn.shape[longest]
        spots.append(tuple(where))
    return drawn.at[spots[0]].set(least).at[spots[1]].set(top_value)


def steps_of(stream_key, shape, cuts, least, top_value):
    def one(dim, parts):
        steps = jax.random.uniform(jax.random.fold_in(jax.random.fold_in(stream_key, 6), dim), (parts,), jnp.float32, least / len(cuts), top_value / len(cuts))
        return jnp.repeat(jnp.exp(steps), shape[dim] // parts).reshape((-1,) + (1,) * (len(shape) - dim - 1))

    gain = one(*cuts[0])
    for cut in cuts[1:]:
        gain = gain * one(*cut)
    return gain


def noise(rng, shape, scale, bound, cuts=(), kind=jnp.bfloat16):
    loudness = steps_of(rng, shape, cuts, -0.22, 0.18) if cuts else 1.0
    values = jax.random.normal(rng, shape, jnp.float32) * scale * loudness
    return jnp.minimum(jnp.maximum(values, -bound), bound).astype(kind)


def setup_inputs(seed: int = 0) -> dict:
    streams_of = jax.random.split(jax.random.key(seed), 21)
    return {
        "tokens": noise(streams_of[0], (ITEMS, ITEM_LEN, D), 1.0, 6.0, ((0, 4), (1, 8))),
        "summaries": noise(streams_of[1], (ITEMS, NSUM, D), 1.0, 6.0, ((0, 4), (2, 8))),
        "segment_lengths": draw_segment_lengths(jax.random.fold_in(streams_of[20], 71), 0),
        "pad_lengths": with_ends(jax.random.randint(streams_of[3], (ITEMS,), 0, SEG_MIN // 2), jax.random.fold_in(streams_of[3], 1), 0, (SEG_MIN // 2) - 1).astype(jnp.int32),
        "output_grad": noise(streams_of[4], (ITEMS, ITEM_LEN, D), 1.0, 6.0, ((0, 4), (1, 8))),
        "norm1_gain": jnp.clip(1.0 + 0.1 * jax.random.normal(streams_of[5], (D,), jnp.float32), 0.5, 1.5).astype(jnp.bfloat16),
        "norm1_bias": noise(streams_of[6], (D,), 0.3, 1.5, ((0, 32),)),
        "query_weight": noise(streams_of[7], (D, D), D ** -0.5, 0.125, ((0, 32),)),
        "query_bias": noise(streams_of[8], (D,), 0.3, 1.5, ((0, 32),)),
        "key_weight": noise(streams_of[9], (D, D), D ** -0.5, 0.125, ((0, 32),)),
        "value_weight": noise(streams_of[10], (D, D), D ** -0.5, 0.125, ((0, 32),)),
        "value_bias": noise(streams_of[11], (D,), 0.3, 1.5, ((0, 32),)),
        "out_weight": noise(streams_of[12], (D, D), (D // 64) ** -0.5, 1.0, ((0, 32),)),
        "out_bias": noise(streams_of[13], (D,), 0.3, 1.5, ((0, 32),)),
        "norm2_gain": jnp.clip(1.0 + 0.1 * jax.random.normal(streams_of[14], (D,), jnp.float32), 0.5, 1.5).astype(jnp.bfloat16),
        "norm2_bias": noise(streams_of[15], (D,), 0.3, 1.5, ((0, 32),)),
        "up_weight": noise(streams_of[16], (D, FF), D ** -0.5, 0.125, ((0, 32),)),
        "up_bias": noise(streams_of[17], (FF,), 0.3, 1.5, ((0, 32),)),
        "down_weight": noise(streams_of[18], (FF, D), FF ** -0.5, 0.0625, ((0, 32),)),
        "down_bias": noise(streams_of[19], (D,), 0.3, 1.5, ((0, 32),)),
    }


@jax.custom_vjp
def low(v):
    return lax.optimization_barrier(v.astype(jnp.bfloat16)).astype(jnp.float32)

@jax.custom_vjp
def low_back(v):
    return v

def low_keep(v):
    return (low(v), None)

def low_pass(kept, grad):
    return (grad,)

def back_keep(v):
    return (v, None)

def back_low(kept, grad):
    return (low(grad),)
low.defvjp(low_keep, low_pass)
low_back.defvjp(back_keep, back_low)
epsilon = 1e-05
masked_score = -1e+30
highest = lax.Precision.HIGHEST

def layer_norm(values, gains, shifts):
    centre = lax.optimization_barrier(jnp.mean(values, axis=-1, keepdims=True))
    centred = values - centre
    spread = lax.optimization_barrier(jnp.mean(centred * centred, axis=-1, keepdims=True))
    return centred * lax.rsqrt(spread + epsilon) * gains + shifts

def product(left, right):
    return jnp.dot(left, right, precision=highest, preferred_element_type=jnp.float32)

def segment_of(lengths, places):
    bounds = jnp.cumsum(lengths).astype(jnp.int32)
    return lax.optimization_barrier(jnp.sum((places[:, None] >= bounds[None, :]).astype(jnp.int32), axis=1))

def visibility(query_places, key_places, lengths, padding, summary_rows, item_length):
    query_segment = segment_of(lengths, query_places)
    key_segment = segment_of(lengths, key_places)
    same = (key_segment[None, :] == query_segment[:, None]) & (key_places[None, :] <= query_places[:, None])
    living = (key_places[None, :] < item_length - padding) | (key_places[None, :] == query_places[:, None])
    summary_segment = jnp.arange(summary_rows, dtype=jnp.int32) // SUMM
    earlier = summary_segment[None, :] < query_segment[:, None]
    return jnp.concatenate([earlier, same & living], axis=1)

def forward_item(params, inputs, summ, lengths, padding):
    norm1_gain, norm1_bias, query_weight, query_bias, key_weight, value_weight, value_bias, out_weight, out_bias, norm2_gain, norm2_bias, up_weight, up_bias, down_weight, down_bias = params
    normed = low(layer_norm(inputs, norm1_gain, norm1_bias))
    normed_summ = low(layer_norm(summ, norm1_gain, norm1_bias))
    queries = low(low_back(product(normed, query_weight) + query_bias))
    keys = low(low_back(product(normed, key_weight)))
    values = low(low_back(product(normed, value_weight) + value_bias))
    summ_keys = low(low_back(product(normed_summ, key_weight)))
    summ_values = low(low_back(product(normed_summ, value_weight) + value_bias))
    key_rows = jnp.concatenate([summ_keys, keys], axis=0).reshape(-1, HEADS, HEAD)
    value_rows = jnp.concatenate([summ_values, values], axis=0).reshape(-1, HEADS, HEAD)
    block = min(512, ITEM_LEN)
    scale = 1.0 / math.sqrt(HEAD)
    key_places = jnp.arange(ITEM_LEN, dtype=jnp.int32)

    def attend(start):
        rows = lax.dynamic_slice_in_dim(queries, start, block, 0).reshape(block, HEADS, HEAD)
        places = start + jnp.arange(block, dtype=jnp.int32)
        mask = visibility(places, key_places, lengths, padding, NSUM, ITEM_LEN)
        scores = jnp.einsum('qhd,khd->hqk', rows, key_rows, precision=highest) * scale
        scores = low_back(scores)
        scores = jnp.where(mask[None], scores, masked_score)
        probs = low(jax.nn.softmax(scores, axis=-1))
        mixed = jnp.einsum('hqk,khd->qhd', probs, value_rows, precision=highest)
        return mixed.reshape(block, D)
    starts = jnp.arange(ITEM_LEN // block, dtype=jnp.int32) * block
    attn = lax.map(jax.checkpoint(attend), starts).reshape(ITEM_LEN, D)
    attn = low(low_back(attn))
    resid = inputs + low_back(product(attn, out_weight) + out_bias)
    normed2 = low(layer_norm(resid, norm2_gain, norm2_bias))
    upper = low_back(product(normed2, up_weight) + up_bias)
    active = low(jax.nn.gelu(upper, approximate=True))
    return resid + product(active, down_weight) + down_bias

def reference(tokens, summaries, segment_lengths, pad_lengths, output_grad, norm1_gain, norm1_bias, query_weight, query_bias, key_weight, value_weight, value_bias, out_weight, out_bias, norm2_gain, norm2_bias, up_weight, up_bias, down_weight, down_bias):
    params = tuple(jax.tree.map(lambda array: array.astype(jnp.float32), [norm1_gain, norm1_bias, query_weight, query_bias, key_weight, value_weight, value_bias, out_weight, out_bias, norm2_gain, norm2_bias, up_weight, up_bias, down_weight, down_bias]))

    def per_item(totals, item):
        item_tokens, item_summ, item_lengths, item_pad, item_grad = item

        def forward(weights, inputs, summ):
            return forward_item(weights, inputs, summ, item_lengths, item_pad)
        result, pull = jax.vjp(forward, params, item_tokens.astype(jnp.float32), item_summ.astype(jnp.float32))
        weight_grads, input_grad, summ_grad = pull(item_grad.astype(jnp.float32))
        totals = jax.tree.map(jnp.add, totals, weight_grads)
        return (totals, (result.astype(jnp.bfloat16), input_grad, summ_grad))
    zeros = jax.tree.map(jnp.zeros_like, params)
    totals, (outputs, input_grads, summ_grads) = lax.scan(per_item, zeros, (tokens, summaries, segment_lengths, pad_lengths, output_grad))
    return (outputs, input_grads, summ_grads, totals[0], totals[1], totals[2], totals[3], totals[4], totals[5], totals[6], totals[7], totals[8], totals[9], totals[10], totals[11], totals[12], totals[13], totals[14])
```

```python
import functools
import math

import jax
import jax.numpy as jnp
from jax import lax
from jax.experimental import pallas as pl
from jax.experimental.pallas import tpu as pltpu
from jax.sharding import PartitionSpec as P

HEAD = 64
SUMM = 50

epsilon = 1e-05
masked_score = -1e30
bf16 = jnp.bfloat16
f32 = jnp.float32
BOTH = ("dp", "fsdp")
score_scale = 1.0 / math.sqrt(HEAD)

ROWS_BY_ROWS = (((1,), (0,)), ((), ()))
ROWS_BY_COLS = (((1,), (1,)), ((), ()))
COLS_BY_ROWS = (((0,), (0,)), ((), ()))


def dot(left, right, dims):
    return lax.dot_general(left, right, dims, preferred_element_type=f32)


def layer_norm(values, gains, shifts):
    centre = jnp.mean(values, axis=-1, keepdims=True)
    centred = values - centre
    spread = jnp.mean(centred * centred, axis=-1, keepdims=True)
    return centred * lax.rsqrt(spread + epsilon) * gains + shifts


def gelu_tanh(values):
    return jax.nn.gelu(values, approximate=True)


def swapped(x, bit):
    devices = lax.axis_size("fsdp")
    return lax.ppermute(x, "fsdp", [(i, i ^ bit) for i in range(devices)])


def gathered(own):
    devices = lax.axis_size("fsdp")
    if devices != 8:
        pieces = [own]
        bit = 1
        while bit < devices:
            pieces = pieces + [swapped(piece, bit) for piece in pieces]
            bit *= 2
        return pieces
    half = own.shape[0] // 2
    along_x = swapped(own, 2)
    along_y = swapped(own, 4)
    mate = swapped(own, 1)
    across = jnp.concatenate([swapped(along_x[:half], 4), swapped(along_y[half:], 2)], axis=0)
    return [
        own,
        mate,
        along_x,
        swapped(along_x, 1),
        along_y,
        swapped(along_y, 1),
        across,
        swapped(across, 1),
    ]


def summed_low(left, right):
    return (left.astype(f32) + right.astype(f32)).astype(bf16)


def scattered_sum(pieces):
    devices = len(pieces)
    if devices != 8:
        bit = devices // 2
        while bit > 1:
            pieces = [summed_low(pieces[m], swapped(pieces[m + bit], bit)) for m in range(bit)]
            bit //= 2
        return pieces[0].astype(f32) + swapped(pieces[1], 1).astype(f32)
    half = pieces[0].shape[0] // 2
    across = summed_low(pieces[6], swapped(pieces[7], 1))
    along_x = summed_low(pieces[2], swapped(pieces[3], 1))
    along_y = summed_low(pieces[4], swapped(pieces[5], 1))
    upper_part = swapped(across[:half], 4)
    lower_part = swapped(across[half:], 2)
    along_x = jnp.concatenate([summed_low(along_x[:half], upper_part), along_x[half:]], axis=0)
    along_y = jnp.concatenate([along_y[:half], summed_low(along_y[half:], lower_part)], axis=0)
    return (
        (pieces[0].astype(f32) + swapped(pieces[1], 1).astype(f32))
        + swapped(along_x, 2).astype(f32)
        + swapped(along_y, 4).astype(f32)
    )


def only_head(values, head):
    columns = lax.broadcasted_iota(jnp.int32, values.shape, 1) // HEAD
    return jnp.where(columns == head, values, jnp.zeros_like(values))


def attn_forward_kernel(
    block, heads, plan_ref, q_ref, k_ref, vt_ref, sk_ref, svt_ref, row_ref, o_ref, log_ref,
    q_heads, tops, sums, mixed,
):
    i = pl.program_id(0)
    blocks = pl.num_programs(0)
    q = q_ref[...].astype(f32) * score_scale
    for h in range(heads):
        q_heads[h] = only_head(q, h).astype(bf16)
    tops[...] = jnp.full_like(tops, masked_score)
    sums[...] = jnp.zeros_like(sums)
    mixed[...] = jnp.zeros_like(mixed)
    lowest = row_ref[0:1, :]
    highest = row_ref[1:2, :]
    summ_end = row_ref[2:3, :]
    me = row_ref[3:4, :]

    def step(keys, values_t, mask):
        each = range(heads)
        scores = [dot(keys, q_heads[h], ROWS_BY_COLS) for h in each]
        if mask is not None:
            scores = [jnp.where(mask, one, masked_score) for one in scores]
        before = [tops[h : h + 1, :] for h in each]
        top = [jnp.maximum(before[h], jnp.max(scores[h], axis=0, keepdims=True)) for h in each]
        weights = [jnp.exp(scores[h] - top[h]) for h in each]
        keep = [jnp.exp(before[h] - top[h]) for h in each]
        added = [jnp.sum(weights[h], axis=0, keepdims=True) for h in each]
        totals = [keep[h] * sums[h : h + 1, :] + added[h] for h in each]
        part_of = [slice(h * HEAD, (h + 1) * HEAD) for h in each]
        more = [dot(values_t[part_of[h], :], weights[h].astype(bf16), ROWS_BY_ROWS) for h in each]
        result = [keep[h] * mixed[part_of[h], :] + more[h] for h in each]
        for h in each:
            tops[h : h + 1, :] = top[h]
            sums[h : h + 1, :] = totals[h]
            mixed[part_of[h], :] = result[h]

    @pl.when(plan_ref[2 * blocks + i] > 0)
    def _():
        places = lax.broadcasted_iota(jnp.int32, (sk_ref.shape[0], block), 0)
        step(sk_ref[...], svt_ref[...], places < summ_end)

    def whole(j, carry):
        start = pl.multiple_of(j * block, block)
        step(k_ref[pl.ds(start, block), :], vt_ref[:, pl.ds(start, block)], None)
        return carry

    def part(j, carry):
        start = pl.multiple_of(j * block, block)
        places = start + lax.broadcasted_iota(jnp.int32, (block, block), 0)
        mask = ((places >= lowest) & (places <= highest)) | (places == me)
        step(k_ref[pl.ds(start, block), :], vt_ref[:, pl.ds(start, block)], mask)
        return carry

    lax.fori_loop(plan_ref[i], plan_ref[blocks + i], whole, 0)
    lax.fori_loop(plan_ref[blocks + i], i + 1, part, 0)
    for h in range(heads):
        r = slice(h * HEAD, (h + 1) * HEAD)
        mixed[r, :] = mixed[r, :] * (1.0 / sums[h : h + 1, :])
    log_ref[...] = tops[...] + jnp.log(jnp.maximum(sums[...], 1e-37))
    o_ref[...] = mixed[...].T.astype(bf16)


def attn_backward_kernel(
    block, heads, plan_ref, q_ref, k_ref, v_ref, kt_ref, sk_ref, sv_ref, skt_ref, row_ref, log_ref,
    o_ref, do_ref, dq_ref, dk_ref, dv_ref, dsk_ref, dsv_ref, q_heads, do_heads, dq_sum, dk_sum,
    dv_sum, dsk_sum, dsv_sum,
):
    i = pl.program_id(0)
    blocks = pl.num_programs(0)

    @pl.when(i == 0)
    def _():
        dk_sum[...] = jnp.zeros_like(dk_sum)
        dv_sum[...] = jnp.zeros_like(dv_sum)
        dsk_sum[...] = jnp.zeros_like(dsk_sum)
        dsv_sum[...] = jnp.zeros_like(dsv_sum)

    q = q_ref[...].astype(f32) * score_scale
    do = do_ref[...].astype(f32)
    for h in range(heads):
        q_heads[h] = only_head(q, h).astype(bf16)
        do_heads[h] = only_head(do, h).astype(bf16)
    both_t = (do * o_ref[...].astype(f32)).T
    row_terms = [
        jnp.sum(both_t[h * HEAD : (h + 1) * HEAD, :], axis=0, keepdims=True) for h in range(heads)
    ]
    dq_sum[...] = jnp.zeros_like(dq_sum)
    lowest = row_ref[0:1, :]
    highest = row_ref[1:2, :]
    summ_end = row_ref[2:3, :]
    me = row_ref[3:4, :]

    def step(keys, values, keys_t, mask, dk_at, dv_at):
        dk = dv = None
        for h in range(heads):
            scores = dot(keys, q_heads[h], ROWS_BY_COLS)
            if mask is not None:
                scores = jnp.where(mask, scores, masked_score)
            probs = jnp.exp(scores - log_ref[h : h + 1, :])
            grad_probs = dot(values, do_heads[h], ROWS_BY_COLS)
            grad_scores = (probs * (grad_probs - row_terms[h])).astype(bf16)
            r = slice(h * HEAD, (h + 1) * HEAD)
            dq_sum[r, :] += dot(keys_t[r, :], grad_scores, ROWS_BY_ROWS)
            dv_own = dot(probs.astype(bf16), do_heads[h], ROWS_BY_ROWS)
            dk_own = dot(grad_scores, q_heads[h], ROWS_BY_ROWS)
            dv = dv_own if dv is None else dv + dv_own
            dk = dk_own if dk is None else dk + dk_own
        dk_at[...] += dk
        dv_at[...] += dv

    @pl.when(plan_ref[2 * blocks + i] > 0)
    def _():
        places = lax.broadcasted_iota(jnp.int32, (sk_ref.shape[0], block), 0)
        step(sk_ref[...], sv_ref[...], skt_ref[...], places < summ_end, dsk_sum, dsv_sum)

    def whole(j, carry):
        d = pl.ds(pl.multiple_of(j * block, block), block)
        step(k_ref[d, :], v_ref[d, :], kt_ref[:, d], None, dk_sum.at[d, :], dv_sum.at[d, :])
        return carry

    def part(j, carry):
        start = pl.multiple_of(j * block, block)
        d = pl.ds(start, block)
        places = start + lax.broadcasted_iota(jnp.int32, (block, block), 0)
        mask = ((places >= lowest) & (places <= highest)) | (places == me)
        step(k_ref[d, :], v_ref[d, :], kt_ref[:, d], mask, dk_sum.at[d, :], dv_sum.at[d, :])
        return carry

    lax.fori_loop(plan_ref[i], plan_ref[blocks + i], whole, 0)
    lax.fori_loop(plan_ref[blocks + i], i + 1, part, 0)
    dq_ref[...] = (dq_sum[...] * score_scale).T.astype(bf16)

    @pl.when(i == blocks - 1)
    def _():
        dk_ref[...] = dk_sum[...].astype(bf16)
        dv_ref[...] = dv_sum[...].astype(bf16)
        dsk_ref[...] = dsk_sum[...].astype(bf16)
        dsv_ref[...] = dsv_sum[...].astype(bf16)


def held(shape):
    return pl.BlockSpec(shape, lambda i, *_: (0, 0))


def attn_forward(plan, rows, q, k, v_t, sk, sv_t, block):
    count, width = q.shape
    heads = width // HEAD
    by_rows = pl.BlockSpec((block, width), lambda i, *_: (i, 0))
    by_cols = pl.BlockSpec((8, block), lambda i, *_: (0, i))
    pairs = count * count // 4
    return pl.pallas_call(
        functools.partial(attn_forward_kernel, block, heads),
        grid_spec=pltpu.PrefetchScalarGridSpec(
            num_scalar_prefetch=1,
            grid=(count // block,),
            in_specs=[by_rows, held(k.shape), held(v_t.shape), held(sk.shape), held(sv_t.shape), by_cols],
            out_specs=[by_rows, by_cols],
            scratch_shapes=[
                pltpu.VMEM((heads, block, width), bf16),
                pltpu.VMEM((8, block), f32),
                pltpu.VMEM((8, block), f32),
                pltpu.VMEM((width, block), f32),
            ],
        ),
        out_shape=[
            jax.ShapeDtypeStruct((count, width), bf16),
            jax.ShapeDtypeStruct((8, count), f32),
        ],
        compiler_params=pltpu.CompilerParams(
            dimension_semantics=("arbitrary",), vmem_limit_bytes=32 * 2**20
        ),
        cost_estimate=pl.CostEstimate(
            flops=16 * pairs * width, bytes_accessed=8 * count * width, transcendentals=pairs * heads
        ),
        name="attn_forward",
    )(plan, q, k, v_t, sk, sv_t, rows)


def attn_backward(plan, rows, q, k, v, k_t, sk, sv, sk_t, logs, o, do, block):
    count, width = q.shape
    heads = width // HEAD
    by_rows = pl.BlockSpec((block, width), lambda i, *_: (i, 0))
    by_cols = pl.BlockSpec((8, block), lambda i, *_: (0, i))
    pairs = count * count // 4
    long = jax.ShapeDtypeStruct((count, width), bf16)
    short = jax.ShapeDtypeStruct(sk.shape, bf16)
    return pl.pallas_call(
        functools.partial(attn_backward_kernel, block, heads),
        grid_spec=pltpu.PrefetchScalarGridSpec(
            num_scalar_prefetch=1,
            grid=(count // block,),
            in_specs=[
                by_rows, held(k.shape), held(v.shape), held(k_t.shape), held(sk.shape),
                held(sv.shape), held(sk_t.shape), by_cols, by_cols, by_rows, by_rows,
            ],
            out_specs=[by_rows, held(k.shape), held(v.shape), held(sk.shape), held(sv.shape)],
            scratch_shapes=[
                pltpu.VMEM((heads, block, width), bf16),
                pltpu.VMEM((heads, block, width), bf16),
                pltpu.VMEM((width, block), f32),
                pltpu.VMEM((count, width), f32),
                pltpu.VMEM((count, width), f32),
                pltpu.VMEM(sk.shape, f32),
                pltpu.VMEM(sv.shape, f32),
            ],
        ),
        out_shape=[long, long, long, short, short],
        compiler_params=pltpu.CompilerParams(
            dimension_semantics=("arbitrary",), vmem_limit_bytes=48 * 2**20
        ),
        cost_estimate=pl.CostEstimate(
            flops=24 * pairs * width, bytes_accessed=20 * count * width, transcendentals=pairs * heads
        ),
        name="attn_backward",
    )(plan, q, k, v, k_t, sk, sv, sk_t, rows, logs, o, do)


def attention_plan(lengths, padding, count, block):
    places = jnp.arange(count, dtype=jnp.int32)
    ends = jnp.cumsum(lengths)
    passed = places[:, None] >= ends[None, :]
    segment = jnp.sum(passed.astype(jnp.int32), axis=1)
    lowest = jnp.max(jnp.where(passed, ends[None, :], 0), axis=1)
    living = count - padding
    highest = jnp.minimum(places, living - 1)
    nothing = jnp.zeros_like(places)
    rows = jnp.stack(
        [lowest, highest, segment * SUMM, places, nothing, nothing, nothing, nothing], axis=0
    )
    blocks = count // block
    starts = jnp.arange(blocks, dtype=jnp.int32) * block
    first = lowest.reshape(blocks, block)[:, 0] // block
    one_piece = lowest.reshape(blocks, block)[:, -1] <= first * block
    whole_end = jnp.maximum(jnp.minimum(starts, living) // block, first)
    split = jnp.where(one_piece, whole_end, first)
    summ_flag = (segment.reshape(blocks, block)[:, -1] > 0).astype(jnp.int32)
    return rows, jnp.concatenate([first, split, summ_flag]).astype(jnp.int32)


def per_device(
    tokens,
    summaries,
    segment_lengths,
    pad_lengths,
    output_grad,
    norm1_gain,
    norm1_bias,
    query_weight,
    query_bias,
    key_weight,
    value_weight,
    value_bias,
    out_weight,
    out_bias,
    norm2_gain,
    norm2_bias,
    up_weight,
    up_bias,
    down_weight,
    down_bias,
):
    shards = lax.axis_size("fsdp")
    items = lax.axis_size("dp")
    devices = shards * items
    position = lax.axis_index("fsdp")
    tok_rows = tokens.shape[1]
    width = tokens.shape[2]
    count = tok_rows * shards
    own_width = width // shards
    rows_held = query_weight.shape[0]
    units_held = up_bias.shape[0]
    own_units = units_held * items
    hidden = units_held * devices
    summary_rows = summaries.shape[1]
    padded_summ = -(-summary_rows // 32) * 32
    spread = rows_held % HEAD == 0
    block = math.gcd(count, 512)

    def for_shards(weight):
        if spread:
            split = weight.reshape(rows_held, items, shards, rows_held)
            return split.transpose(2, 0, 1, 3).reshape(shards, rows_held, own_width)
        return weight.reshape(rows_held, shards, own_width).transpose(1, 0, 2)

    def from_shards(parts):
        if spread:
            split = parts.reshape(shards, rows_held, items, rows_held)
            return split.transpose(1, 2, 0, 3).reshape(rows_held, width)
        return parts.transpose(1, 0, 2).reshape(rows_held, width)

    def own_columns(vector):
        if spread:
            split = vector.reshape(items, shards, rows_held)
            return lax.dynamic_index_in_dim(split, position, 1, keepdims=False).reshape(own_width)
        return lax.dynamic_slice_in_dim(vector, position * own_width, own_width, 0)

    def whole_columns(vector):
        if spread:
            split = jnp.zeros((items, shards, rows_held), f32)
            return lax.dynamic_update_index_in_dim(
                split, vector.reshape(items, 1, rows_held), position, 1
            ).reshape(width)
        return lax.dynamic_update_slice_in_dim(
            jnp.zeros((width,), f32), vector, position * own_width, 0
        )

    token_pieces = gathered(tokens[0])
    vectors = jnp.concatenate(
        [
            norm1_gain, norm1_bias, query_bias, value_bias, out_bias, norm2_gain, norm2_bias,
            down_bias, up_bias,
        ]
    ).astype(f32)
    vectors = lax.all_to_all(
        jnp.broadcast_to(vectors[None], (devices, vectors.shape[0])), BOTH, 0, 0, tiled=True
    )
    gain_one, shift_one, query_shift, value_shift, out_shift, gain_two, shift_two, down_shift = (
        vectors[:, n * rows_held : (n + 1) * rows_held].reshape(width) for n in range(8)
    )
    up_shift = lax.dynamic_index_in_dim(
        vectors[:, 8 * rows_held :].reshape(items, shards, units_held), position, 1, keepdims=False
    ).reshape(own_units)
    query_shift = own_columns(query_shift)
    value_shift = own_columns(value_shift)

    qkv_parts = jnp.concatenate(
        [for_shards(query_weight), for_shards(key_weight), for_shards(value_weight)], axis=2
    )
    qkv_parts = lax.all_to_all(qkv_parts, "fsdp", 0, 0, tiled=True)
    qkv_own = lax.all_gather(
        qkv_parts.reshape(shards * rows_held, 3 * own_width), "dp", axis=0, tiled=True
    )
    if spread:
        out_own = lax.all_gather(out_weight, "dp", axis=0, tiled=True)
    else:
        out_own = lax.dynamic_slice_in_dim(
            lax.all_gather(out_weight, BOTH, axis=0, tiled=True), position * own_width, own_width, 0
        )
    up_parts = up_weight.reshape(rows_held, items, shards, units_held).transpose(2, 0, 1, 3)
    up_parts = lax.all_to_all(
        up_parts.reshape(shards, rows_held, own_units), "fsdp", 0, 0, tiled=True
    )
    up_own = lax.all_gather(
        up_parts.reshape(shards * rows_held, own_units), "dp", axis=0, tiled=True
    )
    down_own = lax.all_gather(down_weight, "dp", axis=0, tiled=True)
    summ_full = lax.all_to_all(
        jnp.broadcast_to(summaries, (shards,) + summaries.shape[1:]), "fsdp", 0, 0, tiled=True
    )
    summ_full = summ_full.transpose(1, 0, 2).reshape(summary_rows, width)
    summ_inputs = jnp.pad(summ_full, ((0, padded_summ - summary_rows), (0, 0))).astype(f32)

    def start_of(m):
        return (position ^ m) * tok_rows

    def in_place(whole, piece, m):
        return lax.dynamic_update_slice(whole, piece, (start_of(m), 0))

    def in_order(whole):
        return [lax.dynamic_slice_in_dim(whole, start_of(m), tok_rows, 0) for m in range(shards)]

    normed = jnp.zeros((count, width), bf16)
    for m, piece in enumerate(token_pieces):
        normed = in_place(normed, layer_norm(piece.astype(f32), gain_one, shift_one).astype(bf16), m)
    normed_summ = layer_norm(summ_inputs, gain_one, shift_one).astype(bf16)
    query_own = qkv_own[:, :own_width]
    key_own = qkv_own[:, own_width : 2 * own_width]
    value_own = qkv_own[:, 2 * own_width :]
    queries = (dot(normed, query_own, ROWS_BY_ROWS) + query_shift).astype(bf16)
    keys = dot(normed, key_own, ROWS_BY_ROWS).astype(bf16)
    values = (dot(normed, value_own, ROWS_BY_ROWS) + value_shift).astype(bf16)
    summ_keys = dot(normed_summ, key_own, ROWS_BY_ROWS).astype(bf16)
    summ_values = (dot(normed_summ, value_own, ROWS_BY_ROWS) + value_shift).astype(bf16)
    rows, plan = attention_plan(segment_lengths[0], pad_lengths[0], count, block)
    attn, logs = attn_forward(
        plan, rows, queries, keys, values.T, summ_keys, summ_values.T, block
    )
    attn_pieces = in_order(attn)
    inputs = tokens[0].astype(f32)
    proj_sum = scattered_sum(
        [dot(piece, out_own, ROWS_BY_ROWS).astype(bf16) for piece in attn_pieces]
    )
    resid = inputs + proj_sum + out_shift

    normed_two_own = layer_norm(resid, gain_two, shift_two).astype(bf16)
    grad_pieces = gathered(output_grad[0])
    grad_rows = jnp.concatenate(grad_pieces, axis=0)
    normed_two = jnp.concatenate(gathered(normed_two_own), axis=0)
    upper = dot(normed_two, up_own, ROWS_BY_ROWS) + up_shift
    active = gelu_tanh(upper).astype(bf16)

    def cut(whole):
        return [whole[m * tok_rows : (m + 1) * tok_rows] for m in range(shards)]

    grad_active = dot(grad_rows, down_own, ROWS_BY_COLS)
    _, gelu_pull = jax.vjp(gelu_tanh, upper)
    grad_upper = gelu_pull(grad_active)[0].astype(bf16)
    grad_normed_two = scattered_sum(
        [dot(piece, up_own, ROWS_BY_COLS).astype(bf16) for piece in cut(grad_upper)]
    )
    result = scattered_sum(
        [dot(piece, down_own, ROWS_BY_ROWS).astype(bf16) for piece in cut(active)]
    )
    result = (resid + result + down_shift).astype(bf16)
    down_grad = dot(active, grad_rows, COLS_BY_ROWS).astype(bf16)
    down_grad = lax.psum_scatter(down_grad, "dp", scatter_dimension=0, tiled=True).astype(f32)
    up_grad = dot(normed_two, grad_upper, COLS_BY_ROWS).astype(bf16)
    up_grad = lax.psum_scatter(up_grad, "dp", scatter_dimension=0, tiled=True)
    up_grad = lax.all_to_all(
        up_grad.reshape(shards, rows_held, own_units), "fsdp", 0, 0, tiled=True
    )
    up_grad = up_grad.reshape(shards, rows_held, items, units_held).transpose(1, 2, 0, 3)
    up_grad = up_grad.reshape(rows_held, hidden).astype(f32)
    up_shift_grad = jnp.sum(grad_upper.astype(f32), axis=0)
    grad_floats = output_grad[0].astype(f32)
    down_shift_grad = jnp.sum(grad_floats, axis=0)
    _, norm_two_pull = jax.vjp(layer_norm, resid, gain_two, shift_two)
    grad_resid, gain_two_grad, shift_two_grad = norm_two_pull(grad_normed_two)
    grad_resid = grad_resid + grad_floats

    grad_proj = grad_resid.astype(bf16)
    out_shift_grad = jnp.sum(grad_proj.astype(f32), axis=0)
    proj_pieces = gathered(grad_proj)
    grad_attn = jnp.zeros((count, own_width), bf16)
    for m, piece in enumerate(proj_pieces):
        grad_attn = in_place(grad_attn, dot(piece, out_own, ROWS_BY_COLS).astype(bf16), m)
    out_grad = dot(
        jnp.concatenate(attn_pieces, axis=0), jnp.concatenate(proj_pieces, axis=0), COLS_BY_ROWS
    ).astype(bf16)
    if spread:
        out_grad = lax.psum_scatter(out_grad, "dp", scatter_dimension=0, tiled=True)
    else:
        out_grad = lax.psum_scatter(
            lax.dynamic_update_slice_in_dim(
                jnp.zeros((width, width), bf16), out_grad, position * own_width, 0
            ),
            BOTH,
            scatter_dimension=0,
            tiled=True,
        )
    out_grad = out_grad.astype(f32)
    grad_queries, grad_keys, grad_values, grad_summ_keys, grad_summ_values = attn_backward(
        plan, rows, queries, keys, values, keys.T, summ_keys, summ_values, summ_keys.T, logs, attn,
        grad_attn, block,
    )
    grad_qkv = jnp.concatenate([grad_queries, grad_keys, grad_values], axis=1)
    grad_summ_kv = jnp.concatenate([grad_summ_keys, grad_summ_values], axis=1)
    grad_normed = scattered_sum(
        [dot(piece, qkv_own, ROWS_BY_COLS).astype(bf16) for piece in in_order(grad_qkv)]
    )
    kv_own = qkv_own[:, own_width:]
    summ_share = -(-padded_summ // (shards * 16)) * 16
    grad_normed_summ = dot(grad_summ_kv, kv_own, ROWS_BY_COLS).astype(bf16)
    grad_normed_summ = jnp.pad(
        grad_normed_summ, ((0, summ_share * shards - padded_summ), (0, 0))
    ).reshape(shards, summ_share, width)
    grad_normed_summ = lax.all_to_all(grad_normed_summ, "fsdp", 0, 0, tiled=True)
    grad_normed_summ = jnp.sum(grad_normed_summ.astype(f32), axis=0)
    summ_own = lax.dynamic_slice_in_dim(
        jnp.pad(summ_inputs, ((0, summ_share * shards - padded_summ), (0, 0))),
        position * summ_share,
        summ_share,
        0,
    )
    qkv_grad = dot(normed, grad_qkv, COLS_BY_ROWS)
    summ_kv_grad = dot(normed_summ, grad_summ_kv, COLS_BY_ROWS)
    qkv_grad = qkv_grad + jnp.pad(summ_kv_grad, ((0, 0), (own_width, 0)))
    qkv_grad = lax.psum_scatter(qkv_grad.astype(bf16), "dp", scatter_dimension=0, tiled=True)
    qkv_grad = lax.all_to_all(
        qkv_grad.reshape(shards, rows_held, 3 * own_width), "fsdp", 0, 0, tiled=True
    )
    query_grad, key_grad, value_grad = (
        from_shards(qkv_grad[:, :, n * own_width : (n + 1) * own_width]).astype(f32)
        for n in range(3)
    )
    query_shift_grad = jnp.sum(grad_queries.astype(f32), axis=0)
    value_shift_grad = jnp.sum(grad_values.astype(f32), axis=0) + jnp.sum(
        grad_summ_values.astype(f32), axis=0
    )
    _, norm_one_pull = jax.vjp(layer_norm, inputs, gain_one, shift_one)
    grad_inputs, gain_one_grad, shift_one_grad = norm_one_pull(grad_normed)
    grad_inputs = grad_inputs + grad_resid
    _, norm_summ_pull = jax.vjp(layer_norm, summ_own, gain_one, shift_one)
    grad_summ, gain_summ_grad, shift_summ_grad = norm_summ_pull(grad_normed_summ)
    summary_cols = summaries.shape[2]
    grad_summ = lax.all_to_all(
        grad_summ.reshape(summ_share, shards, summary_cols).transpose(1, 0, 2),
        "fsdp",
        0,
        0,
        tiled=True,
    )
    summary_grad = grad_summ.reshape(shards * summ_share, summary_cols)[:summary_rows]

    vector_grads = jnp.stack(
        [
            gain_one_grad + gain_summ_grad,
            shift_one_grad + shift_summ_grad,
            whole_columns(query_shift_grad),
            whole_columns(value_shift_grad),
            out_shift_grad,
            gain_two_grad,
            shift_two_grad,
            down_shift_grad,
        ]
    )
    vector_grads = vector_grads.reshape(8, devices, rows_held).transpose(1, 0, 2)
    unit_grads = lax.dynamic_update_index_in_dim(
        jnp.zeros((items, shards, units_held), f32),
        up_shift_grad.reshape(items, 1, units_held),
        position,
        1,
    )
    all_grads = jnp.concatenate(
        [vector_grads.reshape(devices, 8 * rows_held), unit_grads.reshape(devices, units_held)],
        axis=1,
    )
    all_grads = jnp.sum(lax.all_to_all(all_grads, BOTH, 0, 0, tiled=True), axis=0)
    (
        gain_one_grad, shift_one_grad, query_shift_grad, value_shift_grad, out_shift_grad,
        gain_two_grad, shift_two_grad, down_shift_grad,
    ) = (all_grads[n * rows_held : (n + 1) * rows_held] for n in range(8))
    up_shift_grad = all_grads[8 * rows_held :]
    return (
        result[None],
        grad_inputs[None],
        summary_grad[None],
        gain_one_grad,
        shift_one_grad,
        query_grad,
        query_shift_grad,
        key_grad,
        value_grad,
        value_shift_grad,
        out_grad,
        out_shift_grad,
        gain_two_grad,
        shift_two_grad,
        up_grad,
        up_shift_grad,
        down_grad,
        down_shift_grad,
    )


def solution(mesh):
    vector = P(BOTH)
    matrix = P(BOTH, None)
    rows = P("dp", "fsdp", None)
    columns = P("dp", None, "fsdp")
    return jax.shard_map(
        per_device,
        mesh=mesh,
        in_specs=(
            rows, columns, P("dp", None), P("dp"), rows, vector, vector, matrix, vector, matrix,
            matrix, vector, matrix, vector, vector, vector, matrix, vector, matrix, vector,
        ),
        out_specs=(
            rows, rows, columns, vector, vector, matrix, vector, matrix, matrix, vector, matrix,
            vector, vector, vector, matrix, vector, matrix, vector,
        ),
        check_vma=False,
    )
```

```python
import functools
import math

import jax
import jax.numpy as jnp
from jax import lax
from jax.experimental import pallas as pl
from jax.experimental.pallas import tpu as pltpu
from jax.sharding import PartitionSpec as P

HEAD = 64
SUMM = 50

epsilon = 1e-05
masked_score = -1e30
bf16 = jnp.bfloat16
f32 = jnp.float32
BOTH = ("dp", "fsdp")
score_scale = 1.0 / math.sqrt(HEAD)

ROWS_BY_ROWS = (((1,), (0,)), ((), ()))
ROWS_BY_COLS = (((1,), (1,)), ((), ()))
COLS_BY_ROWS = (((0,), (0,)), ((), ()))


def dot(left, right, dims):
    return lax.dot_general(left, right, dims, preferred_element_type=f32)


def layer_norm(values, gains, shifts):
    centre = jnp.mean(values, axis=-1, keepdims=True)
    centred = values - centre
    spread = jnp.mean(centred * centred, axis=-1, keepdims=True)
    return centred * lax.rsqrt(spread + epsilon) * gains + shifts


def gelu_tanh(values):
    return jax.nn.gelu(values, approximate=True)


def slot_order(devices):
    if devices == 8:
        return [
            (0, 0), (0, 1), (1, 0), (1, 1),
            (2, 0), (3, 0), (4, 1), (5, 1),
            (2, 1), (3, 1), (4, 0), (5, 0),
            (6, 0), (6, 1), (7, 0), (7, 1),
        ]
    return [(m, h) for m in range(devices) for h in range(2)]


def slot_groups(devices):
    return len(slot_order(devices)) // 4


def in_groups(items):
    return [items[n : n + 4] for n in range(0, len(items), 4)]


def swapped(x, bit):
    devices = lax.axis_size("fsdp")
    return lax.ppermute(x, "fsdp", [(i, i ^ bit) for i in range(devices)])


def sent(own):
    if lax.axis_size("fsdp") != 8:
        return None
    x0 = swapped(own[0], 2)
    y1 = swapped(own[1], 4)
    x1 = swapped(own[1], 2)
    y0 = swapped(own[0], 4)
    return x0, y1, x1, y0


def passed_on(own, hops, earlier=()):
    devices = lax.axis_size("fsdp")
    if devices != 8:
        pieces = [own]
        bit = 1
        while bit < devices:
            pieces = pieces + [[swapped(half, bit) for half in piece] for piece in pieces]
            bit *= 2
        return in_groups([half for piece in pieces for half in piece])
    x0, y1, x1, y0 = hops
    if earlier:
        x0, y1 = after((x0, y1), *earlier)
    a0 = swapped(x0, 4)
    a1 = swapped(y1, 2)
    return [
        [own[0], own[1], swapped(own[0], 1), swapped(own[1], 1)],
        [x0, swapped(x0, 1), y1, swapped(y1, 1)],
        [x1, swapped(x1, 1), y0, swapped(y0, 1)],
        [a0, a1, swapped(a0, 1), swapped(a1, 1)],
    ]


def total(*terms):
    result = terms[0].astype(f32)
    for term in terms[1:]:
        result = result + term.astype(f32)
    return result


def paired(own, other):
    return total(own, swapped(other, 1)).astype(bf16)


def plain_scattered_sum(groups):
    flat = [half for group in groups for half in group]
    bit = len(flat) // 4
    while bit > 1:
        flat = [
            total(flat[n], swapped(flat[n + 2 * bit], bit)).astype(bf16) for n in range(2 * bit)
        ]
        bit //= 2
    return [total(flat[h], swapped(flat[h + 2], 1)) for h in range(2)]


def scattered_sum(make, groups, first=None, second=None):
    if groups != 4:
        made = [make(g, ()) for g in range(groups)]
        for extra in (first, second):
            if extra:
                done, use = extra(())
                use(done)
        return plain_scattered_sum(made)
    later = make(2, ())
    x1 = paired(later[0], later[1])
    y0 = paired(later[2], later[3])
    if first:
        done, use = first((x1, y0))
        x1, y0, done = after((swapped(x1, 2), swapped(y0, 4), done))
        use(done)
        far = make(3, (x1, y0))
    else:
        far = make(3, (x1, y0))
        far, x1, y0 = after((far, swapped(x1, 2), swapped(y0, 4)))
    a0 = paired(far[0], far[2])
    a1 = paired(far[1], far[3])
    near = make(1, (a0, a1))
    own = make(0, (a0, a1, near[0]))
    own, a0, a1 = after((own, swapped(a0, 4), swapped(a1, 2)))
    x0 = total(near[0], swapped(near[1], 1), a0).astype(bf16)
    y1 = total(near[2], swapped(near[3], 1), a1).astype(bf16)
    mine = [total(own[0], swapped(own[2], 1), y0), total(own[1], swapped(own[3], 1), x1)]
    done, use = second((x0, y1)) if second else ((), None)
    x0, y1, mine, done = after((swapped(x0, 2), swapped(y1, 4), mine, done))
    if use:
        use(done)
    return [total(mine[0], x0), total(mine[1], y1)]


def after(values, *earlier):
    flat, tree = jax.tree.flatten(values)
    flat = lax.optimization_barrier(tuple(flat) + earlier)[: len(flat)]
    return jax.tree.unflatten(tree, flat)


def held(shape, place=None):
    where = place or (0,) * len(shape)
    return pl.BlockSpec(shape, lambda *_: where, pipeline_mode=pl.Buffered(1))


anywhere = pl.BlockSpec(memory_space=pl.ANY)


def half_rows(chunk, width):
    return pl.BlockSpec((chunk, width), lambda s: (s, 0))


def group_rows(group, chunk, width):
    return pl.BlockSpec((4, chunk, width), lambda s: (group, s, 0))


def group_call(kernel, name, steps, ins, specs, outs, out_specs, earlier, scratch, flops, moved):
    aliases = {len(ins) + n: n for n in range(len(earlier))}
    made = pl.pallas_call(
        functools.partial(kernel, len(ins), len(earlier)),
        grid=(steps,),
        in_specs=specs + [anywhere] * len(earlier),
        out_specs=out_specs,
        out_shape=outs,
        scratch_shapes=scratch,
        input_output_aliases=aliases,
        compiler_params=pltpu.CompilerParams(
            dimension_semantics=("arbitrary",), vmem_limit_bytes=52 * 2**20
        ),
        cost_estimate=pl.CostEstimate(flops=flops, bytes_accessed=moved, transcendentals=0),
        name=name,
    )(*ins, *earlier)
    return list(made)


def split_refs(n_ins, n_earlier, refs):
    return refs[:n_ins], refs[n_ins + n_earlier :]


def norm_kernel(n_ins, n_earlier, *refs):
    ins, rest = split_refs(n_ins, n_earlier, refs)
    gain_ref, shift_ref = ins[4:]
    for n in range(4):
        rest[0][n] = layer_norm(
            ins[n][...].astype(f32), gain_ref[...], shift_ref[...]
        ).astype(bf16)


def norm_rows(group, halves, gain, shift, earlier, slots):
    half, wide = halves[0].shape
    chunk = half // 2
    return group_call(
        norm_kernel,
        "norm_rows",
        2,
        list(halves) + [gain, shift],
        [half_rows(chunk, wide)] * 4 + [held(gain.shape), held(shift.shape)],
        [jax.ShapeDtypeStruct((slots, half, wide), bf16)],
        [group_rows(group, chunk, wide)],
        earlier,
        [],
        80 * half * wide,
        16 * half * wide,
    )


def triple_kernel(n_ins, n_earlier, *refs):
    (rows_ref, weight_ref, bias_ref), outs = split_refs(n_ins, n_earlier, refs)
    width = outs[0].shape[1]
    made = (dot(rows_ref[...], weight_ref[...], ROWS_BY_ROWS) + bias_ref[...]).astype(bf16)
    for place in range(3):
        outs[place][...] = made[:, place * width : (place + 1) * width]


def triple(first, steps, rows, weight, bias, earlier, count):
    wide = rows.shape[1]
    size = count // slot_groups(lax.axis_size("fsdp"))
    width = weight.shape[1] // 3
    return group_call(
        triple_kernel,
        "triple",
        steps,
        [rows, weight, bias],
        [
            pl.BlockSpec((size, wide), lambda s: (s + first, 0)),
            held(weight.shape),
            held(bias.shape),
        ],
        [jax.ShapeDtypeStruct((count, width), bf16)] * 3,
        [pl.BlockSpec((size, width), lambda s: (s + first, 0))] * 3,
        earlier,
        [],
        6 * steps * size * wide * width,
        2 * steps * size * wide,
    )


def project_kernel(n_ins, n_earlier, *refs):
    ins, rest = split_refs(n_ins, n_earlier, refs)
    weight_ref, outs = ins[-1], rest[:4]
    chunk, wide = outs[0].shape
    parts = [ref[...].reshape(4 * chunk, ref.shape[2]) for ref in ins[:-1]]
    rows = parts[0] if len(parts) == 1 else jnp.concatenate(parts, axis=1)
    by_rows = weight_ref.shape[0] == rows.shape[1] and weight_ref.shape[1] == wide
    tile = min(wide, 512)
    for start in range(0, wide, tile):
        columns = slice(start, start + tile)
        if by_rows:
            made = dot(rows, weight_ref[:, columns], ROWS_BY_ROWS)
        else:
            made = dot(rows, weight_ref[columns, :], ROWS_BY_COLS)
        made = made.astype(bf16)
        for n in range(4):
            outs[n][:, columns] = made[n * chunk : (n + 1) * chunk, :]


def project(group, parts, weight, wide):
    half = parts[0].shape[1]
    chunk = half // 2
    return group_call(
        project_kernel,
        "project",
        2,
        list(parts) + [weight],
        [group_rows(group, chunk, part.shape[2]) for part in parts] + [held(weight.shape)],
        [jax.ShapeDtypeStruct((half, wide), bf16)] * 4,
        [half_rows(chunk, wide)] * 4,
        [],
        [],
        8 * half * weight.size,
        8 * half * wide + 2 * weight.size,
    )


def project_back_kernel(n_ins, n_earlier, *refs):
    ins, rest = split_refs(n_ins, n_earlier, refs)
    weight_ref = ins[4]
    made_ref, kept_ref, rows = rest
    chunk = ins[0].shape[0]
    for n in range(4):
        kept_ref[n] = ins[n][...]
        rows[n * chunk : (n + 1) * chunk, :] = ins[n][...]
    made = dot(rows[...], weight_ref[...], ROWS_BY_COLS).astype(bf16)
    for n in range(4):
        made_ref[n] = made[n * chunk : (n + 1) * chunk, :]


def project_back(group, halves, weight, earlier, slots):
    half, wide = halves[0].shape
    chunk = half // 2
    width = weight.shape[0]
    return group_call(
        project_back_kernel,
        "project_back",
        2,
        list(halves) + [weight],
        [half_rows(chunk, wide)] * 4 + [held(weight.shape)],
        [jax.ShapeDtypeStruct((slots, half, n), bf16) for n in (width, wide)],
        [group_rows(group, chunk, n) for n in (width, wide)],
        earlier,
        [pltpu.VMEM((4 * chunk, wide), bf16)],
        8 * half * weight.size,
        16 * half * wide,
    )


gelu_rate = math.sqrt(2.0 / math.pi)
gelu_cube = 0.044715


def feed_forward_kernel(n_ins, n_earlier, *refs):
    ins, rest = split_refs(n_ins, n_earlier, refs)
    up_ref, shift_ref, down_ref = ins[8:]
    active_ref, grad_ref, rows_ref, grad_rows_ref = rest[:4]
    back = rest[4:8]
    ahead = rest[8:12]
    shift_grad_ref, rows, grad_rows, active, grad_upper = rest[12:]
    chunk, wide = ins[0].shape
    units = up_ref.shape[1]
    for n in range(4):
        r = slice(n * chunk, (n + 1) * chunk)
        rows[r, :] = ins[n][...]
        grad_rows[r, :] = ins[4 + n][...]
        rows_ref[n] = ins[n][...]
        grad_rows_ref[n] = ins[4 + n][...]
    tile = min(units, 512)

    def hidden(t, carry):
        columns = pl.ds(pl.multiple_of(t * tile, tile), tile)
        upper = dot(rows[...], up_ref[:, columns], ROWS_BY_ROWS) + shift_ref[:, columns]
        grad_active = dot(grad_rows[...], down_ref[columns, :], ROWS_BY_COLS)
        square = upper * upper
        bend = jnp.tanh(gelu_rate * upper * (1.0 + gelu_cube * square))
        share = 0.5 * (1.0 + bend)
        slope = share + 0.5 * upper * (1.0 - bend * bend) * (
            gelu_rate * (1.0 + 3.0 * gelu_cube * square)
        )
        made = (upper * share).astype(bf16)
        grad = (grad_active * slope).astype(bf16)
        active[:, columns] = made
        grad_upper[:, columns] = grad
        shift_grad_ref[0, 0:1, columns] = jnp.sum(grad.astype(f32), axis=0, keepdims=True)
        for n in range(4):
            r = slice(n * chunk, (n + 1) * chunk)
            active_ref[n, :, columns] = made[r, :]
            grad_ref[n, :, columns] = grad[r, :]
        return carry

    lax.fori_loop(0, units // tile, hidden, 0)
    step = min(wide, 1024)

    def outer(t, carry):
        columns = pl.ds(pl.multiple_of(t * step, step), step)
        made_back = dot(grad_upper[...], up_ref[columns, :], ROWS_BY_COLS).astype(bf16)
        made_ahead = dot(active[...], down_ref[:, columns], ROWS_BY_ROWS).astype(bf16)
        for n in range(4):
            r = slice(n * chunk, (n + 1) * chunk)
            back[n][:, columns] = made_back[r, :]
            ahead[n][:, columns] = made_ahead[r, :]
        return carry

    lax.fori_loop(0, wide // step, outer, 0)


def feed_forward(group, halves, grad_halves, up, shift, down, earlier, slots):
    half, wide = halves[0].shape
    chunk = half // 2
    units = up.shape[1]
    sizes = (units, units, wide, wide)
    outs = [jax.ShapeDtypeStruct((slots, half, n), bf16) for n in sizes]
    outs += [jax.ShapeDtypeStruct((half, wide), bf16)] * 8
    outs += [jax.ShapeDtypeStruct((2, 8, units), f32)]
    made = group_call(
        feed_forward_kernel,
        "feed_forward",
        2,
        list(halves) + list(grad_halves) + [up, shift, down],
        [half_rows(chunk, wide)] * 8 + [held(up.shape), held(shift.shape), held(down.shape)],
        outs,
        [group_rows(group, chunk, n) for n in sizes]
        + [half_rows(chunk, wide)] * 8
        + [pl.BlockSpec((1, 8, units), lambda s: (s, 0, 0))],
        earlier,
        [pltpu.VMEM((4 * chunk, n), bf16) for n in (wide, wide, units, units)],
        32 * half * wide * units,
        48 * half * wide + 4 * wide * units,
    )
    return made[:4], made[4:8], made[8:12], jnp.sum(made[12][:, 0], axis=0)


def only_head(values, head):
    columns = lax.broadcasted_iota(jnp.int32, values.shape, 1) // HEAD
    return jnp.where(columns == head, values, jnp.zeros_like(values))


def transposed(values):
    return values.astype(f32).T.astype(bf16)


def places_of(plan_ref, blocks, subs, half, j):
    return [
        pl.ds(pl.multiple_of(plan_ref[3 * blocks + subs * j + n] * half, half), half)
        for n in range(subs)
    ]


def rows_of(ref, places):
    parts = [ref[place, :] for place in places]
    return parts[0] if len(parts) == 1 else jnp.concatenate(parts, axis=0)


def cols_of(ref, places):
    parts = [ref[:, place] for place in places]
    return parts[0] if len(parts) == 1 else jnp.concatenate(parts, axis=1)


def attn_forward_kernel(
    block, half, heads, plan_ref, q_ref, k_ref, v_ref, sk_ref, sv_ref, row_ref, o_ref, log_ref,
    q_heads, vt_all, svt, tops, sums, mixed,
):
    i = pl.program_id(0)
    blocks = pl.num_programs(0)
    subs = block // half

    @pl.when(i == 0)
    def _():
        for n in range(v_ref.shape[0] // half):
            r = slice(n * half, (n + 1) * half)
            vt_all[:, r] = transposed(v_ref[r, :])
        svt[...] = transposed(sv_ref[...])

    mine = places_of(plan_ref, blocks, subs, half, i)
    q = rows_of(q_ref, mine).astype(f32) * score_scale
    for h in range(heads):
        q_heads[h] = only_head(q, h).astype(bf16)
    tops[...] = jnp.full_like(tops, masked_score)
    sums[...] = jnp.zeros_like(sums)
    mixed[...] = jnp.zeros_like(mixed)
    lowest = row_ref[0:1, :]
    highest = row_ref[1:2, :]
    summ_end = row_ref[2:3, :]
    me = row_ref[3:4, :]

    def step(keys, values_t, mask):
        each = range(heads)
        scores = [dot(keys, q_heads[h], ROWS_BY_COLS) for h in each]
        if mask is not None:
            scores = [jnp.where(mask, one, masked_score) for one in scores]
        before = [tops[h : h + 1, :] for h in each]
        top = [jnp.maximum(before[h], jnp.max(scores[h], axis=0, keepdims=True)) for h in each]
        weights = [jnp.exp(scores[h] - top[h]) for h in each]
        keep = [jnp.exp(before[h] - top[h]) for h in each]
        added = [jnp.sum(weights[h], axis=0, keepdims=True) for h in each]
        totals = [keep[h] * sums[h : h + 1, :] + added[h] for h in each]
        part_of = [slice(h * HEAD, (h + 1) * HEAD) for h in each]
        more = [dot(values_t[part_of[h], :], weights[h].astype(bf16), ROWS_BY_ROWS) for h in each]
        result = [keep[h] * mixed[part_of[h], :] + more[h] for h in each]
        for h in each:
            tops[h : h + 1, :] = top[h]
            sums[h : h + 1, :] = totals[h]
            mixed[part_of[h], :] = result[h]

    @pl.when(plan_ref[2 * blocks + i] > 0)
    def _():
        places = lax.broadcasted_iota(jnp.int32, (sk_ref.shape[0], block), 0)
        step(sk_ref[...], svt[...], places < summ_end)

    def whole(j, carry):
        there = places_of(plan_ref, blocks, subs, half, j)
        step(rows_of(k_ref, there), cols_of(vt_all, there), None)
        return carry

    def part(j, carry):
        there = places_of(plan_ref, blocks, subs, half, j)
        places = j * block + lax.broadcasted_iota(jnp.int32, (block, block), 0)
        mask = ((places >= lowest) & (places <= highest)) | (places == me)
        step(rows_of(k_ref, there), cols_of(vt_all, there), mask)
        return carry

    lax.fori_loop(plan_ref[i], plan_ref[blocks + i], whole, 0)
    lax.fori_loop(plan_ref[blocks + i], i + 1, part, 0)
    for h in range(heads):
        r = slice(h * HEAD, (h + 1) * HEAD)
        mixed[r, :] = mixed[r, :] * (1.0 / sums[h : h + 1, :])
    log_ref[...] = tops[...] + jnp.log(jnp.maximum(sums[...], 1e-37))
    made = mixed[...].T.astype(bf16)
    for n, place in enumerate(mine):
        o_ref[place, :] = made[n * half : (n + 1) * half, :]


def attn_backward_kernel(
    block, half, heads, plan_ref, q_ref, k_ref, v_ref, sk_ref, sv_ref, row_ref, log_ref, o_ref, do_ref, dq_ref, dk_ref, dv_ref, dsk_ref, dsv_ref, shift_ref, q_heads, do_heads, kt_all, skt, dq_sum,
    dk_sum, dv_sum, dsk_sum, dsv_sum,
):
    i = pl.program_id(0)
    blocks = pl.num_programs(0)
    subs = block // half

    @pl.when(i == 0)
    def _():
        dk_sum[...] = jnp.zeros_like(dk_sum)
        dv_sum[...] = jnp.zeros_like(dv_sum)
        dsk_sum[...] = jnp.zeros_like(dsk_sum)
        dsv_sum[...] = jnp.zeros_like(dsv_sum)
        for n in range(k_ref.shape[0] // half):
            r = slice(n * half, (n + 1) * half)
            kt_all[:, r] = transposed(k_ref[r, :])
        skt[...] = transposed(sk_ref[...])

    mine = places_of(plan_ref, blocks, subs, half, i)
    q = rows_of(q_ref, mine).astype(f32) * score_scale
    do = rows_of(do_ref, mine).astype(f32)
    for h in range(heads):
        q_heads[h] = only_head(q, h).astype(bf16)
        do_heads[h] = only_head(do, h).astype(bf16)
    both_t = (do * rows_of(o_ref, mine).astype(f32)).T
    row_terms = [
        jnp.sum(both_t[h * HEAD : (h + 1) * HEAD, :], axis=0, keepdims=True) for h in range(heads)
    ]
    dq_sum[...] = jnp.zeros_like(dq_sum)
    lowest = row_ref[0:1, :]
    highest = row_ref[1:2, :]
    summ_end = row_ref[2:3, :]
    me = row_ref[3:4, :]

    def step(keys, values, keys_t, mask):
        dk = dv = None
        for h in range(heads):
            scores = dot(keys, q_heads[h], ROWS_BY_COLS)
            if mask is not None:
                scores = jnp.where(mask, scores, masked_score)
            probs = jnp.exp(scores - log_ref[h : h + 1, :])
            grad_probs = dot(values, do_heads[h], ROWS_BY_COLS)
            grad_scores = (probs * (grad_probs - row_terms[h])).astype(bf16)
            r = slice(h * HEAD, (h + 1) * HEAD)
            dq_sum[r, :] += dot(keys_t[r, :], grad_scores, ROWS_BY_ROWS)
            dv_own = dot(probs.astype(bf16), do_heads[h], ROWS_BY_ROWS)
            dk_own = dot(grad_scores, q_heads[h], ROWS_BY_ROWS)
            dv = dv_own if dv is None else dv + dv_own
            dk = dk_own if dk is None else dk + dk_own
        return dk, dv

    @pl.when(plan_ref[2 * blocks + i] > 0)
    def _():
        places = lax.broadcasted_iota(jnp.int32, (sk_ref.shape[0], block), 0)
        dk, dv = step(sk_ref[...], sv_ref[...], skt[...], places < summ_end)
        dsk_sum[...] += dk
        dsv_sum[...] += dv

    def whole(j, masked):
        there = places_of(plan_ref, blocks, subs, half, j)
        mask = None
        if masked:
            places = j * block + lax.broadcasted_iota(jnp.int32, (block, block), 0)
            mask = ((places >= lowest) & (places <= highest)) | (places == me)
        dk, dv = step(rows_of(k_ref, there), rows_of(v_ref, there), cols_of(kt_all, there), mask)
        for n, place in enumerate(there):
            dk_sum[place, :] += dk[n * half : (n + 1) * half, :]
            dv_sum[place, :] += dv[n * half : (n + 1) * half, :]

    def plain(j, carry):
        whole(j, False)
        return carry

    def part(j, carry):
        whole(j, True)
        return carry

    lax.fori_loop(plan_ref[i], plan_ref[blocks + i], plain, 0)
    lax.fori_loop(plan_ref[blocks + i], i + 1, part, 0)
    made = (dq_sum[...] * score_scale).T.astype(bf16)
    for n, place in enumerate(mine):
        dq_ref[place, :] = made[n * half : (n + 1) * half, :]

    @pl.when(i == blocks - 1)
    def _():
        dk_ref[...] = dk_sum[...].astype(bf16)
        dv_ref[...] = dv_sum[...].astype(bf16)
        dsk_ref[...] = dsk_sum[...].astype(bf16)
        dsv_ref[...] = dsv_sum[...].astype(bf16)

        def added(ref):
            return jnp.sum(ref[...].astype(f32), axis=0, keepdims=True)

        shift_ref[...] = jnp.zeros_like(shift_ref)
        shift_ref[0:1, :] = added(dq_ref)
        shift_ref[1:2, :] = added(dv_ref) + added(dsv_ref)


def attn_forward(part, parts, plan, rows, q, k, v, sk, sv, block, half):
    count = q.shape[0]
    width = q.shape[1] // parts
    heads = width // HEAD
    by_cols = pl.BlockSpec((8, block), lambda i, *_: (0, i))
    pairs = count * count // 4
    return pl.pallas_call(
        functools.partial(attn_forward_kernel, block, half, heads),
        grid_spec=pltpu.PrefetchScalarGridSpec(
            num_scalar_prefetch=1,
            grid=(count // block,),
            in_specs=[held((one.shape[0], width), (0, part)) for one in (q, k, v, sk, sv)] + [by_cols],
            out_specs=[held((count, width)), by_cols],
            scratch_shapes=[
                pltpu.VMEM((heads, block, width), bf16),
                pltpu.VMEM((width, count), bf16),
                pltpu.VMEM((width, sk.shape[0]), bf16),
                pltpu.VMEM((8, block), f32),
                pltpu.VMEM((8, block), f32),
                pltpu.VMEM((width, block), f32),
            ],
        ),
        out_shape=[
            jax.ShapeDtypeStruct((count, width), bf16),
            jax.ShapeDtypeStruct((8, count), f32),
        ],
        compiler_params=pltpu.CompilerParams(
            dimension_semantics=("arbitrary",), vmem_limit_bytes=40 * 2**20
        ),
        cost_estimate=pl.CostEstimate(
            flops=16 * pairs * width, bytes_accessed=8 * count * width, transcendentals=pairs * heads
        ),
        name="attn_forward",
    )(plan, q, k, v, sk, sv, rows)


def attn_backward(part, parts, plan, rows, q, k, v, sk, sv, logs, o, do, block, half):
    count = q.shape[0]
    width = q.shape[1] // parts
    heads = width // HEAD
    by_cols = pl.BlockSpec((8, block), lambda i, *_: (0, i))
    pairs = count * count // 4
    long = jax.ShapeDtypeStruct((count, width), bf16)
    short = jax.ShapeDtypeStruct((sk.shape[0], width), bf16)
    shift = jax.ShapeDtypeStruct((8, width), f32)
    long_in = held((count, width), (0, part))
    short_in = held((sk.shape[0], width), (0, part))
    return pl.pallas_call(
        functools.partial(attn_backward_kernel, block, half, heads),
        grid_spec=pltpu.PrefetchScalarGridSpec(
            num_scalar_prefetch=1,
            grid=(count // block,),
            in_specs=[long_in] * 3
            + [short_in] * 2
            + [by_cols] * 2
            + [held((count, width)), long_in],
            out_specs=[held(one.shape) for one in (long, long, long, short, short, shift)],
            scratch_shapes=[
                pltpu.VMEM((heads, block, width), bf16),
                pltpu.VMEM((heads, block, width), bf16),
                pltpu.VMEM((width, count), bf16),
                pltpu.VMEM((width, sk.shape[0]), bf16),
                pltpu.VMEM((width, block), f32),
                pltpu.VMEM((count, width), f32),
                pltpu.VMEM((count, width), f32),
                pltpu.VMEM((sk.shape[0], width), f32),
                pltpu.VMEM((sk.shape[0], width), f32),
            ],
        ),
        out_shape=[long, long, long, short, short, shift],
        compiler_params=pltpu.CompilerParams(
            dimension_semantics=("arbitrary",), vmem_limit_bytes=48 * 2**20
        ),
        cost_estimate=pl.CostEstimate(
            flops=24 * pairs * width, bytes_accessed=20 * count * width, transcendentals=pairs * heads
        ),
        name="attn_backward",
    )(plan, q, k, v, sk, sv, rows, logs, o, do)


def spread_columns_kernel(parts_ref, *outs):
    shards = parts_ref.shape[0]
    width = parts_ref.shape[2] // 3
    for n, ref in enumerate(outs):
        for d in range(width // HEAD):
            start = n * width + d * HEAD
            for f in range(0, shards, 2):
                pair = [parts_ref[f + m, :, start : start + HEAD].astype(f32) for m in range(2)]
                place = (d * shards + f) * HEAD
                ref[:, place : place + 2 * HEAD] = jnp.concatenate(pair, axis=1)


def spread_columns(parts):
    shards, count, width = parts.shape
    return pl.pallas_call(
        spread_columns_kernel,
        out_shape=[jax.ShapeDtypeStruct((count, shards * width // 3), f32)] * 3,
        name="spread_columns",
    )(parts)


def attention_plan(lengths, padding, count, block, slots):
    places = jnp.arange(count, dtype=jnp.int32)
    ends = jnp.cumsum(lengths)
    passed = places[:, None] >= ends[None, :]
    segment = jnp.sum(passed.astype(jnp.int32), axis=1)
    lowest = jnp.max(jnp.where(passed, ends[None, :], 0), axis=1)
    living = count - padding
    highest = jnp.minimum(places, living - 1)
    nothing = jnp.zeros_like(places)
    rows = jnp.stack(
        [lowest, highest, segment * SUMM, places, nothing, nothing, nothing, nothing], axis=0
    )
    blocks = count // block
    starts = jnp.arange(blocks, dtype=jnp.int32) * block
    first = lowest.reshape(blocks, block)[:, 0] // block
    one_piece = lowest.reshape(blocks, block)[:, -1] <= first * block
    whole_end = jnp.maximum(jnp.minimum(starts, living) // block, first)
    split = jnp.where(one_piece, whole_end, first)
    summ_flag = (segment.reshape(blocks, block)[:, -1] > 0).astype(jnp.int32)
    return rows, jnp.concatenate([first, split, summ_flag, slots]).astype(jnp.int32)


def per_device(
    tokens,
    summaries,
    segment_lengths,
    pad_lengths,
    output_grad,
    norm1_gain,
    norm1_bias,
    query_weight,
    query_bias,
    key_weight,
    value_weight,
    value_bias,
    out_weight,
    out_bias,
    norm2_gain,
    norm2_bias,
    up_weight,
    up_bias,
    down_weight,
    down_bias,
):
    shards = lax.axis_size("fsdp")
    items = lax.axis_size("dp")
    devices = shards * items
    position = lax.axis_index("fsdp")
    tok_rows = tokens.shape[1]
    width = tokens.shape[2]
    count = tok_rows * shards
    own_width = width // shards
    rows_held = query_weight.shape[0]
    units_held = up_bias.shape[0]
    own_units = units_held * items
    hidden = units_held * devices
    summary_rows = summaries.shape[1]
    padded_summ = -(-summary_rows // 32) * 32
    spread = rows_held % HEAD == 0
    block = math.gcd(count, 512)

    def for_shards(weight):
        if spread:
            split = weight.reshape(rows_held, items, shards, rows_held)
            return split.transpose(2, 0, 1, 3).reshape(shards, rows_held, own_width)
        return weight.reshape(rows_held, shards, own_width).transpose(1, 0, 2)

    def from_shards(parts):
        if spread:
            split = parts.reshape(shards, rows_held, items, rows_held)
            return split.transpose(1, 2, 0, 3).reshape(rows_held, width)
        return parts.transpose(1, 0, 2).reshape(rows_held, width)

    def own_columns(vector):
        if spread:
            split = vector.reshape(items, shards, rows_held)
            return lax.dynamic_index_in_dim(split, position, 1, keepdims=False).reshape(own_width)
        return lax.dynamic_slice_in_dim(vector, position * own_width, own_width, 0)

    def whole_columns(vector):
        if spread:
            split = jnp.zeros((items, shards, rows_held), f32)
            return lax.dynamic_update_index_in_dim(
                split, vector.reshape(items, 1, rows_held), position, 1
            ).reshape(width)
        return lax.dynamic_update_slice_in_dim(
            jnp.zeros((width,), f32), vector, position * own_width, 0
        )

    half = tok_rows // 2
    order = slot_order(shards)
    groups = len(order) // 4
    eight = shards == 8

    def halves(whole):
        return [whole[:half], whole[half:]]

    def flat(slotted):
        return slotted.reshape(count, slotted.shape[2])

    def slot_rows(slotted):
        return slotted.reshape(slotted.shape[0] * half, slotted.shape[2])

    qkv_parts = jnp.concatenate(
        [for_shards(query_weight), for_shards(key_weight), for_shards(value_weight)], axis=2
    )
    qkv_parts = lax.all_to_all(qkv_parts, "fsdp", 0, 0, tiled=True)
    qkv_own = lax.all_gather(
        qkv_parts.reshape(shards * rows_held, 3 * own_width), "dp", axis=0, tiled=True
    )
    vectors = jnp.concatenate(
        [
            norm1_gain, norm1_bias, query_bias, value_bias, out_bias, norm2_gain, norm2_bias,
            down_bias, up_bias,
        ]
    ).astype(f32)
    vectors = lax.all_to_all(
        jnp.broadcast_to(vectors[None], (devices, vectors.shape[0])), BOTH, 0, 0, tiled=True
    )
    gain_one, shift_one, query_shift, value_shift, out_shift, gain_two, shift_two, down_shift = (
        vectors[:, n * rows_held : (n + 1) * rows_held].reshape(width) for n in range(8)
    )
    token_halves = after(halves(tokens[0]), qkv_parts, vectors)
    token_hops = sent(token_halves)
    grad_own = halves(output_grad[0])
    up_parts = up_weight.reshape(rows_held, items, shards, units_held).transpose(2, 0, 1, 3)
    up_parts = up_parts.reshape(shards, rows_held, own_units)
    more_slots = -(-padded_summ // half)

    def normed_group(g, group, normed):
        return norm_rows(
            g, group, gain_one[None], shift_one[None], normed, 4 * groups + more_slots
        )

    if eight:
        mine = [*token_halves, *[swapped(one, 1) for one in token_halves]]
        normed = normed_group(0, mine, [])
        x0, y1, x1, y0 = token_hops
        x0, y1 = after((x0, y1), normed[0], up_parts, *grad_own)
        a0, a1 = swapped(x0, 4), swapped(y1, 2)
        normed = normed_group(1, [x0, swapped(x0, 1), y1, swapped(y1, 1)], normed)
        x1, y0, a0, a1 = after((x1, y0, a0, a1), normed[0])
        last_tokens = [a0, a1, swapped(a0, 1), swapped(a1, 1)]
        normed = normed_group(2, [x1, swapped(x1, 1), y0, swapped(y0, 1)], normed)
    else:
        normed = []
        token_groups = passed_on(token_halves, token_hops)
        last_tokens = token_groups[-1]
        for g in range(groups - 1):
            normed = normed_group(g, token_groups[g], normed)
    up_shift = lax.dynamic_index_in_dim(
        vectors[:, 8 * rows_held :].reshape(items, shards, units_held), position, 1, keepdims=False
    ).reshape(1, own_units)
    query_shift = own_columns(query_shift)
    value_shift = own_columns(value_shift)
    qkv_shift = jnp.concatenate([query_shift, jnp.zeros_like(query_shift), value_shift])[None]

    early = token_hops[:1] if eight else ()
    if spread:
        both = after(jnp.concatenate([out_weight, down_weight], axis=0), *early)
        both = lax.all_gather(both, "dp", axis=0)
        out_own = both[:, :rows_held].reshape(own_width, width)
        down_own = both[:, rows_held:].reshape(own_units, width)
    else:
        out_own = lax.dynamic_slice_in_dim(
            lax.all_gather(out_weight, BOTH, axis=0, tiled=True), position * own_width, own_width, 0
        )
        down_own = lax.all_gather(down_weight, "dp", axis=0, tiled=True)
    up_parts = after(up_parts, last_tokens[0])
    up_parts = lax.all_to_all(up_parts, "fsdp", 0, 0, tiled=True)
    grad_own = after(grad_own, *last_tokens)
    grad_hops = sent(grad_own)

    summ_full = after(
        jnp.broadcast_to(summaries, (shards,) + summaries.shape[1:]), last_tokens[0]
    )
    summ_full = lax.all_to_all(summ_full, "fsdp", 0, 0, tiled=True)
    made = triple(0, groups - 1, slot_rows(normed[0]), qkv_own, qkv_shift, [], count)
    last_tokens, made = after((last_tokens, made))
    normed = normed_group(groups - 1, last_tokens, normed)
    queries, keys, values = triple(
        groups - 1, 1, slot_rows(normed[0]), qkv_own, qkv_shift, made, count
    )
    queries, keys, values, summ_full, up_parts = after(
        (queries, keys, values, summ_full, up_parts)
    )
    up_own = lax.all_gather(
        up_parts.reshape(shards * rows_held, own_units), "dp", axis=0, tiled=True
    )
    summ_full = summ_full.transpose(1, 0, 2).reshape(summary_rows, width)
    summ_inputs = jnp.pad(summ_full, ((0, padded_summ - summary_rows), (0, 0))).astype(f32)
    normed_summ = layer_norm(summ_inputs, gain_one, shift_one).astype(bf16)
    extra_rows = ((0, more_slots * half - padded_summ), (0, 0))
    normed = lax.dynamic_update_slice(
        slot_rows(normed[0]), jnp.pad(normed_summ, extra_rows), (count, 0)
    )
    summ_qkv = dot(normed_summ, qkv_own, ROWS_BY_ROWS) + qkv_shift
    summ_keys = summ_qkv[:, own_width : 2 * own_width].astype(bf16)
    summ_values = summ_qkv[:, 2 * own_width :].astype(bf16)
    slot_of = [[order.index((m, h)) for h in range(2)] for m in range(shards)]
    slots = jnp.array(slot_of, jnp.int32)[jnp.arange(shards) ^ position].reshape(-1)
    rows, plan = attention_plan(segment_lengths[0], pad_lengths[0], count, block, slots)
    parts = 2 if own_width % 256 == 0 else 1
    attn = []
    logs = []
    for part in range(parts):
        one, log = attn_forward(
            part, parts, plan, rows, queries, keys, values, summ_keys, summ_values, block, half
        )
        if eight and part == 0:
            one, log, plan, *grad_hops = after((one, log, plan, *grad_hops))
            x0, y1, x1, y0 = grad_hops
            a0, a1 = swapped(x0, 4), swapped(y1, 2)
        elif eight:
            one, log, a0, a1 = after((one, log, a0, a1))
            grad_groups = [
                [*grad_own, swapped(grad_own[0], 1), swapped(grad_own[1], 1)],
                [x0, swapped(x0, 1), y1, swapped(y1, 1)],
                [x1, swapped(x1, 1), y0, swapped(y0, 1)],
                [a0, a1, swapped(a0, 1), swapped(a1, 1)],
            ]
        attn.append(one)
        logs.append(log)
    if not eight:
        grad_groups = passed_on(grad_own, grad_hops)
    attn_slots = [one.reshape(4 * groups, half, own_width // parts) for one in attn]
    inputs = [one.astype(f32) for one in halves(tokens[0])]
    proj_sums = scattered_sum(
        lambda g, earlier: project(g, attn_slots, after(out_own, *earlier), width), groups
    )
    resid = [inputs[h] + proj_sums[h] + out_shift for h in range(2)]

    normed_two_own = [layer_norm(one, gain_two, shift_two).astype(bf16) for one in resid]
    two_hops = sent(normed_two_own)
    two_groups = passed_on(normed_two_own, two_hops)
    made = []
    back = {}
    ahead = {}
    unit_sums = []

    def feed(g, earlier):
        nonlocal made
        for n in [1, 2, 3, 0] if eight else range(groups):
            if n not in back and g not in back:
                mine = two_groups[n]
                if n == 2 and eight:
                    x1, y0 = after((mine[0], mine[2]), back[1][0])
                    mine = [x1, swapped(x1, 1), y0, swapped(y0, 1)]
                made, back[n], ahead[n], unit_sum = feed_forward(
                    n, mine, grad_groups[n], up_own, up_shift, after(down_own, *earlier),
                    made, 4 * groups,
                )
                unit_sums.append(unit_sum)
        return back[g]

    kept = {}

    def down_grad_of(earlier):
        active, _, _, grad_rows = (flat(one) for one in made)
        grad = dot(after(active, *earlier), grad_rows, COLS_BY_ROWS).astype(bf16)
        return grad, functools.partial(kept.__setitem__, "down")

    def up_grad_of(earlier):
        _, grad_upper, normed_two, _ = (flat(one) for one in feed_made)
        return dot(after(normed_two, *earlier), grad_upper, COLS_BY_ROWS).astype(bf16)

    grad_normed_two = scattered_sum(feed, groups, None, down_grad_of)
    feed_made = made
    down_grad = lax.psum_scatter(kept["down"], "dp", scatter_dimension=0, tiled=True)
    grad_floats = [one.astype(f32) for one in halves(output_grad[0])]
    down_shift_grad = jnp.sum(output_grad[0].astype(f32), axis=0)

    def norm_back(values, gains, shifts, grads):
        pulled = [
            jax.vjp(layer_norm, value, gains, shifts)[1](grad) for value, grad in zip(values, grads)
        ]
        return (
            [one[0] for one in pulled],
            sum(one[1] for one in pulled),
            sum(one[2] for one in pulled),
        )

    grad_two, gain_two_grad, shift_two_grad = norm_back(resid, gain_two, shift_two, grad_normed_two)
    grad_resid = [grad_two[h] + grad_floats[h] for h in range(2)]

    grad_proj = [one.astype(bf16) for one in grad_resid]
    out_shift_grad = sum(jnp.sum(one.astype(f32), axis=0) for one in grad_proj)
    proj_hops = sent(grad_proj)
    if eight:
        mine = grad_proj + [swapped(one, 1) for one in grad_proj]
        made = project_back(0, mine, out_own, [], 4 * groups)
        up_grad = up_grad_of((made[0],))
        x0, y1, x1, y0 = proj_hops
        x0, y1, x1, y0, up_grad = after((x0, y1, x1, y0, up_grad))
        up_grad_dot = up_grad
        a0, a1 = swapped(x0, 4), swapped(y1, 2)
        made = project_back(
            1, [x0, swapped(x0, 1), y1, swapped(y1, 1)], out_own, made, 4 * groups
        )
        x1, y0, a0, a1 = after((x1, y0, a0, a1), made[0])
        made = project_back(
            2, [x1, swapped(x1, 1), y0, swapped(y0, 1)], out_own, made, 4 * groups
        )
        proj_groups = [None, None, None, [a0, a1, swapped(a0, 1), swapped(a1, 1)]]
    else:
        up_grad = up_grad_of(())
        made = []
        proj_groups = passed_on(grad_proj, proj_hops)
    up_grad = lax.psum_scatter(up_grad, "dp", scatter_dimension=0, tiled=True)
    up_grad = up_grad.reshape(shards, rows_held, own_units)
    if not eight:
        up_grad = lax.all_to_all(up_grad, "fsdp", 0, 0, tiled=True)
    ahead = [ahead[g] for g in range(groups)]
    if eight:
        own, near, later, far = after(ahead, up_grad_dot)
        x1, y0 = paired(later[0], later[1]), paired(later[2], later[3])
        a0, a1 = paired(far[0], far[2]), paired(far[1], far[3])
        near = [total(near[0], swapped(near[1], 1)), total(near[2], swapped(near[3], 1))]
        own = [total(own[0], swapped(own[2], 1)), total(own[1], swapped(own[3], 1))]
    for g in range(groups - 1 if eight else 0, groups):
        halves_now = proj_groups[g]
        if eight:
            halves_now, x1, y0, a0, a1, near, own = after(
                (halves_now, x1, y0, a0, a1, near, own)
            )
        made = project_back(g, halves_now, out_own, made, 4 * groups)
    grad_attn, proj_rows = (flat(one) for one in made)
    grad_attn, down_grad = after((grad_attn, down_grad))
    if eight:
        x1, y0, a0, a1 = after((x1, y0, a0, a1), *proj_groups[-1])
        travelling = [swapped(x1, 2), swapped(y0, 4), swapped(a0, 4), swapped(a1, 2)]
    else:
        result = plain_scattered_sum(ahead)
    pulled = []
    again = grad_attn
    for part in range(parts):
        one = list(attn_backward(
            part, parts, plan, rows, queries, keys, values, summ_keys, summ_values, logs[part],
            attn[part], again, block, half,
        ))
        if eight and part == 0:
            one, again, *travelling = after((one, again, *travelling))
            x1, y0, a0, a1 = travelling
            x0, y1 = total(near[0], a0).astype(bf16), total(near[1], a1).astype(bf16)
            travelling = [swapped(x0, 2), swapped(y1, 4)]
            up_grad = after(up_grad, x0, y1)
            up_grad = lax.all_to_all(up_grad, "fsdp", 0, 0, tiled=True)
        elif eight:
            one, up_grad, *travelling = after((one, up_grad, *travelling))
        pulled.append(one)
    grad_slots = [
        pulled[part][n].reshape(4 * groups, half, own_width // parts)
        for n in range(3)
        for part in range(parts)
    ]
    grad_summ_kv = jnp.concatenate(
        [pulled[part][n] for n in (3, 4) for part in range(parts)], axis=1
    )

    summ_share = -(-padded_summ // (shards * 16)) * 16
    more_rows = ((0, summ_share * shards - padded_summ), (0, 0))

    def qkv_grad_of(earlier):
        slots_now, summ_now = after((grad_slots, grad_summ_kv), *earlier)
        grad_qkv = jnp.concatenate([flat(one) for one in slots_now], axis=1)
        grad_qkv = jnp.concatenate(
            [grad_qkv, jnp.pad(summ_now, (extra_rows[0], (own_width, 0)))], axis=0
        )
        grad = dot(normed, grad_qkv, COLS_BY_ROWS).astype(bf16)
        return grad, functools.partial(kept.__setitem__, "qkv")

    def side_work(earlier):
        grad = lax.psum_scatter(kept["qkv"], "dp", scatter_dimension=0, tiled=True)
        up_now, down_now, result_parts = after((up_grad, down_grad, result_terms), *earlier)
        grad = after(grad, *earlier).reshape(shards, rows_held, 3 * own_width)
        kept["qkv_parts"] = lax.all_to_all(grad, "fsdp", 0, 0, tiled=True)
        made = jnp.concatenate(
            [(total(*result_parts[h]) + down_shift).astype(bf16) for h in range(2)], axis=0
        )
        up_now = up_now.reshape(shards, rows_held, items, units_held).transpose(1, 2, 0, 3)
        up_now = up_now.reshape(rows_held, hidden).astype(f32)

        def use(done):
            kept.update(zip(("qkv_parts", "result", "up", "down"), done))

        return (kept["qkv_parts"], made, up_now, down_now.astype(f32)), use

    if eight:
        x0, y1 = travelling
        result_terms = [(resid[0], own[0], y0, x0), (resid[1], own[1], x1, y1)]
    else:
        result_terms = [(resid[h], result[h]) for h in range(2)]

    def grad_rows_back(g, earlier):
        if g == 1 or not eight:
            back = dot(after(grad_summ_kv, *earlier), qkv_own[:, own_width:], ROWS_BY_COLS)
            kept["summ"] = jnp.pad(back.astype(bf16), more_rows).reshape(shards, summ_share, width)
            columns = jnp.concatenate(after(attn, *earlier), axis=1)
            kept["out"] = dot(columns, proj_rows, COLS_BY_ROWS).astype(bf16)
        made = project(g, grad_slots, after(qkv_own, *earlier), width)
        if g == 1:
            made, kept["out"] = after((made, kept["out"]))
        return made

    grad_normed = scattered_sum(
        grad_rows_back,
        groups,
        qkv_grad_of,
        side_work,
    )
    out_grad = kept["out"]
    result, up_grad, down_grad = kept["result"], kept["up"], kept["down"]
    if spread:
        out_grad = lax.psum_scatter(out_grad, "dp", scatter_dimension=0, tiled=True)
    else:
        out_grad = lax.psum_scatter(
            lax.dynamic_update_slice_in_dim(
                jnp.zeros((width, width), bf16), out_grad, position * own_width, 0
            ),
            BOTH,
            scatter_dimension=0,
            tiled=True,
        )
    out_grad = out_grad.astype(f32)
    grad_normed_summ = lax.all_to_all(kept["summ"], "fsdp", 0, 0, tiled=True)
    grad_normed_summ = jnp.sum(grad_normed_summ.astype(f32), axis=0)
    summ_own = lax.dynamic_slice_in_dim(
        jnp.pad(summ_inputs, more_rows),
        position * summ_share,
        summ_share,
        0,
    )
    qkv_grad = kept["qkv_parts"]
    if rows_held == HEAD and shards % 2 == 0:
        query_grad, key_grad, value_grad = spread_columns(qkv_grad)
    else:
        query_grad, key_grad, value_grad = (
            from_shards(qkv_grad[:, :, n * own_width : (n + 1) * own_width]).astype(f32)
            for n in range(3)
        )
    up_shift_grad = sum(unit_sums)
    query_shift_grad = jnp.concatenate([one[5][0] for one in pulled])
    value_shift_grad = jnp.concatenate([one[5][1] for one in pulled])
    grad_one, gain_one_grad, shift_one_grad = norm_back(inputs, gain_one, shift_one, grad_normed)
    grad_inputs = jnp.concatenate([grad_one[h] + grad_resid[h] for h in range(2)], axis=0)
    _, norm_summ_pull = jax.vjp(layer_norm, summ_own, gain_one, shift_one)
    grad_summ, gain_summ_grad, shift_summ_grad = norm_summ_pull(grad_normed_summ)
    summary_cols = summaries.shape[2]
    grad_summ = lax.all_to_all(
        grad_summ.reshape(summ_share, shards, summary_cols).transpose(1, 0, 2),
        "fsdp",
        0,
        0,
        tiled=True,
    )
    summary_grad = grad_summ.reshape(shards * summ_share, summary_cols)[:summary_rows]

    vector_grads = jnp.stack(
        [
            gain_one_grad + gain_summ_grad,
            shift_one_grad + shift_summ_grad,
            whole_columns(query_shift_grad),
            whole_columns(value_shift_grad),
            out_shift_grad,
            gain_two_grad,
            shift_two_grad,
            down_shift_grad,
        ]
    )
    vector_grads = vector_grads.reshape(8, devices, rows_held).transpose(1, 0, 2)
    unit_grads = lax.dynamic_update_index_in_dim(
        jnp.zeros((items, shards, units_held), f32),
        up_shift_grad.reshape(items, 1, units_held),
        position,
        1,
    )
    all_grads = jnp.concatenate(
        [vector_grads.reshape(devices, 8 * rows_held), unit_grads.reshape(devices, units_held)],
        axis=1,
    )
    all_grads = jnp.sum(lax.all_to_all(all_grads, BOTH, 0, 0, tiled=True), axis=0)
    (
        gain_one_grad, shift_one_grad, query_shift_grad, value_shift_grad, out_shift_grad,
        gain_two_grad, shift_two_grad, down_shift_grad,
    ) = (all_grads[n * rows_held : (n + 1) * rows_held] for n in range(8))
    up_shift_grad = all_grads[8 * rows_held :]
    return (
        result[None],
        grad_inputs[None],
        summary_grad[None],
        gain_one_grad,
        shift_one_grad,
        query_grad,
        query_shift_grad,
        key_grad,
        value_grad,
        value_shift_grad,
        out_grad,
        out_shift_grad,
        gain_two_grad,
        shift_two_grad,
        up_grad,
        up_shift_grad,
        down_grad,
        down_shift_grad,
    )


def solution(mesh):
    vector = P(BOTH)
    matrix = P(BOTH, None)
    rows = P("dp", "fsdp", None)
    columns = P("dp", None, "fsdp")
    return jax.shard_map(
        per_device,
        mesh=mesh,
        in_specs=(
            rows, columns, P("dp", None), P("dp"), rows, vector, vector, matrix, vector, matrix,
            matrix, vector, matrix, vector, vector, vector, matrix, vector, matrix, vector,
        ),
        out_specs=(
            rows, rows, columns, vector, vector, matrix, vector, matrix, matrix, vector, matrix,
            vector, vector, vector, matrix, vector, matrix, vector,
        ),
        check_vma=False,
    )
```

```python
import functools
import math

import jax
import jax.numpy as jnp
from jax import lax
from jax.experimental import pallas as pl
from jax.experimental.pallas import tpu as pltpu
from jax.sharding import PartitionSpec as P

HEAD = 64
SUMM = 50

epsilon = 1e-05
masked_score = -1e30
bf16 = jnp.bfloat16
f32 = jnp.float32
BOTH = ("dp", "fsdp")
score_scale = 1.0 / math.sqrt(HEAD)

ROWS_BY_ROWS = (((1,), (0,)), ((), ()))
ROWS_BY_COLS = (((1,), (1,)), ((), ()))
COLS_BY_ROWS = (((0,), (0,)), ((), ()))


def dot(left, right, dims):
    return lax.dot_general(left, right, dims, preferred_element_type=f32)


def layer_norm(values, gains, shifts):
    centre = jnp.mean(values, axis=-1, keepdims=True)
    centred = values - centre
    spread = jnp.mean(centred * centred, axis=-1, keepdims=True)
    return centred * lax.rsqrt(spread + epsilon) * gains + shifts


def gelu_tanh(values):
    return jax.nn.gelu(values, approximate=True)


def slot_order(devices):
    if devices == 8:
        return [
            (0, 0), (0, 1), (1, 0), (1, 1),
            (2, 0), (3, 0), (4, 1), (5, 1),
            (2, 1), (3, 1), (4, 0), (5, 0),
            (6, 0), (6, 1), (7, 0), (7, 1),
        ]
    return [(m, h) for m in range(devices) for h in range(2)]


def slot_groups(devices):
    return len(slot_order(devices)) // 4


def in_groups(items):
    return [items[n : n + 4] for n in range(0, len(items), 4)]


def swapped(x, bit):
    devices = lax.axis_size("fsdp")
    return lax.ppermute(x, "fsdp", [(i, i ^ bit) for i in range(devices)])


def sent(own):
    if lax.axis_size("fsdp") != 8:
        return None
    x0 = swapped(own[0], 2)
    y1 = swapped(own[1], 4)
    x1 = swapped(own[1], 2)
    y0 = swapped(own[0], 4)
    return x0, y1, x1, y0


def passed_on(own, hops, earlier=()):
    devices = lax.axis_size("fsdp")
    if devices != 8:
        pieces = [own]
        bit = 1
        while bit < devices:
            pieces = pieces + [[swapped(half, bit) for half in piece] for piece in pieces]
            bit *= 2
        return in_groups([half for piece in pieces for half in piece])
    x0, y1, x1, y0 = hops
    if earlier:
        x0, y1 = after((x0, y1), *earlier)
    a0 = swapped(x0, 4)
    a1 = swapped(y1, 2)
    return [
        [own[0], own[1], swapped(own[0], 1), swapped(own[1], 1)],
        [x0, swapped(x0, 1), y1, swapped(y1, 1)],
        [x1, swapped(x1, 1), y0, swapped(y0, 1)],
        [a0, a1, swapped(a0, 1), swapped(a1, 1)],
    ]


def total(*terms):
    result = terms[0].astype(f32)
    for term in terms[1:]:
        result = result + term.astype(f32)
    return result


def paired(own, other):
    return total(own, swapped(other, 1)).astype(bf16)


def plain_scattered_sum(groups):
    flat = [half for group in groups for half in group]
    bit = len(flat) // 4
    while bit > 1:
        flat = [
            total(flat[n], swapped(flat[n + 2 * bit], bit)).astype(bf16) for n in range(2 * bit)
        ]
        bit //= 2
    return [[flat[h], swapped(flat[h + 2], 1)] for h in range(2)]


def scattered_sum(make, groups, first=None, second=None):
    if groups != 4:
        made = [make(g, ()) for g in range(groups)]
        for extra in (first, second):
            if extra:
                done, use = extra(())
                use(done)
        return plain_scattered_sum(made)
    later = make(2, ())
    x1 = paired(later[0], later[1])
    y0 = paired(later[2], later[3])
    if first:
        done, use = first((x1, y0))
        x1, y0, done = after((swapped(x1, 2), swapped(y0, 4), done))
        use(done)
        far = make(3, (x1, y0))
    else:
        far = make(3, (x1, y0))
        far, x1, y0 = after((far, swapped(x1, 2), swapped(y0, 4)))
    a0 = paired(far[0], far[2])
    a1 = paired(far[1], far[3])
    near = make(1, (a0, a1))
    own = make(0, (a0, a1, near[0]))
    own, a0, a1 = after((own, swapped(a0, 4), swapped(a1, 2)))
    x0 = total(near[0], swapped(near[1], 1), a0).astype(bf16)
    y1 = total(near[2], swapped(near[3], 1), a1).astype(bf16)
    mine = [[own[0], swapped(own[2], 1), y0], [own[1], swapped(own[3], 1), x1]]
    done, use = second((x0, y1)) if second else ((), None)
    x0, y1, mine, done = after((swapped(x0, 2), swapped(y1, 4), mine, done))
    if use:
        use(done)
    return [mine[0] + [x0], mine[1] + [y1]]


def after(values, *earlier):
    flat, tree = jax.tree.flatten(values)
    flat = lax.optimization_barrier(tuple(flat) + earlier)[: len(flat)]
    return jax.tree.unflatten(tree, flat)


def held(shape, place=None):
    where = place or (0,) * len(shape)
    return pl.BlockSpec(shape, lambda *_: where, pipeline_mode=pl.Buffered(1))


anywhere = pl.BlockSpec(memory_space=pl.ANY)


def half_rows(chunk, width):
    return pl.BlockSpec((chunk, width), lambda s: (s, 0))


def group_rows(group, chunk, width):
    return pl.BlockSpec((4, chunk, width), lambda s: (group, s, 0))


def group_call(kernel, name, steps, ins, specs, outs, out_specs, earlier, scratch, flops, moved):
    aliases = {len(ins) + n: n for n in range(len(earlier))}
    made = pl.pallas_call(
        functools.partial(kernel, len(ins), len(earlier)),
        grid=(steps,),
        in_specs=specs + [anywhere] * len(earlier),
        out_specs=out_specs,
        out_shape=outs,
        scratch_shapes=scratch,
        input_output_aliases=aliases,
        compiler_params=pltpu.CompilerParams(
            dimension_semantics=("arbitrary",), vmem_limit_bytes=52 * 2**20
        ),
        cost_estimate=pl.CostEstimate(flops=flops, bytes_accessed=moved, transcendentals=0),
        name=name,
    )(*ins, *earlier)
    return list(made)


def split_refs(n_ins, n_earlier, refs):
    return refs[:n_ins], refs[n_ins + n_earlier :]


def norm_kernel(n_ins, n_earlier, *refs):
    ins, rest = split_refs(n_ins, n_earlier, refs)
    gain_ref, shift_ref = ins[4:]
    for n in range(4):
        rest[0][n] = layer_norm(
            ins[n][...].astype(f32), gain_ref[...], shift_ref[...]
        ).astype(bf16)


def norm_rows(group, halves, gain, shift, earlier, slots):
    half, wide = halves[0].shape
    chunk = half // 2
    return group_call(
        norm_kernel,
        "norm_rows",
        2,
        list(halves) + [gain, shift],
        [half_rows(chunk, wide)] * 4 + [held(gain.shape), held(shift.shape)],
        [jax.ShapeDtypeStruct((slots, half, wide), bf16)],
        [group_rows(group, chunk, wide)],
        earlier,
        [],
        80 * half * wide,
        16 * half * wide,
    )


def triple_kernel(n_ins, n_earlier, *refs):
    (rows_ref, weight_ref, bias_ref), outs = split_refs(n_ins, n_earlier, refs)
    width = outs[0].shape[1]
    made = (dot(rows_ref[...], weight_ref[...], ROWS_BY_ROWS) + bias_ref[...]).astype(bf16)
    for place in range(3):
        outs[place][...] = made[:, place * width : (place + 1) * width]


def triple(first, steps, rows, weight, bias, earlier, count):
    wide = rows.shape[1]
    size = count // slot_groups(lax.axis_size("fsdp"))
    width = weight.shape[1] // 3
    return group_call(
        triple_kernel,
        "triple",
        steps,
        [rows, weight, bias],
        [
            pl.BlockSpec((size, wide), lambda s: (s + first, 0)),
            held(weight.shape),
            held(bias.shape),
        ],
        [jax.ShapeDtypeStruct((count, width), bf16)] * 3,
        [pl.BlockSpec((size, width), lambda s: (s + first, 0))] * 3,
        earlier,
        [],
        6 * steps * size * wide * width,
        2 * steps * size * wide,
    )


def norm_back_kernel(count, low, *refs):
    values, terms, rest = refs[:2], refs[2 : 2 + 2 * count], refs[2 + 2 * count :]
    extra_ref, gain_ref, grad_ref, sum_ref = rest[:4]

    @pl.when(pl.program_id(0) == 0)
    def _():
        sum_ref[...] = jnp.zeros_like(sum_ref)

    def average(one):
        return jnp.mean(one, axis=-1, keepdims=True)

    def add_rows(place, one):
        sum_ref[place : place + 1, :] += jnp.sum(one, axis=0, keepdims=True)

    for h in range(2):
        value = values[h][...].astype(f32)
        grad = total(*[ref[...] for ref in terms[h * count : (h + 1) * count]])
        extra = extra_ref[h].astype(f32)
        centred = value - average(value)
        rate = lax.rsqrt(average(centred * centred) + epsilon)
        unit = centred * rate
        scaled = grad * gain_ref[...]
        back = (scaled - average(scaled) - unit * average(scaled * unit)) * rate + extra
        grad_ref[h] = back
        add_rows(0, grad * unit)
        add_rows(1, grad)
        if low:
            rounded = back.astype(bf16)
            rest[4 + h][...] = rounded
            add_rows(2, rounded.astype(f32))
            add_rows(3, extra)


def norm_back(values, sums, extra, gain, low):
    half, wide = values[0].shape
    chunk = min(half, 64)
    rows = half_rows(chunk, wide)
    both = pl.BlockSpec((2, chunk, wide), lambda s: (0, s, 0))
    outs = [
        jax.ShapeDtypeStruct((2, half, wide), f32), jax.ShapeDtypeStruct((8, wide), f32)
    ] + [jax.ShapeDtypeStruct((half, wide), bf16)] * (2 * low)
    return pl.pallas_call(
        functools.partial(norm_back_kernel, len(sums[0]), low),
        grid=(half // chunk,),
        in_specs=[rows] * (2 + 2 * len(sums[0])) + [both, held(gain.shape)],
        out_specs=[both, pl.BlockSpec((8, wide), lambda s: (0, 0))] + [rows] * (2 * low),
        out_shape=outs,
        compiler_params=pltpu.CompilerParams(
            dimension_semantics=("arbitrary",), vmem_limit_bytes=40 * 2**20
        ),
        cost_estimate=pl.CostEstimate(
            flops=80 * half * wide, bytes_accessed=36 * half * wide, transcendentals=0
        ),
        name="norm_back",
    )(*values, *sums[0], *sums[1], extra, gain)


def project_kernel(n_ins, n_earlier, *refs):
    ins, rest = split_refs(n_ins, n_earlier, refs)
    weight_ref, outs = ins[-1], rest[:4]
    chunk, wide = outs[0].shape
    parts = [ref[...].reshape(4 * chunk, ref.shape[2]) for ref in ins[:-1]]
    rows = parts[0] if len(parts) == 1 else jnp.concatenate(parts, axis=1)
    by_rows = weight_ref.shape[0] == rows.shape[1] and weight_ref.shape[1] == wide
    tile = min(wide, 512)
    for start in range(0, wide, tile):
        columns = slice(start, start + tile)
        if by_rows:
            made = dot(rows, weight_ref[:, columns], ROWS_BY_ROWS)
        else:
            made = dot(rows, weight_ref[columns, :], ROWS_BY_COLS)
        made = made.astype(bf16)
        for n in range(4):
            outs[n][:, columns] = made[n * chunk : (n + 1) * chunk, :]


def project(group, parts, weight, wide):
    half = parts[0].shape[1]
    chunk = half // 2
    return group_call(
        project_kernel,
        "project",
        2,
        list(parts) + [weight],
        [group_rows(group, chunk, part.shape[2]) for part in parts] + [held(weight.shape)],
        [jax.ShapeDtypeStruct((half, wide), bf16)] * 4,
        [half_rows(chunk, wide)] * 4,
        [],
        [],
        8 * half * weight.size,
        8 * half * wide + 2 * weight.size,
    )


def project_back_kernel(n_ins, n_earlier, *refs):
    ins, rest = split_refs(n_ins, n_earlier, refs)
    weight_ref = ins[4]
    made_ref, kept_ref, rows = rest
    chunk = ins[0].shape[0]
    for n in range(4):
        kept_ref[n] = ins[n][...]
        rows[n * chunk : (n + 1) * chunk, :] = ins[n][...]
    made = dot(rows[...], weight_ref[...], ROWS_BY_COLS).astype(bf16)
    for n in range(4):
        made_ref[n] = made[n * chunk : (n + 1) * chunk, :]


def project_back(group, halves, weight, earlier, slots):
    half, wide = halves[0].shape
    chunk = half // 2
    width = weight.shape[0]
    return group_call(
        project_back_kernel,
        "project_back",
        2,
        list(halves) + [weight],
        [half_rows(chunk, wide)] * 4 + [held(weight.shape)],
        [jax.ShapeDtypeStruct((slots, half, n), bf16) for n in (width, wide)],
        [group_rows(group, chunk, n) for n in (width, wide)],
        earlier,
        [pltpu.VMEM((4 * chunk, wide), bf16)],
        8 * half * weight.size,
        16 * half * wide,
    )


gelu_rate = math.sqrt(2.0 / math.pi)
gelu_cube = 0.044715


def feed_forward_kernel(n_ins, n_earlier, *refs):
    ins, rest = split_refs(n_ins, n_earlier, refs)
    up_ref, shift_ref, down_ref = ins[8:]
    active_ref, grad_ref, rows_ref, grad_rows_ref = rest[:4]
    back = rest[4:8]
    ahead = rest[8:12]
    shift_grad_ref, rows, grad_rows, active, grad_upper = rest[12:]
    chunk, wide = ins[0].shape
    units = up_ref.shape[1]
    for n in range(4):
        r = slice(n * chunk, (n + 1) * chunk)
        rows[r, :] = ins[n][...]
        grad_rows[r, :] = ins[4 + n][...]
        rows_ref[n] = ins[n][...]
        grad_rows_ref[n] = ins[4 + n][...]
    tile = min(units, 512)

    def hidden(t, carry):
        columns = pl.ds(pl.multiple_of(t * tile, tile), tile)
        upper = dot(rows[...], up_ref[:, columns], ROWS_BY_ROWS) + shift_ref[:, columns]
        grad_active = dot(grad_rows[...], down_ref[columns, :], ROWS_BY_COLS)
        square = upper * upper
        bend = jnp.tanh(gelu_rate * upper * (1.0 + gelu_cube * square))
        share = 0.5 * (1.0 + bend)
        slope = share + 0.5 * upper * (1.0 - bend * bend) * (
            gelu_rate * (1.0 + 3.0 * gelu_cube * square)
        )
        made = (upper * share).astype(bf16)
        grad = (grad_active * slope).astype(bf16)
        active[:, columns] = made
        grad_upper[:, columns] = grad
        shift_grad_ref[0, 0:1, columns] = jnp.sum(grad.astype(f32), axis=0, keepdims=True)
        for n in range(4):
            r = slice(n * chunk, (n + 1) * chunk)
            active_ref[n, :, columns] = made[r, :]
            grad_ref[n, :, columns] = grad[r, :]
        return carry

    lax.fori_loop(0, units // tile, hidden, 0)
    step = min(wide, 1024)

    def outer(t, carry):
        columns = pl.ds(pl.multiple_of(t * step, step), step)
        made_back = dot(grad_upper[...], up_ref[columns, :], ROWS_BY_COLS).astype(bf16)
        made_ahead = dot(active[...], down_ref[:, columns], ROWS_BY_ROWS).astype(bf16)
        for n in range(4):
            r = slice(n * chunk, (n + 1) * chunk)
            back[n][:, columns] = made_back[r, :]
            ahead[n][:, columns] = made_ahead[r, :]
        return carry

    lax.fori_loop(0, wide // step, outer, 0)


def feed_forward(group, halves, grad_halves, up, shift, down, earlier, slots):
    half, wide = halves[0].shape
    chunk = half // 2
    units = up.shape[1]
    sizes = (units, units, wide, wide)
    outs = [jax.ShapeDtypeStruct((slots, half, n), bf16) for n in sizes]
    outs += [jax.ShapeDtypeStruct((half, wide), bf16)] * 8
    outs += [jax.ShapeDtypeStruct((2, 8, units), f32)]
    made = group_call(
        feed_forward_kernel,
        "feed_forward",
        2,
        list(halves) + list(grad_halves) + [up, shift, down],
        [half_rows(chunk, wide)] * 8 + [held(up.shape), held(shift.shape), held(down.shape)],
        outs,
        [group_rows(group, chunk, n) for n in sizes]
        + [half_rows(chunk, wide)] * 8
        + [pl.BlockSpec((1, 8, units), lambda s: (s, 0, 0))],
        earlier,
        [pltpu.VMEM((4 * chunk, n), bf16) for n in (wide, wide, units, units)],
        32 * half * wide * units,
        48 * half * wide + 4 * wide * units,
    )
    return made[:4], made[4:8], made[8:12], jnp.sum(made[12][:, 0], axis=0)


def only_head(values, head):
    columns = lax.broadcasted_iota(jnp.int32, values.shape, 1) // HEAD
    return jnp.where(columns == head, values, jnp.zeros_like(values))


def transposed(values):
    return values.astype(f32).T.astype(bf16)


def places_of(plan_ref, blocks, subs, half, j):
    return [
        pl.ds(pl.multiple_of(plan_ref[3 * blocks + subs * j + n] * half, half), half)
        for n in range(subs)
    ]


def rows_of(ref, places):
    parts = [ref[place, :] for place in places]
    return parts[0] if len(parts) == 1 else jnp.concatenate(parts, axis=0)


def cols_of(ref, places):
    parts = [ref[:, place] for place in places]
    return parts[0] if len(parts) == 1 else jnp.concatenate(parts, axis=1)


def attn_forward_kernel(
    block, half, heads, plan_ref, q_ref, k_ref, v_ref, sk_ref, sv_ref, row_ref, o_ref, log_ref,
    q_heads, vt_all, svt, tops, sums, mixed,
):
    i = pl.program_id(0)
    blocks = pl.num_programs(0)
    subs = block // half

    @pl.when(i == 0)
    def _():
        for n in range(v_ref.shape[0] // half):
            r = slice(n * half, (n + 1) * half)
            vt_all[:, r] = transposed(v_ref[r, :])
        svt[...] = transposed(sv_ref[...])

    mine = places_of(plan_ref, blocks, subs, half, i)
    q = rows_of(q_ref, mine).astype(f32) * score_scale
    for h in range(heads):
        q_heads[h] = only_head(q, h).astype(bf16)
    tops[...] = jnp.full_like(tops, masked_score)
    sums[...] = jnp.zeros_like(sums)
    mixed[...] = jnp.zeros_like(mixed)
    lowest = row_ref[0:1, :]
    highest = row_ref[1:2, :]
    summ_end = row_ref[2:3, :]
    me = row_ref[3:4, :]

    def step(keys, values_t, mask):
        each = range(heads)
        scores = [dot(keys, q_heads[h], ROWS_BY_COLS) for h in each]
        if mask is not None:
            scores = [jnp.where(mask, one, masked_score) for one in scores]
        before = [tops[h : h + 1, :] for h in each]
        top = [jnp.maximum(before[h], jnp.max(scores[h], axis=0, keepdims=True)) for h in each]
        weights = [jnp.exp(scores[h] - top[h]) for h in each]
        keep = [jnp.exp(before[h] - top[h]) for h in each]
        added = [jnp.sum(weights[h], axis=0, keepdims=True) for h in each]
        totals = [keep[h] * sums[h : h + 1, :] + added[h] for h in each]
        part_of = [slice(h * HEAD, (h + 1) * HEAD) for h in each]
        more = [dot(values_t[part_of[h], :], weights[h].astype(bf16), ROWS_BY_ROWS) for h in each]
        result = [keep[h] * mixed[part_of[h], :] + more[h] for h in each]
        for h in each:
            tops[h : h + 1, :] = top[h]
            sums[h : h + 1, :] = totals[h]
            mixed[part_of[h], :] = result[h]

    @pl.when(plan_ref[2 * blocks + i] > 0)
    def _():
        places = lax.broadcasted_iota(jnp.int32, (sk_ref.shape[0], block), 0)
        step(sk_ref[...], svt[...], places < summ_end)

    def whole(j, carry):
        there = places_of(plan_ref, blocks, subs, half, j)
        step(rows_of(k_ref, there), cols_of(vt_all, there), None)
        return carry

    def part(j, carry):
        there = places_of(plan_ref, blocks, subs, half, j)
        places = j * block + lax.broadcasted_iota(jnp.int32, (block, block), 0)
        mask = ((places >= lowest) & (places <= highest)) | (places == me)
        step(rows_of(k_ref, there), cols_of(vt_all, there), mask)
        return carry

    lax.fori_loop(plan_ref[i], plan_ref[blocks + i], whole, 0)
    lax.fori_loop(plan_ref[blocks + i], i + 1, part, 0)
    for h in range(heads):
        r = slice(h * HEAD, (h + 1) * HEAD)
        mixed[r, :] = mixed[r, :] * (1.0 / sums[h : h + 1, :])
    log_ref[...] = tops[...] + jnp.log(jnp.maximum(sums[...], 1e-37))
    made = mixed[...].T.astype(bf16)
    for n, place in enumerate(mine):
        o_ref[place, :] = made[n * half : (n + 1) * half, :]


def attn_backward_kernel(
    block, half, heads, plan_ref, q_ref, k_ref, v_ref, sk_ref, sv_ref, row_ref, log_ref, o_ref, do_ref, dq_ref, dk_ref, dv_ref, dsk_ref, dsv_ref, shift_ref, q_heads, do_heads, kt_all, skt, dq_sum,
    dk_sum, dv_sum, dsk_sum, dsv_sum,
):
    i = pl.program_id(0)
    blocks = pl.num_programs(0)
    subs = block // half

    @pl.when(i == 0)
    def _():
        dk_sum[...] = jnp.zeros_like(dk_sum)
        dv_sum[...] = jnp.zeros_like(dv_sum)
        dsk_sum[...] = jnp.zeros_like(dsk_sum)
        dsv_sum[...] = jnp.zeros_like(dsv_sum)
        for n in range(k_ref.shape[0] // half):
            r = slice(n * half, (n + 1) * half)
            kt_all[:, r] = transposed(k_ref[r, :])
        skt[...] = transposed(sk_ref[...])

    mine = places_of(plan_ref, blocks, subs, half, i)
    q = rows_of(q_ref, mine).astype(f32) * score_scale
    do = rows_of(do_ref, mine).astype(f32)
    for h in range(heads):
        q_heads[h] = only_head(q, h).astype(bf16)
        do_heads[h] = only_head(do, h).astype(bf16)
    both_t = (do * rows_of(o_ref, mine).astype(f32)).T
    row_terms = [
        jnp.sum(both_t[h * HEAD : (h + 1) * HEAD, :], axis=0, keepdims=True) for h in range(heads)
    ]
    dq_sum[...] = jnp.zeros_like(dq_sum)
    lowest = row_ref[0:1, :]
    highest = row_ref[1:2, :]
    summ_end = row_ref[2:3, :]
    me = row_ref[3:4, :]

    def step(keys, values, keys_t, mask):
        dk = dv = None
        for h in range(heads):
            scores = dot(keys, q_heads[h], ROWS_BY_COLS)
            if mask is not None:
                scores = jnp.where(mask, scores, masked_score)
            probs = jnp.exp(scores - log_ref[h : h + 1, :])
            grad_probs = dot(values, do_heads[h], ROWS_BY_COLS)
            grad_scores = (probs * (grad_probs - row_terms[h])).astype(bf16)
            r = slice(h * HEAD, (h + 1) * HEAD)
            dq_sum[r, :] += dot(keys_t[r, :], grad_scores, ROWS_BY_ROWS)
            dv_own = dot(probs.astype(bf16), do_heads[h], ROWS_BY_ROWS)
            dk_own = dot(grad_scores, q_heads[h], ROWS_BY_ROWS)
            dv = dv_own if dv is None else dv + dv_own
            dk = dk_own if dk is None else dk + dk_own
        return dk, dv

    @pl.when(plan_ref[2 * blocks + i] > 0)
    def _():
        places = lax.broadcasted_iota(jnp.int32, (sk_ref.shape[0], block), 0)
        dk, dv = step(sk_ref[...], sv_ref[...], skt[...], places < summ_end)
        dsk_sum[...] += dk
        dsv_sum[...] += dv

    def whole(j, masked):
        there = places_of(plan_ref, blocks, subs, half, j)
        mask = None
        if masked:
            places = j * block + lax.broadcasted_iota(jnp.int32, (block, block), 0)
            mask = ((places >= lowest) & (places <= highest)) | (places == me)
        dk, dv = step(rows_of(k_ref, there), rows_of(v_ref, there), cols_of(kt_all, there), mask)
        for n, place in enumerate(there):
            dk_sum[place, :] += dk[n * half : (n + 1) * half, :]
            dv_sum[place, :] += dv[n * half : (n + 1) * half, :]

    def plain(j, carry):
        whole(j, False)
        return carry

    def part(j, carry):
        whole(j, True)
        return carry

    lax.fori_loop(plan_ref[i], plan_ref[blocks + i], plain, 0)
    lax.fori_loop(plan_ref[blocks + i], i + 1, part, 0)
    made = (dq_sum[...] * score_scale).T.astype(bf16)
    for n, place in enumerate(mine):
        dq_ref[place, :] = made[n * half : (n + 1) * half, :]

    @pl.when(i == blocks - 1)
    def _():
        dk_ref[...] = dk_sum[...].astype(bf16)
        dv_ref[...] = dv_sum[...].astype(bf16)
        dsk_ref[...] = dsk_sum[...].astype(bf16)
        dsv_ref[...] = dsv_sum[...].astype(bf16)

        def added(ref):
            return jnp.sum(ref[...].astype(f32), axis=0, keepdims=True)

        shift_ref[...] = jnp.zeros_like(shift_ref)
        shift_ref[0:1, :] = added(dq_ref)
        shift_ref[1:2, :] = added(dv_ref) + added(dsv_ref)


def attn_forward(part, parts, plan, rows, q, k, v, sk, sv, block, half):
    count = q.shape[0]
    width = q.shape[1] // parts
    heads = width // HEAD
    by_cols = pl.BlockSpec((8, block), lambda i, *_: (0, i))
    pairs = count * count // 4
    return pl.pallas_call(
        functools.partial(attn_forward_kernel, block, half, heads),
        grid_spec=pltpu.PrefetchScalarGridSpec(
            num_scalar_prefetch=1,
            grid=(count // block,),
            in_specs=[held((one.shape[0], width), (0, part)) for one in (q, k, v, sk, sv)] + [by_cols],
            out_specs=[held((count, width)), by_cols],
            scratch_shapes=[
                pltpu.VMEM((heads, block, width), bf16),
                pltpu.VMEM((width, count), bf16),
                pltpu.VMEM((width, sk.shape[0]), bf16),
                pltpu.VMEM((8, block), f32),
                pltpu.VMEM((8, block), f32),
                pltpu.VMEM((width, block), f32),
            ],
        ),
        out_shape=[
            jax.ShapeDtypeStruct((count, width), bf16),
            jax.ShapeDtypeStruct((8, count), f32),
        ],
        compiler_params=pltpu.CompilerParams(
            dimension_semantics=("arbitrary",), vmem_limit_bytes=40 * 2**20
        ),
        cost_estimate=pl.CostEstimate(
            flops=16 * pairs * width, bytes_accessed=8 * count * width, transcendentals=pairs * heads
        ),
        name="attn_forward",
    )(plan, q, k, v, sk, sv, rows)


def attn_backward(part, parts, plan, rows, q, k, v, sk, sv, logs, o, do, block, half):
    count = q.shape[0]
    width = q.shape[1] // parts
    heads = width // HEAD
    by_cols = pl.BlockSpec((8, block), lambda i, *_: (0, i))
    pairs = count * count // 4
    long = jax.ShapeDtypeStruct((count, width), bf16)
    short = jax.ShapeDtypeStruct((sk.shape[0], width), bf16)
    shift = jax.ShapeDtypeStruct((8, width), f32)
    long_in = held((count, width), (0, part))
    short_in = held((sk.shape[0], width), (0, part))
    return pl.pallas_call(
        functools.partial(attn_backward_kernel, block, half, heads),
        grid_spec=pltpu.PrefetchScalarGridSpec(
            num_scalar_prefetch=1,
            grid=(count // block,),
            in_specs=[long_in] * 3
            + [short_in] * 2
            + [by_cols] * 2
            + [held((count, width)), long_in],
            out_specs=[held(one.shape) for one in (long, long, long, short, short, shift)],
            scratch_shapes=[
                pltpu.VMEM((heads, block, width), bf16),
                pltpu.VMEM((heads, block, width), bf16),
                pltpu.VMEM((width, count), bf16),
                pltpu.VMEM((width, sk.shape[0]), bf16),
                pltpu.VMEM((width, block), f32),
                pltpu.VMEM((count, width), f32),
                pltpu.VMEM((count, width), f32),
                pltpu.VMEM((sk.shape[0], width), f32),
                pltpu.VMEM((sk.shape[0], width), f32),
            ],
        ),
        out_shape=[long, long, long, short, short, shift],
        compiler_params=pltpu.CompilerParams(
            dimension_semantics=("arbitrary",), vmem_limit_bytes=48 * 2**20
        ),
        cost_estimate=pl.CostEstimate(
            flops=24 * pairs * width, bytes_accessed=20 * count * width, transcendentals=pairs * heads
        ),
        name="attn_backward",
    )(plan, q, k, v, sk, sv, rows, logs, o, do)


def spread_columns_kernel(parts_ref, *outs):
    shards = parts_ref.shape[0]
    width = parts_ref.shape[2] // 3
    for n, ref in enumerate(outs):
        for d in range(width // HEAD):
            start = n * width + d * HEAD
            for f in range(0, shards, 2):
                pair = [parts_ref[f + m, :, start : start + HEAD].astype(f32) for m in range(2)]
                place = (d * shards + f) * HEAD
                ref[:, place : place + 2 * HEAD] = jnp.concatenate(pair, axis=1)


def spread_columns(parts):
    shards, count, width = parts.shape
    return pl.pallas_call(
        spread_columns_kernel,
        out_shape=[jax.ShapeDtypeStruct((count, shards * width // 3), f32)] * 3,
        name="spread_columns",
    )(parts)


def attention_plan(lengths, padding, count, block, slots):
    places = jnp.arange(count, dtype=jnp.int32)
    ends = jnp.cumsum(lengths)
    passed = places[:, None] >= ends[None, :]
    segment = jnp.sum(passed.astype(jnp.int32), axis=1)
    lowest = jnp.max(jnp.where(passed, ends[None, :], 0), axis=1)
    living = count - padding
    highest = jnp.minimum(places, living - 1)
    nothing = jnp.zeros_like(places)
    rows = jnp.stack(
        [lowest, highest, segment * SUMM, places, nothing, nothing, nothing, nothing], axis=0
    )
    blocks = count // block
    starts = jnp.arange(blocks, dtype=jnp.int32) * block
    first = lowest.reshape(blocks, block)[:, 0] // block
    one_piece = lowest.reshape(blocks, block)[:, -1] <= first * block
    whole_end = jnp.maximum(jnp.minimum(starts, living) // block, first)
    split = jnp.where(one_piece, whole_end, first)
    summ_flag = (segment.reshape(blocks, block)[:, -1] > 0).astype(jnp.int32)
    return rows, jnp.concatenate([first, split, summ_flag, slots]).astype(jnp.int32)


def per_device(
    tokens,
    summaries,
    segment_lengths,
    pad_lengths,
    output_grad,
    norm1_gain,
    norm1_bias,
    query_weight,
    query_bias,
    key_weight,
    value_weight,
    value_bias,
    out_weight,
    out_bias,
    norm2_gain,
    norm2_bias,
    up_weight,
    up_bias,
    down_weight,
    down_bias,
):
    shards = lax.axis_size("fsdp")
    items = lax.axis_size("dp")
    devices = shards * items
    position = lax.axis_index("fsdp")
    tok_rows = tokens.shape[1]
    width = tokens.shape[2]
    count = tok_rows * shards
    own_width = width // shards
    rows_held = query_weight.shape[0]
    units_held = up_bias.shape[0]
    own_units = units_held * items
    hidden = units_held * devices
    summary_rows = summaries.shape[1]
    padded_summ = -(-summary_rows // 32) * 32
    spread = rows_held % HEAD == 0
    block = math.gcd(count, 512)

    def for_shards(weight):
        if spread:
            split = weight.reshape(rows_held, items, shards, rows_held)
            return split.transpose(2, 0, 1, 3).reshape(shards, rows_held, own_width)
        return weight.reshape(rows_held, shards, own_width).transpose(1, 0, 2)

    def from_shards(parts):
        if spread:
            split = parts.reshape(shards, rows_held, items, rows_held)
            return split.transpose(1, 2, 0, 3).reshape(rows_held, width)
        return parts.transpose(1, 0, 2).reshape(rows_held, width)

    def own_columns(vector):
        if spread:
            split = vector.reshape(items, shards, rows_held)
            return lax.dynamic_index_in_dim(split, position, 1, keepdims=False).reshape(own_width)
        return lax.dynamic_slice_in_dim(vector, position * own_width, own_width, 0)

    def whole_columns(vector):
        if spread:
            split = jnp.zeros((items, shards, rows_held), f32)
            return lax.dynamic_update_index_in_dim(
                split, vector.reshape(items, 1, rows_held), position, 1
            ).reshape(width)
        return lax.dynamic_update_slice_in_dim(
            jnp.zeros((width,), f32), vector, position * own_width, 0
        )

    half = tok_rows // 2
    order = slot_order(shards)
    groups = len(order) // 4
    eight = shards == 8

    def halves(whole):
        return [whole[:half], whole[half:]]

    def flat(slotted):
        return slotted.reshape(count, slotted.shape[2])

    def slot_rows(slotted):
        return slotted.reshape(slotted.shape[0] * half, slotted.shape[2])

    qkv_parts = jnp.concatenate(
        [for_shards(query_weight), for_shards(key_weight), for_shards(value_weight)], axis=2
    )
    qkv_parts = lax.all_to_all(qkv_parts, "fsdp", 0, 0, tiled=True)
    qkv_own = lax.all_gather(
        qkv_parts.reshape(shards * rows_held, 3 * own_width), "dp", axis=0, tiled=True
    )
    vectors = jnp.concatenate(
        [
            norm1_gain, norm1_bias, query_bias, value_bias, out_bias, norm2_gain, norm2_bias,
            down_bias, up_bias,
        ]
    ).astype(f32)
    vectors = lax.all_to_all(
        jnp.broadcast_to(vectors[None], (devices, vectors.shape[0])), BOTH, 0, 0, tiled=True
    )
    gain_one, shift_one, query_shift, value_shift, out_shift, gain_two, shift_two, down_shift = (
        vectors[:, n * rows_held : (n + 1) * rows_held].reshape(width) for n in range(8)
    )
    token_halves = after(halves(tokens[0]), qkv_parts, vectors)
    token_hops = sent(token_halves)
    grad_own = halves(output_grad[0])
    up_parts = up_weight.reshape(rows_held, items, shards, units_held).transpose(2, 0, 1, 3)
    up_parts = up_parts.reshape(shards, rows_held, own_units)
    more_slots = -(-padded_summ // half)

    query_shift = own_columns(query_shift)
    value_shift = own_columns(value_shift)
    qkv_shift = jnp.concatenate([query_shift, jnp.zeros_like(query_shift), value_shift])[None]

    def normed_group(g, group, normed):
        return norm_rows(
            g, group, gain_one[None], shift_one[None], normed, 4 * groups + more_slots
        )

    if eight:
        mine = [*token_halves, *[swapped(one, 1) for one in token_halves]]
        normed = normed_group(0, mine, [])
        x0, y1, x1, y0 = token_hops
        x0, y1, x1, y0 = after((x0, y1, x1, y0), normed[0], up_parts, *grad_own)
        a0, a1 = swapped(x0, 4), swapped(y1, 2)
        normed = normed_group(1, [x0, swapped(x0, 1), y1, swapped(y1, 1)], normed)
        normed = normed_group(2, [x1, swapped(x1, 1), y0, swapped(y0, 1)], normed)
        made = triple(0, groups - 1, slot_rows(normed[0]), qkv_own, qkv_shift, [], count)
        a0, a1, made = after((a0, a1, made))
        last_tokens = [a0, a1, swapped(a0, 1), swapped(a1, 1)]
    else:
        normed = []
        token_groups = passed_on(token_halves, token_hops)
        last_tokens = token_groups[-1]
        for g in range(groups - 1):
            normed = normed_group(g, token_groups[g], normed)
        made = triple(0, groups - 1, slot_rows(normed[0]), qkv_own, qkv_shift, [], count)
    up_shift = lax.dynamic_index_in_dim(
        vectors[:, 8 * rows_held :].reshape(items, shards, units_held), position, 1, keepdims=False
    ).reshape(1, own_units)

    early = token_hops[:2] if eight else ()
    if spread:
        both = after(jnp.concatenate([out_weight, down_weight], axis=0), *early)
        both = lax.all_gather(both, "dp", axis=0)
        out_own = both[:, :rows_held].reshape(own_width, width)
        down_shares = both
    else:
        out_own = lax.dynamic_slice_in_dim(
            lax.all_gather(out_weight, BOTH, axis=0, tiled=True), position * own_width, own_width, 0
        )
        down_shares = lax.all_gather(down_weight, "dp", axis=0)
    up_parts = after(up_parts, last_tokens[0])
    up_parts = lax.all_to_all(up_parts, "fsdp", 0, 0, tiled=True)
    grad_own = after(grad_own, *last_tokens)
    grad_hops = sent(grad_own)

    summ_full = after(
        jnp.broadcast_to(summaries, (shards,) + summaries.shape[1:]), last_tokens[0]
    )
    summ_full = lax.all_to_all(summ_full, "fsdp", 0, 0, tiled=True)
    normed = normed_group(groups - 1, last_tokens, normed)
    queries, keys, values = triple(
        groups - 1, 1, slot_rows(normed[0]), qkv_own, qkv_shift, made, count
    )
    queries, keys, values, summ_full = after((queries, keys, values, summ_full))
    summ_full = summ_full.transpose(1, 0, 2).reshape(summary_rows, width)
    summ_inputs = jnp.pad(summ_full, ((0, padded_summ - summary_rows), (0, 0))).astype(f32)
    normed_summ = layer_norm(summ_inputs, gain_one, shift_one).astype(bf16)
    extra_rows = ((0, more_slots * half - padded_summ), (0, 0))
    normed = lax.dynamic_update_slice(
        slot_rows(normed[0]), jnp.pad(normed_summ, extra_rows), (count, 0)
    )
    summ_qkv = dot(normed_summ, qkv_own, ROWS_BY_ROWS) + qkv_shift
    summ_keys = summ_qkv[:, own_width : 2 * own_width].astype(bf16)
    summ_values = summ_qkv[:, 2 * own_width :].astype(bf16)
    slot_of = [[order.index((m, h)) for h in range(2)] for m in range(shards)]
    slots = jnp.array(slot_of, jnp.int32)[jnp.arange(shards) ^ position].reshape(-1)
    rows, plan = attention_plan(segment_lengths[0], pad_lengths[0], count, block, slots)
    parts = 2 if own_width % 256 == 0 else 1
    attn = []
    logs = []
    for part in range(parts):
        one, log = attn_forward(
            part, parts, plan, rows, queries, keys, values, summ_keys, summ_values, block, half
        )
        if eight and part == 0:
            one, log, plan, *grad_hops = after((one, log, plan, *grad_hops))
            x0, y1, x1, y0 = grad_hops
            a0, a1 = swapped(x0, 4), swapped(y1, 2)
        elif eight:
            one, log, a0, a1, up_parts, out_own = after((one, log, a0, a1, up_parts, out_own))
            grad_groups = [
                [*grad_own, swapped(grad_own[0], 1), swapped(grad_own[1], 1)],
                [x0, swapped(x0, 1), y1, swapped(y1, 1)],
                [x1, swapped(x1, 1), y0, swapped(y0, 1)],
                [a0, a1, swapped(a0, 1), swapped(a1, 1)],
            ]
        attn.append(one)
        logs.append(log)
    if not eight:
        grad_groups = passed_on(grad_own, grad_hops)
    up_own = lax.all_gather(
        up_parts.reshape(shards * rows_held, own_units), "dp", axis=0, tiled=True
    )
    attn_slots = [one.reshape(4 * groups, half, own_width // parts) for one in attn]
    inputs = [one.astype(f32) for one in halves(tokens[0])]
    proj_sums = scattered_sum(
        lambda g, earlier: project(g, attn_slots, after(out_own, *earlier), width), groups
    )
    resid = [
        total(inputs[h], *proj_sums[h]) + out_shift for h in range(2)
    ]

    normed_two_own = [layer_norm(one, gain_two, shift_two).astype(bf16) for one in resid]
    two_hops = sent(normed_two_own)
    down_own = after(down_shares, *normed_two_own)[:, down_shares.shape[1] - units_held :]
    down_own = down_own.reshape(own_units, width)
    if eight:
        x0, y1, x1, y0 = two_hops
        x0, y1, down_own = after((x0, y1, down_own))
        two_hops = (x0, y1, x1, y0)
    two_groups = passed_on(normed_two_own, two_hops)
    made = []
    back = {}
    ahead = {}
    unit_sums = []

    def feed(g, earlier):
        nonlocal made
        for n in [1, 2, 3, 0] if eight else range(groups):
            if n not in back and g not in back:
                mine = two_groups[n]
                if n == 2 and eight:
                    x1, y0 = after((mine[0], mine[2]), back[1][0])
                    mine = [x1, swapped(x1, 1), y0, swapped(y0, 1)]
                made, back[n], ahead[n], unit_sum = feed_forward(
                    n, mine, grad_groups[n], up_own, up_shift, after(down_own, *earlier),
                    made, 4 * groups,
                )
                unit_sums.append(unit_sum)
        return back[g]

    kept = {}

    def down_grad_of(earlier):
        active, _, _, grad_rows = (flat(one) for one in made)
        grad = dot(after(active, *earlier), grad_rows, COLS_BY_ROWS).astype(bf16)
        return grad, functools.partial(kept.__setitem__, "down")

    def up_grad_of(earlier):
        _, grad_upper, normed_two, _ = (flat(one) for one in feed_made)
        return dot(after(normed_two, *earlier), grad_upper, COLS_BY_ROWS).astype(bf16)

    grad_normed_two = scattered_sum(feed, groups, None, down_grad_of)
    feed_made = made
    down_grad = lax.psum_scatter(kept["down"], "dp", scatter_dimension=0, tiled=True)
    grad_resid, sums_two, *grad_proj = norm_back(
        resid, grad_normed_two, output_grad.reshape(2, half, width), gain_two[None], True
    )

    proj_hops = sent(grad_proj)
    if eight:
        mine = grad_proj + [swapped(one, 1) for one in grad_proj]
        made = project_back(0, mine, out_own, [], 4 * groups)
        up_grad = up_grad_of((made[0],))
        x0, y1, x1, y0, up_grad = after((*proj_hops, up_grad))
        own, near, later, far = after([ahead[g] for g in range(groups)], up_grad)
        sends = [
            paired(later[0], later[1]), paired(later[2], later[3]),
            paired(far[0], far[2]), paired(far[1], far[3]),
        ]
        near = [total(near[0], swapped(near[1], 1)), total(near[2], swapped(near[3], 1))]
        own = [total(own[0], swapped(own[2], 1)), total(own[1], swapped(own[3], 1))]
        a0, a1 = swapped(x0, 4), swapped(y1, 2)
        made = project_back(
            1, [x0, swapped(x0, 1), y1, swapped(y1, 1)], out_own, made, 4 * groups
        )
        made = project_back(
            2, [x1, swapped(x1, 1), y0, swapped(y0, 1)], out_own, made, 4 * groups
        )
        a0, a1, made, near, own, sends = after((a0, a1, made, near, own, sends))
        proj_groups = [None, None, None, [a0, a1, swapped(a0, 1), swapped(a1, 1)]]
    else:
        up_grad = up_grad_of(())
        made = []
        proj_groups = passed_on(grad_proj, proj_hops)
    up_grad = lax.psum_scatter(up_grad, "dp", scatter_dimension=0, tiled=True)
    up_grad = up_grad.reshape(shards, rows_held, own_units)
    if not eight:
        up_grad = lax.all_to_all(up_grad, "fsdp", 0, 0, tiled=True)
    ahead = [ahead[g] for g in range(groups)]
    for g in range(groups - 1 if eight else 0, groups):
        halves_now = proj_groups[g]
        made = project_back(g, halves_now, out_own, made, 4 * groups)
    grad_attn, proj_rows = (flat(one) for one in made)
    grad_attn, down_grad = after((grad_attn, down_grad))
    if eight:
        x1, y0, a0, a1 = after(sends, *proj_groups[-1])
        travelling = [swapped(x1, 2), swapped(y0, 4), swapped(a0, 4), swapped(a1, 2)]
    else:
        result = plain_scattered_sum(ahead)
    pulled = []
    again = grad_attn
    for part in range(parts):
        one = list(attn_backward(
            part, parts, plan, rows, queries, keys, values, summ_keys, summ_values, logs[part],
            attn[part], again, block, half,
        ))
        if eight and part == 0:
            one, again, *travelling = after((one, again, *travelling))
            x1, y0, a0, a1 = travelling
            x0, y1 = total(near[0], a0).astype(bf16), total(near[1], a1).astype(bf16)
            travelling = [swapped(x0, 2), swapped(y1, 4)]
            up_grad = after(up_grad, x0, y1)
            up_grad = lax.all_to_all(up_grad, "fsdp", 0, 0, tiled=True)
        elif eight:
            one, up_grad, *travelling = after((one, up_grad, *travelling))
        pulled.append(one)
    grad_slots = [
        pulled[part][n].reshape(4 * groups, half, own_width // parts)
        for n in range(3)
        for part in range(parts)
    ]
    grad_summ_kv = jnp.concatenate(
        [pulled[part][n] for n in (3, 4) for part in range(parts)], axis=1
    )

    summ_share = -(-padded_summ // (shards * 16)) * 16
    more_rows = ((0, summ_share * shards - padded_summ), (0, 0))

    def qkv_grad_of(earlier):
        slots_now, summ_now = after((grad_slots, grad_summ_kv), *earlier)
        grad_qkv = jnp.concatenate([flat(one) for one in slots_now], axis=1)
        grad_qkv = jnp.concatenate(
            [grad_qkv, jnp.pad(summ_now, (extra_rows[0], (own_width, 0)))], axis=0
        )
        grad = dot(normed, grad_qkv, COLS_BY_ROWS).astype(bf16)
        return grad, functools.partial(kept.__setitem__, "qkv")

    def side_work(earlier):
        kept["late"] = earlier
        grad = lax.psum_scatter(kept["qkv"], "dp", scatter_dimension=0, tiled=True)
        up_now, down_now, result_parts = after((up_grad, down_grad, result_terms), *earlier)
        grad = after(grad, *earlier).reshape(shards, rows_held, 3 * own_width)
        kept["qkv_parts"] = lax.all_to_all(grad, "fsdp", 0, 0, tiled=True)
        made = jnp.concatenate(
            [(total(*result_parts[h]) + down_shift).astype(bf16) for h in range(2)], axis=0
        )
        up_now = up_now.reshape(shards, rows_held, items, units_held).transpose(1, 2, 0, 3)
        up_now = up_now.reshape(rows_held, hidden).astype(f32)

        def use(done):
            kept.update(zip(("qkv_parts", "result", "up", "down"), done))

        return (kept["qkv_parts"], made, up_now, down_now.astype(f32)), use

    if eight:
        x0, y1 = travelling
        result_terms = [(resid[0], own[0], y0, x0), (resid[1], own[1], x1, y1)]
    else:
        result_terms = [(resid[h], *result[h]) for h in range(2)]

    def grad_rows_back(g, earlier):
        if g == 1 or not eight:
            back = dot(after(grad_summ_kv, *earlier), qkv_own[:, own_width:], ROWS_BY_COLS)
            kept["summ"] = jnp.pad(back.astype(bf16), more_rows).reshape(shards, summ_share, width)
            columns = jnp.concatenate(after(attn, *earlier), axis=1)
            kept["out"] = dot(columns, proj_rows, COLS_BY_ROWS).astype(bf16)
        made = project(g, grad_slots, after(qkv_own, *earlier), width)
        if g == 1:
            made, kept["out"] = after((made, kept["out"]))
        return made

    grad_normed = scattered_sum(
        grad_rows_back,
        groups,
        qkv_grad_of,
        side_work,
    )
    out_grad = kept["out"]
    result, up_grad, down_grad = kept["result"], kept["up"], kept["down"]
    if spread:
        out_grad = lax.psum_scatter(out_grad, "dp", scatter_dimension=0, tiled=True)
    else:
        out_grad = lax.psum_scatter(
            lax.dynamic_update_slice_in_dim(
                jnp.zeros((width, width), bf16), out_grad, position * own_width, 0
            ),
            BOTH,
            scatter_dimension=0,
            tiled=True,
        )
    out_grad = out_grad.astype(f32)
    grad_normed_summ = lax.all_to_all(kept["summ"], "fsdp", 0, 0, tiled=True)
    grad_normed_summ = after(grad_normed_summ, *kept["late"])
    grad_normed_summ = jnp.sum(grad_normed_summ.astype(f32), axis=0)
    summ_own = lax.dynamic_slice_in_dim(
        jnp.pad(summ_inputs, more_rows),
        position * summ_share,
        summ_share,
        0,
    )
    qkv_grad = kept["qkv_parts"]
    if rows_held == HEAD and shards % 2 == 0:
        query_grad, key_grad, value_grad = spread_columns(qkv_grad)
    else:
        query_grad, key_grad, value_grad = (
            from_shards(qkv_grad[:, :, n * own_width : (n + 1) * own_width]).astype(f32)
            for n in range(3)
        )
    up_shift_grad = sum(unit_sums)
    query_shift_grad = jnp.concatenate([one[5][0] for one in pulled])
    value_shift_grad = jnp.concatenate([one[5][1] for one in pulled])
    grad_inputs, sums_one = norm_back(
        halves(tokens[0]), grad_normed, grad_resid, gain_one[None], False
    )
    grad_inputs = grad_inputs.reshape(tok_rows, width)
    _, norm_summ_pull = jax.vjp(layer_norm, summ_own, gain_one, shift_one)
    grad_summ, gain_summ_grad, shift_summ_grad = norm_summ_pull(grad_normed_summ)
    summary_cols = summaries.shape[2]
    grad_summ = lax.all_to_all(
        after(grad_summ, sums_one).reshape(summ_share, shards, summary_cols).transpose(1, 0, 2),
        "fsdp",
        0,
        0,
        tiled=True,
    )
    summary_grad = grad_summ.reshape(shards * summ_share, summary_cols)[:summary_rows]

    vector_grads = jnp.stack(
        [
            sums_one[0] + gain_summ_grad,
            sums_one[1] + shift_summ_grad,
            whole_columns(query_shift_grad),
            whole_columns(value_shift_grad),
            sums_two[2],
            sums_two[0],
            sums_two[1],
            sums_two[3],
        ]
    )
    vector_grads = vector_grads.reshape(8, devices, rows_held).transpose(1, 0, 2)
    unit_grads = lax.dynamic_update_index_in_dim(
        jnp.zeros((items, shards, units_held), f32),
        up_shift_grad.reshape(items, 1, units_held),
        position,
        1,
    )
    all_grads = jnp.concatenate(
        [vector_grads.reshape(devices, 8 * rows_held), unit_grads.reshape(devices, units_held)],
        axis=1,
    )
    all_grads = jnp.sum(lax.all_to_all(all_grads, BOTH, 0, 0, tiled=True), axis=0)
    (
        gain_one_grad, shift_one_grad, query_shift_grad, value_shift_grad, out_shift_grad,
        gain_two_grad, shift_two_grad, down_shift_grad,
    ) = (all_grads[n * rows_held : (n + 1) * rows_held] for n in range(8))
    up_shift_grad = all_grads[8 * rows_held :]
    return (
        result[None],
        grad_inputs[None],
        summary_grad[None],
        gain_one_grad,
        shift_one_grad,
        query_grad,
        query_shift_grad,
        key_grad,
        value_grad,
        value_shift_grad,
        out_grad,
        out_shift_grad,
        gain_two_grad,
        shift_two_grad,
        up_grad,
        up_shift_grad,
        down_grad,
        down_shift_grad,
    )


def solution(mesh):
    vector = P(BOTH)
    matrix = P(BOTH, None)
    rows = P("dp", "fsdp", None)
    columns = P("dp", None, "fsdp")
    return jax.shard_map(
        per_device,
        mesh=mesh,
        in_specs=(
            rows, columns, P("dp", None), P("dp"), rows, vector, vector, matrix, vector, matrix,
            matrix, vector, matrix, vector, vector, vector, matrix, vector, matrix, vector,
        ),
        out_specs=(
            rows, rows, columns, vector, vector, matrix, vector, matrix, matrix, vector, matrix,
            vector, vector, vector, matrix, vector, matrix, vector,
        ),
        check_vma=False,
    )
```

```python
import functools
import math

import jax
import jax.numpy as jnp
from jax import lax
from jax.experimental import pallas as pl
from jax.experimental.pallas import tpu as pltpu
from jax.sharding import PartitionSpec as P

HEAD = 64
SUMM = 50

epsilon = 1e-05
masked_score = -1e30
bf16 = jnp.bfloat16
f32 = jnp.float32
BOTH = ("dp", "fsdp")
score_scale = 1.0 / math.sqrt(HEAD)

ROWS_BY_ROWS = (((1,), (0,)), ((), ()))
ROWS_BY_COLS = (((1,), (1,)), ((), ()))
COLS_BY_ROWS = (((0,), (0,)), ((), ()))


def dot(left, right, dims):
    return lax.dot_general(left, right, dims, preferred_element_type=f32)


def layer_norm(values, gains, shifts):
    centre = jnp.mean(values, axis=-1, keepdims=True)
    centred = values - centre
    spread = jnp.mean(centred * centred, axis=-1, keepdims=True)
    return centred * lax.rsqrt(spread + epsilon) * gains + shifts


def gelu_tanh(values):
    return jax.nn.gelu(values, approximate=True)


def slot_order(devices):
    if devices == 8:
        return [
            (0, 0), (0, 1), (1, 0), (1, 1),
            (2, 0), (3, 0), (4, 1), (5, 1),
            (2, 1), (3, 1), (4, 0), (5, 0),
            (6, 0), (6, 1), (7, 0), (7, 1),
        ]
    return [(m, h) for m in range(devices) for h in range(2)]


def slot_groups(devices):
    return len(slot_order(devices)) // 4


def in_groups(items):
    return [items[n : n + 4] for n in range(0, len(items), 4)]


def swapped(x, bit):
    devices = lax.axis_size("fsdp")
    return lax.ppermute(x, "fsdp", [(i, i ^ bit) for i in range(devices)])


def sent(own):
    if lax.axis_size("fsdp") != 8:
        return None
    x0 = swapped(own[0], 2)
    y1 = swapped(own[1], 4)
    x1 = swapped(own[1], 2)
    y0 = swapped(own[0], 4)
    return x0, y1, x1, y0


def passed_on(own, hops, earlier=()):
    devices = lax.axis_size("fsdp")
    if devices != 8:
        pieces = [own]
        bit = 1
        while bit < devices:
            pieces = pieces + [[swapped(half, bit) for half in piece] for piece in pieces]
            bit *= 2
        return in_groups([half for piece in pieces for half in piece])
    x0, y1, x1, y0 = hops
    if earlier:
        x0, y1 = after((x0, y1), *earlier)
    a0 = swapped(x0, 4)
    a1 = swapped(y1, 2)
    return [
        [own[0], own[1], swapped(own[0], 1), swapped(own[1], 1)],
        [x0, swapped(x0, 1), y1, swapped(y1, 1)],
        [x1, swapped(x1, 1), y0, swapped(y0, 1)],
        [a0, a1, swapped(a0, 1), swapped(a1, 1)],
    ]


def total(*terms):
    result = terms[0].astype(f32)
    for term in terms[1:]:
        result = result + term.astype(f32)
    return result


def low_sums_kernel(counts, *refs):
    place = 0
    for count, out in zip(counts, refs[sum(counts) :]):
        terms = [ref[...].reshape(out.shape) for ref in refs[place : place + count]]
        out[...] = total(*terms).astype(bf16)
        place += count


def low_sums(*lists):
    half, wide = lists[0][0].shape
    chunk = half // 2
    rows = pl.BlockSpec((chunk, wide), lambda s: (s, 0))
    terms = [term for one in lists for term in one]

    def place_of(term):
        if not isinstance(term, tuple):
            return rows
        return pl.BlockSpec((1, chunk, wide), lambda s, slot=term[1]: (slot, s, 0))

    return pl.pallas_call(
        functools.partial(low_sums_kernel, [len(one) for one in lists]),
        grid=(2,),
        in_specs=[place_of(term) for term in terms],
        out_specs=[rows] * len(lists),
        out_shape=[jax.ShapeDtypeStruct((half, wide), bf16)] * len(lists),
        compiler_params=pltpu.CompilerParams(
            dimension_semantics=("arbitrary",), vmem_limit_bytes=32 * 2**20
        ),
        cost_estimate=pl.CostEstimate(
            flops=half * wide * len(terms),
            bytes_accessed=2 * half * wide * (len(terms) + len(lists)),
            transcendentals=0,
        ),
        name="low_sums",
    )(*[term[0] if isinstance(term, tuple) else term for term in terms])


def plain_scattered_sum(groups):
    flat = [half for group in groups for half in group]
    bit = len(flat) // 4
    while bit > 1:
        flat = [
            total(flat[n], swapped(flat[n + 2 * bit], bit)).astype(bf16) for n in range(2 * bit)
        ]
        bit //= 2
    return [[flat[h], swapped(flat[h + 2], 1)] for h in range(2)]


def scattered_sum(make, groups, first=None, second=None):
    if groups != 4:
        made = [make(g, ()) for g in range(groups)]
        for extra in (first, second):
            if extra:
                done, use = extra(())
                use(done)
        return plain_scattered_sum(made)
    later = make(2, ())
    x1, y0 = low_sums([later[0], swapped(later[1], 1)], [later[2], swapped(later[3], 1)])
    if first:
        done, use = first((x1, y0))
        x1, y0, done = after((swapped(x1, 2), swapped(y0, 4), done))
        use(done)
        far = make(3, (x1, y0))
    else:
        far = make(3, (x1, y0))
        far, x1, y0 = after((far, swapped(x1, 2), swapped(y0, 4)))
    a0, a1 = low_sums([far[0], swapped(far[2], 1)], [far[1], swapped(far[3], 1)])
    near = make(1, (a0, a1))
    own = make(0, (a0, a1, near[0]))
    own, a0, a1 = after((own, swapped(a0, 4), swapped(a1, 2)))
    x0, y1 = low_sums([near[0], swapped(near[1], 1), a0], [near[2], swapped(near[3], 1), a1])
    mine = [[own[0], swapped(own[2], 1), y0], [own[1], swapped(own[3], 1), x1]]
    done, use = second((x0, y1)) if second else ((), None)
    x0, y1, mine, done = after((swapped(x0, 2), swapped(y1, 4), mine, done))
    if use:
        use(done)
    return [mine[0] + [x0], mine[1] + [y1]]


def after(values, *earlier):
    flat, tree = jax.tree.flatten(values)
    flat = lax.optimization_barrier(tuple(flat) + earlier)[: len(flat)]
    return jax.tree.unflatten(tree, flat)


def held(shape, place=None):
    where = place or (0,) * len(shape)
    return pl.BlockSpec(shape, lambda *_: where, pipeline_mode=pl.Buffered(1))


anywhere = pl.BlockSpec(memory_space=pl.ANY)


def half_rows(chunk, width):
    return pl.BlockSpec((chunk, width), lambda s: (s, 0))


def group_rows(group, chunk, width):
    return pl.BlockSpec((4, chunk, width), lambda s: (group, s, 0))


def group_call(kernel, name, steps, ins, specs, outs, out_specs, earlier, scratch, flops, moved):
    aliases = {len(ins) + n: n for n in range(len(earlier))}
    made = pl.pallas_call(
        functools.partial(kernel, len(ins), len(earlier)),
        grid=(steps,),
        in_specs=specs + [anywhere] * len(earlier),
        out_specs=out_specs,
        out_shape=outs,
        scratch_shapes=scratch,
        input_output_aliases=aliases,
        compiler_params=pltpu.CompilerParams(
            dimension_semantics=("arbitrary",), vmem_limit_bytes=52 * 2**20
        ),
        cost_estimate=pl.CostEstimate(flops=flops, bytes_accessed=moved, transcendentals=0),
        name=name,
    )(*ins, *earlier)
    return list(made)


def split_refs(n_ins, n_earlier, refs):
    return refs[:n_ins], refs[n_ins + n_earlier :]


def norm_kernel(n_ins, n_earlier, *refs):
    ins, rest = split_refs(n_ins, n_earlier, refs)
    gain_ref, shift_ref = ins[4:]
    for n in range(4):
        rest[0][n] = layer_norm(
            ins[n][...].astype(f32), gain_ref[...], shift_ref[...]
        ).astype(bf16)


def norm_rows(group, halves, gain, shift, earlier, slots):
    half, wide = halves[0].shape
    chunk = half // 2
    return group_call(
        norm_kernel,
        "norm_rows",
        2,
        list(halves) + [gain, shift],
        [half_rows(chunk, wide)] * 4 + [held(gain.shape), held(shift.shape)],
        [jax.ShapeDtypeStruct((slots, half, wide), bf16)],
        [group_rows(group, chunk, wide)],
        earlier,
        [],
        80 * half * wide,
        16 * half * wide,
    )


def triple_kernel(n_ins, n_earlier, *refs):
    (rows_ref, weight_ref, bias_ref), outs = split_refs(n_ins, n_earlier, refs)
    width = outs[0].shape[1]
    made = (dot(rows_ref[...], weight_ref[...], ROWS_BY_ROWS) + bias_ref[...]).astype(bf16)
    for place in range(3):
        outs[place][...] = made[:, place * width : (place + 1) * width]


def triple(first, steps, rows, weight, bias, earlier, count):
    wide = rows.shape[1]
    size = count // slot_groups(lax.axis_size("fsdp"))
    width = weight.shape[1] // 3
    return group_call(
        triple_kernel,
        "triple",
        steps,
        [rows, weight, bias],
        [
            pl.BlockSpec((size, wide), lambda s: (s + first, 0)),
            held(weight.shape),
            held(bias.shape),
        ],
        [jax.ShapeDtypeStruct((count, width), bf16)] * 3,
        [pl.BlockSpec((size, width), lambda s: (s + first, 0))] * 3,
        earlier,
        [],
        6 * steps * size * wide * width,
        2 * steps * size * wide,
    )


def norm_back_kernel(count, low, *refs):
    values, terms, rest = refs[:2], refs[2 : 2 + 2 * count], refs[2 + 2 * count :]
    extra_ref, gain_ref, grad_ref, sum_ref = rest[:4]

    @pl.when(pl.program_id(0) == 0)
    def _():
        sum_ref[...] = jnp.zeros_like(sum_ref)

    def average(one):
        return jnp.mean(one, axis=-1, keepdims=True)

    def add_rows(place, one):
        sum_ref[place : place + 1, :] += jnp.sum(one, axis=0, keepdims=True)

    for h in range(2):
        value = values[h][...].astype(f32)
        grad = total(*[ref[...] for ref in terms[h * count : (h + 1) * count]])
        extra = extra_ref[h].astype(f32)
        centred = value - average(value)
        rate = lax.rsqrt(average(centred * centred) + epsilon)
        unit = centred * rate
        scaled = grad * gain_ref[...]
        back = (scaled - average(scaled) - unit * average(scaled * unit)) * rate + extra
        grad_ref[h] = back
        add_rows(0, grad * unit)
        add_rows(1, grad)
        if low:
            rounded = back.astype(bf16)
            rest[4 + h][...] = rounded
            add_rows(2, rounded.astype(f32))
            add_rows(3, extra)


def norm_back(values, sums, extra, gain, low):
    half, wide = values[0].shape
    chunk = min(half, 64)
    rows = half_rows(chunk, wide)
    both = pl.BlockSpec((2, chunk, wide), lambda s: (0, s, 0))
    outs = [
        jax.ShapeDtypeStruct((2, half, wide), f32), jax.ShapeDtypeStruct((8, wide), f32)
    ] + [jax.ShapeDtypeStruct((half, wide), bf16)] * (2 * low)
    return pl.pallas_call(
        functools.partial(norm_back_kernel, len(sums[0]), low),
        grid=(half // chunk,),
        in_specs=[rows] * (2 + 2 * len(sums[0])) + [both, held(gain.shape)],
        out_specs=[both, pl.BlockSpec((8, wide), lambda s: (0, 0))] + [rows] * (2 * low),
        out_shape=outs,
        compiler_params=pltpu.CompilerParams(
            dimension_semantics=("arbitrary",), vmem_limit_bytes=40 * 2**20
        ),
        cost_estimate=pl.CostEstimate(
            flops=80 * half * wide, bytes_accessed=36 * half * wide, transcendentals=0
        ),
        name="norm_back",
    )(*values, *sums[0], *sums[1], extra, gain)


def project_kernel(n_ins, n_earlier, *refs):
    ins, rest = split_refs(n_ins, n_earlier, refs)
    weight_ref, outs = ins[-1], rest[:4]
    chunk, wide = outs[0].shape
    parts = [ref[...].reshape(4 * chunk, ref.shape[2]) for ref in ins[:-1]]
    rows = parts[0] if len(parts) == 1 else jnp.concatenate(parts, axis=1)
    by_rows = weight_ref.shape[0] == rows.shape[1] and weight_ref.shape[1] == wide
    tile = min(wide, 512)
    for start in range(0, wide, tile):
        columns = slice(start, start + tile)
        if by_rows:
            made = dot(rows, weight_ref[:, columns], ROWS_BY_ROWS)
        else:
            made = dot(rows, weight_ref[columns, :], ROWS_BY_COLS)
        made = made.astype(bf16)
        for n in range(4):
            outs[n][:, columns] = made[n * chunk : (n + 1) * chunk, :]


def project(group, parts, weight, wide):
    half = parts[0].shape[1]
    chunk = half // 2
    return group_call(
        project_kernel,
        "project",
        2,
        list(parts) + [weight],
        [group_rows(group, chunk, part.shape[2]) for part in parts] + [held(weight.shape)],
        [jax.ShapeDtypeStruct((half, wide), bf16)] * 4,
        [half_rows(chunk, wide)] * 4,
        [],
        [],
        8 * half * weight.size,
        8 * half * wide + 2 * weight.size,
    )


def project_back_kernel(n_ins, n_earlier, *refs):
    ins, rest = split_refs(n_ins, n_earlier, refs)
    weight_ref = ins[4]
    made_ref, kept_ref, rows = rest
    chunk = ins[0].shape[0]
    for n in range(4):
        kept_ref[n] = ins[n][...]
        rows[n * chunk : (n + 1) * chunk, :] = ins[n][...]
    made = dot(rows[...], weight_ref[...], ROWS_BY_COLS).astype(bf16)
    for n in range(4):
        made_ref[n] = made[n * chunk : (n + 1) * chunk, :]


def project_back(group, halves, weight, earlier, slots):
    half, wide = halves[0].shape
    chunk = half // 2
    width = weight.shape[0]
    return group_call(
        project_back_kernel,
        "project_back",
        2,
        list(halves) + [weight],
        [half_rows(chunk, wide)] * 4 + [held(weight.shape)],
        [jax.ShapeDtypeStruct((slots, half, n), bf16) for n in (width, wide)],
        [group_rows(group, chunk, n) for n in (width, wide)],
        earlier,
        [pltpu.VMEM((4 * chunk, wide), bf16)],
        8 * half * weight.size,
        16 * half * wide,
    )


gelu_rate = math.sqrt(2.0 / math.pi)
gelu_cube = 0.044715


def feed_forward_kernel(keep, n_ins, n_earlier, *refs):
    ins, rest = split_refs(n_ins, n_earlier, refs)
    up_ref, shift_ref, down_ref = ins[8:]
    active_ref, grad_ref, rows_ref, grad_rows_ref, other_ref = rest[:5]
    back = rest[5:9]
    gone = [n for n in range(4) if n not in keep]
    ahead = [
        rest[9 + keep.index(n)] if n in keep else other_ref.at[gone.index(n)] for n in range(4)
    ]
    shift_grad_ref, rows, grad_rows, active, grad_upper = rest[11:]
    chunk, wide = ins[0].shape
    units = up_ref.shape[1]
    for n in range(4):
        r = slice(n * chunk, (n + 1) * chunk)
        rows[r, :] = ins[n][...]
        grad_rows[r, :] = ins[4 + n][...]
        rows_ref[n] = ins[n][...]
        grad_rows_ref[n] = ins[4 + n][...]
    tile = min(units, 512)

    def hidden(t, carry):
        columns = pl.ds(pl.multiple_of(t * tile, tile), tile)
        upper = dot(rows[...], up_ref[:, columns], ROWS_BY_ROWS) + shift_ref[:, columns]
        grad_active = dot(grad_rows[...], down_ref[columns, :], ROWS_BY_COLS)
        square = upper * upper
        bend = jnp.tanh(gelu_rate * upper * (1.0 + gelu_cube * square))
        share = 0.5 * (1.0 + bend)
        slope = share + 0.5 * upper * (1.0 - bend * bend) * (
            gelu_rate * (1.0 + 3.0 * gelu_cube * square)
        )
        made = (upper * share).astype(bf16)
        grad = (grad_active * slope).astype(bf16)
        active[:, columns] = made
        grad_upper[:, columns] = grad
        shift_grad_ref[0, 0:1, columns] = jnp.sum(grad.astype(f32), axis=0, keepdims=True)
        for n in range(4):
            r = slice(n * chunk, (n + 1) * chunk)
            active_ref[n, :, columns] = made[r, :]
            grad_ref[n, :, columns] = grad[r, :]
        return carry

    lax.fori_loop(0, units // tile, hidden, 0)
    step = min(wide, 1024)

    def outer(t, carry):
        columns = pl.ds(pl.multiple_of(t * step, step), step)
        made_back = dot(grad_upper[...], up_ref[columns, :], ROWS_BY_COLS).astype(bf16)
        made_ahead = dot(active[...], down_ref[:, columns], ROWS_BY_ROWS).astype(bf16)
        for n in range(4):
            r = slice(n * chunk, (n + 1) * chunk)
            back[n][:, columns] = made_back[r, :]
            ahead[n][:, columns] = made_ahead[r, :]
        return carry

    lax.fori_loop(0, wide // step, outer, 0)


def feed_forward(group, keep, halves, grad_halves, up, shift, down, earlier, slots):
    half, wide = halves[0].shape
    chunk = half // 2
    units = up.shape[1]
    sizes = (units, units, wide, wide)
    outs = [jax.ShapeDtypeStruct((slots, half, n), bf16) for n in sizes]
    outs += [jax.ShapeDtypeStruct((slots // 2, half, wide), bf16)]
    outs += [jax.ShapeDtypeStruct((half, wide), bf16)] * 6
    outs += [jax.ShapeDtypeStruct((2, 8, units), f32)]
    made = group_call(
        functools.partial(feed_forward_kernel, keep),
        "feed_forward",
        2,
        list(halves) + list(grad_halves) + [up, shift, down],
        [half_rows(chunk, wide)] * 8 + [held(up.shape), held(shift.shape), held(down.shape)],
        outs,
        [group_rows(group, chunk, n) for n in sizes]
        + [pl.BlockSpec((2, chunk, wide), lambda s: (group, s, 0))]
        + [half_rows(chunk, wide)] * 6
        + [pl.BlockSpec((1, 8, units), lambda s: (s, 0, 0))],
        earlier,
        [pltpu.VMEM((4 * chunk, n), bf16) for n in (wide, wide, units, units)],
        32 * half * wide * units,
        48 * half * wide + 4 * wide * units,
    )
    return made[:5], made[5:9], made[9:11], jnp.sum(made[11][:, 0], axis=0)


def only_head(values, head):
    columns = lax.broadcasted_iota(jnp.int32, values.shape, 1) // HEAD
    return jnp.where(columns == head, values, jnp.zeros_like(values))


def transposed(values):
    return values.astype(f32).T.astype(bf16)


def places_of(plan_ref, blocks, subs, half, j):
    return [
        pl.ds(pl.multiple_of(plan_ref[3 * blocks + subs * j + n] * half, half), half)
        for n in range(subs)
    ]


def rows_of(ref, places):
    parts = [ref[place, :] for place in places]
    return parts[0] if len(parts) == 1 else jnp.concatenate(parts, axis=0)


def cols_of(ref, places):
    parts = [ref[:, place] for place in places]
    return parts[0] if len(parts) == 1 else jnp.concatenate(parts, axis=1)


def attn_forward_kernel(
    block, half, heads, plan_ref, q_ref, k_ref, v_ref, sk_ref, sv_ref, row_ref, o_ref, log_ref,
    q_heads, vt_all, svt, tops, sums, mixed,
):
    i = pl.program_id(0)
    blocks = pl.num_programs(0)
    subs = block // half

    @pl.when(i == 0)
    def _():
        for n in range(v_ref.shape[0] // half):
            r = slice(n * half, (n + 1) * half)
            vt_all[:, r] = transposed(v_ref[r, :])
        svt[...] = transposed(sv_ref[...])

    mine = places_of(plan_ref, blocks, subs, half, i)
    q = rows_of(q_ref, mine).astype(f32) * score_scale
    for h in range(heads):
        q_heads[h] = only_head(q, h).astype(bf16)
    tops[...] = jnp.full_like(tops, masked_score)
    sums[...] = jnp.zeros_like(sums)
    mixed[...] = jnp.zeros_like(mixed)
    lowest = row_ref[0:1, :]
    highest = row_ref[1:2, :]
    summ_end = row_ref[2:3, :]
    me = row_ref[3:4, :]

    def step(keys, values_t, mask):
        each = range(heads)
        scores = [dot(keys, q_heads[h], ROWS_BY_COLS) for h in each]
        if mask is not None:
            scores = [jnp.where(mask, one, masked_score) for one in scores]
        before = [tops[h : h + 1, :] for h in each]
        top = [jnp.maximum(before[h], jnp.max(scores[h], axis=0, keepdims=True)) for h in each]
        weights = [jnp.exp(scores[h] - top[h]) for h in each]
        keep = [jnp.exp(before[h] - top[h]) for h in each]
        added = [jnp.sum(weights[h], axis=0, keepdims=True) for h in each]
        totals = [keep[h] * sums[h : h + 1, :] + added[h] for h in each]
        part_of = [slice(h * HEAD, (h + 1) * HEAD) for h in each]
        more = [dot(values_t[part_of[h], :], weights[h].astype(bf16), ROWS_BY_ROWS) for h in each]
        result = [keep[h] * mixed[part_of[h], :] + more[h] for h in each]
        for h in each:
            tops[h : h + 1, :] = top[h]
            sums[h : h + 1, :] = totals[h]
            mixed[part_of[h], :] = result[h]

    @pl.when(plan_ref[2 * blocks + i] > 0)
    def _():
        places = lax.broadcasted_iota(jnp.int32, (sk_ref.shape[0], block), 0)
        step(sk_ref[...], svt[...], places < summ_end)

    def whole(j, carry):
        there = places_of(plan_ref, blocks, subs, half, j)
        step(rows_of(k_ref, there), cols_of(vt_all, there), None)
        return carry

    def part(j, carry):
        there = places_of(plan_ref, blocks, subs, half, j)
        places = j * block + lax.broadcasted_iota(jnp.int32, (block, block), 0)
        mask = ((places >= lowest) & (places <= highest)) | (places == me)
        step(rows_of(k_ref, there), cols_of(vt_all, there), mask)
        return carry

    lax.fori_loop(plan_ref[i], plan_ref[blocks + i], whole, 0)
    lax.fori_loop(plan_ref[blocks + i], i + 1, part, 0)
    for h in range(heads):
        r = slice(h * HEAD, (h + 1) * HEAD)
        mixed[r, :] = mixed[r, :] * (1.0 / sums[h : h + 1, :])
    log_ref[...] = tops[...] + jnp.log(jnp.maximum(sums[...], 1e-37))
    made = mixed[...].T.astype(bf16)
    for n, place in enumerate(mine):
        o_ref[place, :] = made[n * half : (n + 1) * half, :]


def attn_backward_kernel(
    block, half, heads, plan_ref, q_ref, k_ref, v_ref, sk_ref, sv_ref, row_ref, log_ref, o_ref, do_ref, dq_ref, dk_ref, dv_ref, dsk_ref, dsv_ref, shift_ref, q_heads, do_heads, kt_all, skt, dq_sum,
    dk_sum, dv_sum, dsk_sum, dsv_sum,
):
    i = pl.program_id(0)
    blocks = pl.num_programs(0)
    subs = block // half

    @pl.when(i == 0)
    def _():
        dk_sum[...] = jnp.zeros_like(dk_sum)
        dv_sum[...] = jnp.zeros_like(dv_sum)
        dsk_sum[...] = jnp.zeros_like(dsk_sum)
        dsv_sum[...] = jnp.zeros_like(dsv_sum)
        for n in range(k_ref.shape[0] // half):
            r = slice(n * half, (n + 1) * half)
            kt_all[:, r] = transposed(k_ref[r, :])
        skt[...] = transposed(sk_ref[...])

    mine = places_of(plan_ref, blocks, subs, half, i)
    q = rows_of(q_ref, mine).astype(f32) * score_scale
    do = rows_of(do_ref, mine).astype(f32)
    for h in range(heads):
        q_heads[h] = only_head(q, h).astype(bf16)
        do_heads[h] = only_head(do, h).astype(bf16)
    both_t = (do * rows_of(o_ref, mine).astype(f32)).T
    row_terms = [
        jnp.sum(both_t[h * HEAD : (h + 1) * HEAD, :], axis=0, keepdims=True) for h in range(heads)
    ]
    dq_sum[...] = jnp.zeros_like(dq_sum)
    lowest = row_ref[0:1, :]
    highest = row_ref[1:2, :]
    summ_end = row_ref[2:3, :]
    me = row_ref[3:4, :]

    def step(keys, values, keys_t, mask):
        dk = dv = None
        for h in range(heads):
            scores = dot(keys, q_heads[h], ROWS_BY_COLS)
            if mask is not None:
                scores = jnp.where(mask, scores, masked_score)
            probs = jnp.exp(scores - log_ref[h : h + 1, :])
            grad_probs = dot(values, do_heads[h], ROWS_BY_COLS)
            grad_scores = (probs * (grad_probs - row_terms[h])).astype(bf16)
            r = slice(h * HEAD, (h + 1) * HEAD)
            dq_sum[r, :] += dot(keys_t[r, :], grad_scores, ROWS_BY_ROWS)
            dv_own = dot(probs.astype(bf16), do_heads[h], ROWS_BY_ROWS)
            dk_own = dot(grad_scores, q_heads[h], ROWS_BY_ROWS)
            dv = dv_own if dv is None else dv + dv_own
            dk = dk_own if dk is None else dk + dk_own
        return dk, dv

    @pl.when(plan_ref[2 * blocks + i] > 0)
    def _():
        places = lax.broadcasted_iota(jnp.int32, (sk_ref.shape[0], block), 0)
        dk, dv = step(sk_ref[...], sv_ref[...], skt[...], places < summ_end)
        dsk_sum[...] += dk
        dsv_sum[...] += dv

    def whole(j, masked):
        there = places_of(plan_ref, blocks, subs, half, j)
        mask = None
        if masked:
            places = j * block + lax.broadcasted_iota(jnp.int32, (block, block), 0)
            mask = ((places >= lowest) & (places <= highest)) | (places == me)
        dk, dv = step(rows_of(k_ref, there), rows_of(v_ref, there), cols_of(kt_all, there), mask)
        for n, place in enumerate(there):
            dk_sum[place, :] += dk[n * half : (n + 1) * half, :]
            dv_sum[place, :] += dv[n * half : (n + 1) * half, :]

    def plain(j, carry):
        whole(j, False)
        return carry

    def part(j, carry):
        whole(j, True)
        return carry

    lax.fori_loop(plan_ref[i], plan_ref[blocks + i], plain, 0)
    lax.fori_loop(plan_ref[blocks + i], i + 1, part, 0)
    made = (dq_sum[...] * score_scale).T.astype(bf16)
    for n, place in enumerate(mine):
        dq_ref[place, :] = made[n * half : (n + 1) * half, :]

    @pl.when(i == blocks - 1)
    def _():
        dk_ref[...] = dk_sum[...].astype(bf16)
        dv_ref[...] = dv_sum[...].astype(bf16)
        dsk_ref[...] = dsk_sum[...].astype(bf16)
        dsv_ref[...] = dsv_sum[...].astype(bf16)

        def added(ref):
            return jnp.sum(ref[...].astype(f32), axis=0, keepdims=True)

        shift_ref[...] = jnp.zeros_like(shift_ref)
        shift_ref[0:1, :] = added(dq_ref)
        shift_ref[1:2, :] = added(dv_ref) + added(dsv_ref)


def attn_forward(part, parts, plan, rows, q, k, v, sk, sv, block, half):
    count = q.shape[0]
    width = q.shape[1] // parts
    heads = width // HEAD
    by_cols = pl.BlockSpec((8, block), lambda i, *_: (0, i))
    pairs = count * count // 4
    return pl.pallas_call(
        functools.partial(attn_forward_kernel, block, half, heads),
        grid_spec=pltpu.PrefetchScalarGridSpec(
            num_scalar_prefetch=1,
            grid=(count // block,),
            in_specs=[held((one.shape[0], width), (0, part)) for one in (q, k, v, sk, sv)] + [by_cols],
            out_specs=[held((count, width)), by_cols],
            scratch_shapes=[
                pltpu.VMEM((heads, block, width), bf16),
                pltpu.VMEM((width, count), bf16),
                pltpu.VMEM((width, sk.shape[0]), bf16),
                pltpu.VMEM((8, block), f32),
                pltpu.VMEM((8, block), f32),
                pltpu.VMEM((width, block), f32),
            ],
        ),
        out_shape=[
            jax.ShapeDtypeStruct((count, width), bf16),
            jax.ShapeDtypeStruct((8, count), f32),
        ],
        compiler_params=pltpu.CompilerParams(
            dimension_semantics=("arbitrary",), vmem_limit_bytes=40 * 2**20
        ),
        cost_estimate=pl.CostEstimate(
            flops=16 * pairs * width, bytes_accessed=8 * count * width, transcendentals=pairs * heads
        ),
        name="attn_forward",
    )(plan, q, k, v, sk, sv, rows)


def attn_backward(part, parts, plan, rows, q, k, v, sk, sv, logs, o, do, block, half):
    count = q.shape[0]
    width = q.shape[1] // parts
    heads = width // HEAD
    by_cols = pl.BlockSpec((8, block), lambda i, *_: (0, i))
    pairs = count * count // 4
    long = jax.ShapeDtypeStruct((count, width), bf16)
    short = jax.ShapeDtypeStruct((sk.shape[0], width), bf16)
    shift = jax.ShapeDtypeStruct((8, width), f32)
    long_in = held((count, width), (0, part))
    short_in = held((sk.shape[0], width), (0, part))
    return pl.pallas_call(
        functools.partial(attn_backward_kernel, block, half, heads),
        grid_spec=pltpu.PrefetchScalarGridSpec(
            num_scalar_prefetch=1,
            grid=(count // block,),
            in_specs=[long_in] * 3
            + [short_in] * 2
            + [by_cols] * 2
            + [held((count, width)), long_in],
            out_specs=[held(one.shape) for one in (long, long, long, short, short, shift)],
            scratch_shapes=[
                pltpu.VMEM((heads, block, width), bf16),
                pltpu.VMEM((heads, block, width), bf16),
                pltpu.VMEM((width, count), bf16),
                pltpu.VMEM((width, sk.shape[0]), bf16),
                pltpu.VMEM((width, block), f32),
                pltpu.VMEM((count, width), f32),
                pltpu.VMEM((count, width), f32),
                pltpu.VMEM((sk.shape[0], width), f32),
                pltpu.VMEM((sk.shape[0], width), f32),
            ],
        ),
        out_shape=[long, long, long, short, short, shift],
        compiler_params=pltpu.CompilerParams(
            dimension_semantics=("arbitrary",), vmem_limit_bytes=48 * 2**20
        ),
        cost_estimate=pl.CostEstimate(
            flops=24 * pairs * width, bytes_accessed=20 * count * width, transcendentals=pairs * heads
        ),
        name="attn_backward",
    )(plan, q, k, v, sk, sv, rows, logs, o, do)


def spread_columns_kernel(parts_ref, *outs):
    shards = parts_ref.shape[0]
    width = parts_ref.shape[2] // 3
    for n, ref in enumerate(outs):
        for d in range(width // HEAD):
            start = n * width + d * HEAD
            for f in range(0, shards, 2):
                pair = [parts_ref[f + m, :, start : start + HEAD].astype(f32) for m in range(2)]
                place = (d * shards + f) * HEAD
                ref[:, place : place + 2 * HEAD] = jnp.concatenate(pair, axis=1)


def spread_columns(parts):
    shards, count, width = parts.shape
    return pl.pallas_call(
        spread_columns_kernel,
        out_shape=[jax.ShapeDtypeStruct((count, shards * width // 3), f32)] * 3,
        name="spread_columns",
    )(parts)


def attention_plan(lengths, padding, count, block, slots):
    places = jnp.arange(count, dtype=jnp.int32)
    ends = jnp.cumsum(lengths)
    passed = places[:, None] >= ends[None, :]
    segment = jnp.sum(passed.astype(jnp.int32), axis=1)
    lowest = jnp.max(jnp.where(passed, ends[None, :], 0), axis=1)
    living = count - padding
    highest = jnp.minimum(places, living - 1)
    nothing = jnp.zeros_like(places)
    rows = jnp.stack(
        [lowest, highest, segment * SUMM, places, nothing, nothing, nothing, nothing], axis=0
    )
    blocks = count // block
    starts = jnp.arange(blocks, dtype=jnp.int32) * block
    first = lowest.reshape(blocks, block)[:, 0] // block
    one_piece = lowest.reshape(blocks, block)[:, -1] <= first * block
    whole_end = jnp.maximum(jnp.minimum(starts, living) // block, first)
    split = jnp.where(one_piece, whole_end, first)
    summ_flag = (segment.reshape(blocks, block)[:, -1] > 0).astype(jnp.int32)
    return rows, jnp.concatenate([first, split, summ_flag, slots]).astype(jnp.int32)


def per_device(
    tokens,
    summaries,
    segment_lengths,
    pad_lengths,
    output_grad,
    norm1_gain,
    norm1_bias,
    query_weight,
    query_bias,
    key_weight,
    value_weight,
    value_bias,
    out_weight,
    out_bias,
    norm2_gain,
    norm2_bias,
    up_weight,
    up_bias,
    down_weight,
    down_bias,
):
    shards = lax.axis_size("fsdp")
    items = lax.axis_size("dp")
    devices = shards * items
    position = lax.axis_index("fsdp")
    tok_rows = tokens.shape[1]
    width = tokens.shape[2]
    count = tok_rows * shards
    own_width = width // shards
    rows_held = query_weight.shape[0]
    units_held = up_bias.shape[0]
    own_units = units_held * items
    hidden = units_held * devices
    summary_rows = summaries.shape[1]
    padded_summ = -(-summary_rows // 32) * 32
    spread = rows_held % HEAD == 0
    block = math.gcd(count, 512)

    def for_shards(weight):
        if spread:
            split = weight.reshape(rows_held, items, shards, rows_held)
            return split.transpose(2, 0, 1, 3).reshape(shards, rows_held, own_width)
        return weight.reshape(rows_held, shards, own_width).transpose(1, 0, 2)

    def from_shards(parts):
        if spread:
            split = parts.reshape(shards, rows_held, items, rows_held)
            return split.transpose(1, 2, 0, 3).reshape(rows_held, width)
        return parts.transpose(1, 0, 2).reshape(rows_held, width)

    def own_columns(vector):
        if spread:
            split = vector.reshape(items, shards, rows_held)
            return lax.dynamic_index_in_dim(split, position, 1, keepdims=False).reshape(own_width)
        return lax.dynamic_slice_in_dim(vector, position * own_width, own_width, 0)

    def whole_columns(vector):
        if spread:
            split = jnp.zeros((items, shards, rows_held), f32)
            return lax.dynamic_update_index_in_dim(
                split, vector.reshape(items, 1, rows_held), position, 1
            ).reshape(width)
        return lax.dynamic_update_slice_in_dim(
            jnp.zeros((width,), f32), vector, position * own_width, 0
        )

    half = tok_rows // 2
    order = slot_order(shards)
    groups = len(order) // 4
    eight = shards == 8

    def halves(whole):
        return [whole[:half], whole[half:]]

    def flat(slotted):
        return slotted.reshape(count, slotted.shape[2])

    def slot_rows(slotted):
        return slotted.reshape(slotted.shape[0] * half, slotted.shape[2])

    qkv_parts = jnp.concatenate(
        [for_shards(query_weight), for_shards(key_weight), for_shards(value_weight)], axis=2
    )
    qkv_parts = lax.all_to_all(qkv_parts, "fsdp", 0, 0, tiled=True)
    qkv_own = lax.all_gather(
        qkv_parts.reshape(shards * rows_held, 3 * own_width), "dp", axis=0, tiled=True
    )
    vectors = jnp.concatenate(
        [
            norm1_gain, norm1_bias, query_bias, value_bias, out_bias, norm2_gain, norm2_bias,
            down_bias, up_bias,
        ]
    ).astype(f32)
    vectors = lax.all_to_all(
        jnp.broadcast_to(vectors[None], (devices, vectors.shape[0])), BOTH, 0, 0, tiled=True
    )
    gain_one, shift_one, query_shift, value_shift, out_shift, gain_two, shift_two, down_shift = (
        vectors[:, n * rows_held : (n + 1) * rows_held].reshape(width) for n in range(8)
    )
    token_halves = after(halves(tokens[0]), qkv_parts, vectors)
    token_hops = sent(token_halves)
    grad_own = halves(output_grad[0])
    up_parts = up_weight.reshape(rows_held, items, shards, units_held).transpose(2, 0, 1, 3)
    up_parts = up_parts.reshape(shards, rows_held, own_units)
    more_slots = -(-padded_summ // half)

    query_shift = own_columns(query_shift)
    value_shift = own_columns(value_shift)
    qkv_shift = jnp.concatenate([query_shift, jnp.zeros_like(query_shift), value_shift])[None]

    def normed_group(g, group, normed):
        return norm_rows(
            g, group, gain_one[None], shift_one[None], normed, 4 * groups + more_slots
        )

    if eight:
        mine = [*token_halves, *[swapped(one, 1) for one in token_halves]]
        normed = normed_group(0, mine, [])
        x0, y1, x1, y0 = token_hops
        x0, y1, x1, y0 = after((x0, y1, x1, y0), normed[0], up_parts, *grad_own)
        a0, a1 = swapped(x0, 4), swapped(y1, 2)
        normed = normed_group(1, [x0, swapped(x0, 1), y1, swapped(y1, 1)], normed)
        normed = normed_group(2, [x1, swapped(x1, 1), y0, swapped(y0, 1)], normed)
        made = triple(0, groups - 1, slot_rows(normed[0]), qkv_own, qkv_shift, [], count)
        a0, a1, made = after((a0, a1, made))
        last_tokens = [a0, a1, swapped(a0, 1), swapped(a1, 1)]
    else:
        normed = []
        token_groups = passed_on(token_halves, token_hops)
        last_tokens = token_groups[-1]
        for g in range(groups - 1):
            normed = normed_group(g, token_groups[g], normed)
        made = triple(0, groups - 1, slot_rows(normed[0]), qkv_own, qkv_shift, [], count)
    up_shift = lax.dynamic_index_in_dim(
        vectors[:, 8 * rows_held :].reshape(items, shards, units_held), position, 1, keepdims=False
    ).reshape(1, own_units)

    early = token_hops[:2] if eight else ()
    if spread:
        both = after(jnp.concatenate([out_weight, down_weight], axis=0), *early)
        both = lax.all_gather(both, "dp", axis=0)
        out_own = both[:, :rows_held].reshape(own_width, width)
        down_shares = both
    else:
        out_own = lax.dynamic_slice_in_dim(
            lax.all_gather(out_weight, BOTH, axis=0, tiled=True), position * own_width, own_width, 0
        )
        down_shares = lax.all_gather(down_weight, "dp", axis=0)
    up_parts = after(up_parts, last_tokens[0])
    up_parts = lax.all_to_all(up_parts, "fsdp", 0, 0, tiled=True)
    grad_own = after(grad_own, *last_tokens)
    grad_hops = sent(grad_own)

    summ_full = after(
        jnp.broadcast_to(summaries, (shards,) + summaries.shape[1:]), last_tokens[0]
    )
    summ_full = lax.all_to_all(summ_full, "fsdp", 0, 0, tiled=True)
    normed = normed_group(groups - 1, last_tokens, normed)
    queries, keys, values = triple(
        groups - 1, 1, slot_rows(normed[0]), qkv_own, qkv_shift, made, count
    )
    queries, keys, values, summ_full = after((queries, keys, values, summ_full))
    summ_full = summ_full.transpose(1, 0, 2).reshape(summary_rows, width)
    summ_inputs = jnp.pad(summ_full, ((0, padded_summ - summary_rows), (0, 0))).astype(f32)
    normed_summ = layer_norm(summ_inputs, gain_one, shift_one).astype(bf16)
    extra_rows = ((0, more_slots * half - padded_summ), (0, 0))
    normed = lax.dynamic_update_slice(
        slot_rows(normed[0]), jnp.pad(normed_summ, extra_rows), (count, 0)
    )
    summ_qkv = dot(normed_summ, qkv_own, ROWS_BY_ROWS) + qkv_shift
    summ_keys = summ_qkv[:, own_width : 2 * own_width].astype(bf16)
    summ_values = summ_qkv[:, 2 * own_width :].astype(bf16)
    slot_of = [[order.index((m, h)) for h in range(2)] for m in range(shards)]
    slots = jnp.array(slot_of, jnp.int32)[jnp.arange(shards) ^ position].reshape(-1)
    rows, plan = attention_plan(segment_lengths[0], pad_lengths[0], count, block, slots)
    parts = 2 if own_width % 256 == 0 else 1
    attn = []
    logs = []
    for part in range(parts):
        one, log = attn_forward(
            part, parts, plan, rows, queries, keys, values, summ_keys, summ_values, block, half
        )
        if eight and part == 0:
            one, log, plan, *grad_hops = after((one, log, plan, *grad_hops))
            x0, y1, x1, y0 = grad_hops
            a0, a1 = swapped(x0, 4), swapped(y1, 2)
        elif eight:
            one, log, a0, a1, up_parts, out_own = after((one, log, a0, a1, up_parts, out_own))
            grad_groups = [
                [*grad_own, swapped(grad_own[0], 1), swapped(grad_own[1], 1)],
                [x0, swapped(x0, 1), y1, swapped(y1, 1)],
                [x1, swapped(x1, 1), y0, swapped(y0, 1)],
                [a0, a1, swapped(a0, 1), swapped(a1, 1)],
            ]
        attn.append(one)
        logs.append(log)
    if not eight:
        grad_groups = passed_on(grad_own, grad_hops)
    up_own = lax.all_gather(
        up_parts.reshape(shards * rows_held, own_units), "dp", axis=0, tiled=True
    )
    attn_slots = [one.reshape(4 * groups, half, own_width // parts) for one in attn]
    inputs = [one.astype(f32) for one in halves(tokens[0])]
    proj_sums = scattered_sum(
        lambda g, earlier: project(g, attn_slots, after(out_own, *earlier), width), groups
    )
    resid = [
        total(inputs[h], *proj_sums[h]) + out_shift for h in range(2)
    ]

    normed_two_own = [layer_norm(one, gain_two, shift_two).astype(bf16) for one in resid]
    two_hops = sent(normed_two_own)
    down_own = after(down_shares, *normed_two_own)[:, down_shares.shape[1] - units_held :]
    down_own = down_own.reshape(own_units, width)
    if eight:
        x0, y1, x1, y0 = two_hops
        x0, y1, down_own = after((x0, y1, down_own))
        two_hops = (x0, y1, x1, y0)
    two_groups = passed_on(normed_two_own, two_hops)
    made = []
    back = {}
    ahead = {}
    unit_sums = []

    def feed(g, earlier):
        nonlocal made
        for n in [1, 2, 3, 0] if eight else range(groups):
            if n not in back and g not in back:
                mine = two_groups[n]
                if n == 2 and eight:
                    x1, y0 = after((mine[0], mine[2]), back[1][0])
                    mine = [x1, swapped(x1, 1), y0, swapped(y0, 1)]
                keep = (0, 2) if eight and n in (1, 2) else (0, 1)
                made, back[n], ahead[n], unit_sum = feed_forward(
                    n, keep, mine, grad_groups[n], up_own, up_shift, after(down_own, *earlier),
                    made, 4 * groups,
                )
                unit_sums.append(unit_sum)
        return back[g]

    kept = {}

    def down_grad_of(earlier):
        active, grad_rows = flat(made[0]), flat(made[3])
        grad = dot(after(active, *earlier), grad_rows, COLS_BY_ROWS).astype(bf16)
        others = swapped(after(made[4], *earlier), 1) if eight else made[4]

        def use(done):
            kept["down"], kept["others"] = done

        return (grad, others), use

    def up_grad_of(earlier):
        grad_upper, normed_two = flat(feed_made[1]), flat(feed_made[2])
        return dot(after(normed_two, *earlier), grad_upper, COLS_BY_ROWS).astype(bf16)

    grad_normed_two = scattered_sum(feed, groups, None, down_grad_of)
    feed_made = made
    down_grad = lax.psum_scatter(kept["down"], "dp", scatter_dimension=0, tiled=True)
    grad_resid, sums_two, *grad_proj = norm_back(
        resid, grad_normed_two, output_grad.reshape(2, half, width), gain_two[None], True
    )

    proj_hops = sent(grad_proj)
    if eight:
        mine = grad_proj + [swapped(one, 1) for one in grad_proj]
        made = project_back(0, mine, out_own, [], 4 * groups)
        up_grad = up_grad_of((made[0],))
        x0, y1, x1, y0, up_grad = after((*proj_hops, up_grad))
        others = kept["others"]
        own, near, later, far = after([ahead[g] for g in range(groups)], up_grad)
        sends = low_sums(
            [later[0], (others, 4)],
            [later[1], (others, 5)],
            [far[0], (others, 6)],
            [far[1], (others, 7)],
        )
        near = [[near[0], (others, 2)], [near[1], (others, 3)]]
        a0, a1 = swapped(x0, 4), swapped(y1, 2)
        made = project_back(
            1, [x0, swapped(x0, 1), y1, swapped(y1, 1)], out_own, made, 4 * groups
        )
        made = project_back(
            2, [x1, swapped(x1, 1), y0, swapped(y0, 1)], out_own, made, 4 * groups
        )
        a0, a1, made, sends = after((a0, a1, made, sends))
        proj_groups = [None, None, None, [a0, a1, swapped(a0, 1), swapped(a1, 1)]]
    else:
        up_grad = up_grad_of(())
        made = []
        proj_groups = passed_on(grad_proj, proj_hops)
    up_grad = lax.psum_scatter(up_grad, "dp", scatter_dimension=0, tiled=True)
    up_grad = up_grad.reshape(shards, rows_held, own_units)
    if not eight:
        up_grad = lax.all_to_all(up_grad, "fsdp", 0, 0, tiled=True)
    ahead = [
        [*ahead[g], kept["others"][2 * g], kept["others"][2 * g + 1]] for g in range(groups)
    ]
    for g in range(groups - 1 if eight else 0, groups):
        halves_now = proj_groups[g]
        made = project_back(g, halves_now, out_own, made, 4 * groups)
    grad_attn, proj_rows = (flat(one) for one in made)
    grad_attn, down_grad = after((grad_attn, down_grad))
    if eight:
        x1, y0, a0, a1 = after(sends, *proj_groups[-1])
        travelling = [swapped(x1, 2), swapped(y0, 4), swapped(a0, 4), swapped(a1, 2)]
    else:
        result = plain_scattered_sum(ahead)
    pulled = []
    again = grad_attn
    for part in range(parts):
        one = list(attn_backward(
            part, parts, plan, rows, queries, keys, values, summ_keys, summ_values, logs[part],
            attn[part], again, block, half,
        ))
        if eight and part == 0:
            one, again, *travelling = after((one, again, *travelling))
            x1, y0, a0, a1 = travelling
            x0, y1 = low_sums(near[0] + [a0], near[1] + [a1])
            travelling = [swapped(x0, 2), swapped(y1, 4)]
            up_grad = after(up_grad, x0, y1)
            up_grad = lax.all_to_all(up_grad, "fsdp", 0, 0, tiled=True)
        elif eight:
            one, up_grad, *travelling = after((one, up_grad, *travelling))
        pulled.append(one)
    grad_slots = [
        pulled[part][n].reshape(4 * groups, half, own_width // parts)
        for n in range(3)
        for part in range(parts)
    ]
    grad_summ_kv = jnp.concatenate(
        [pulled[part][n] for n in (3, 4) for part in range(parts)], axis=1
    )

    summ_share = -(-padded_summ // (shards * 16)) * 16
    more_rows = ((0, summ_share * shards - padded_summ), (0, 0))

    def qkv_grad_of(earlier):
        slots_now, summ_now = after((grad_slots, grad_summ_kv), *earlier)
        grad_qkv = jnp.concatenate([flat(one) for one in slots_now], axis=1)
        grad_qkv = jnp.concatenate(
            [grad_qkv, jnp.pad(summ_now, (extra_rows[0], (own_width, 0)))], axis=0
        )
        grad = dot(normed, grad_qkv, COLS_BY_ROWS).astype(bf16)
        return grad, functools.partial(kept.__setitem__, "qkv")

    def side_work(earlier):
        kept["late"] = earlier
        grad = lax.psum_scatter(kept["qkv"], "dp", scatter_dimension=0, tiled=True)
        up_now, down_now = after((up_grad, down_grad), *earlier)
        grad = after(grad, *earlier).reshape(shards, rows_held, 3 * own_width)
        kept["qkv_parts"] = lax.all_to_all(grad, "fsdp", 0, 0, tiled=True)
        up_now = up_now.reshape(shards, rows_held, items, units_held).transpose(1, 2, 0, 3)
        up_now = up_now.reshape(rows_held, hidden).astype(f32)

        def use(done):
            kept.update(zip(("qkv_parts", "up", "down"), done))

        return (kept["qkv_parts"], up_now, down_now.astype(f32)), use

    if eight:
        x0, y1 = travelling
        result_terms = [(resid[0], own[0], y0, x0), (resid[1], own[1], x1, y1)]
    else:
        result_terms = [(resid[h], *result[h]) for h in range(2)]

    def grad_rows_back(g, earlier):
        if g == 1 or not eight:
            back = dot(after(grad_summ_kv, *earlier), qkv_own[:, own_width:], ROWS_BY_COLS)
            kept["summ"] = jnp.pad(back.astype(bf16), more_rows).reshape(shards, summ_share, width)
            columns = jnp.concatenate(after(attn, *earlier), axis=1)
            kept["out"] = dot(columns, proj_rows, COLS_BY_ROWS).astype(bf16)
        made = project(g, grad_slots, after(qkv_own, *earlier), width)
        if g == 1:
            made, kept["out"] = after((made, kept["out"]))
        return made

    grad_normed = scattered_sum(
        grad_rows_back,
        groups,
        qkv_grad_of,
        side_work,
    )
    out_grad = kept["out"]
    up_grad, down_grad = kept["up"], kept["down"]
    if spread:
        out_grad = lax.psum_scatter(out_grad, "dp", scatter_dimension=0, tiled=True)
    else:
        out_grad = lax.psum_scatter(
            lax.dynamic_update_slice_in_dim(
                jnp.zeros((width, width), bf16), out_grad, position * own_width, 0
            ),
            BOTH,
            scatter_dimension=0,
            tiled=True,
        )
    out_grad_low = out_grad
    grad_normed_summ = lax.all_to_all(kept["summ"], "fsdp", 0, 0, tiled=True)
    grad_normed_summ = after(grad_normed_summ, *kept["late"])
    grad_normed_summ = jnp.sum(grad_normed_summ.astype(f32), axis=0)
    summ_own = lax.dynamic_slice_in_dim(
        jnp.pad(summ_inputs, more_rows),
        position * summ_share,
        summ_share,
        0,
    )
    qkv_grad = kept["qkv_parts"]
    if rows_held == HEAD and shards % 2 == 0:
        query_grad, key_grad, value_grad = spread_columns(qkv_grad)
    else:
        query_grad, key_grad, value_grad = (
            from_shards(qkv_grad[:, :, n * own_width : (n + 1) * own_width]).astype(f32)
            for n in range(3)
        )
    up_shift_grad = sum(unit_sums)
    query_shift_grad = jnp.concatenate([one[5][0] for one in pulled])
    value_shift_grad = jnp.concatenate([one[5][1] for one in pulled])
    grad_inputs, sums_one = norm_back(
        halves(tokens[0]), grad_normed, grad_resid, gain_one[None], False
    )
    grad_inputs = grad_inputs.reshape(tok_rows, width)
    result_terms, out_grad, others = after((result_terms, out_grad_low, kept["others"]), sums_one)
    if eight:
        result_terms = [(*result_terms[h], others[h]) for h in range(2)]
    out_grad = out_grad.astype(f32)
    result = jnp.concatenate(
        [(total(*result_terms[h]) + down_shift).astype(bf16) for h in range(2)], axis=0
    )
    _, norm_summ_pull = jax.vjp(layer_norm, summ_own, gain_one, shift_one)
    grad_summ, gain_summ_grad, shift_summ_grad = norm_summ_pull(grad_normed_summ)
    summary_cols = summaries.shape[2]
    grad_summ = lax.all_to_all(
        after(grad_summ, sums_one).reshape(summ_share, shards, summary_cols).transpose(1, 0, 2),
        "fsdp",
        0,
        0,
        tiled=True,
    )
    summary_grad = grad_summ.reshape(shards * summ_share, summary_cols)[:summary_rows]

    vector_grads = jnp.stack(
        [
            sums_one[0] + gain_summ_grad,
            sums_one[1] + shift_summ_grad,
            whole_columns(query_shift_grad),
            whole_columns(value_shift_grad),
            sums_two[2],
            sums_two[0],
            sums_two[1],
            sums_two[3],
        ]
    )
    vector_grads = vector_grads.reshape(8, devices, rows_held).transpose(1, 0, 2)
    unit_grads = lax.dynamic_update_index_in_dim(
        jnp.zeros((items, shards, units_held), f32),
        up_shift_grad.reshape(items, 1, units_held),
        position,
        1,
    )
    all_grads = jnp.concatenate(
        [vector_grads.reshape(devices, 8 * rows_held), unit_grads.reshape(devices, units_held)],
        axis=1,
    )
    all_grads = jnp.sum(lax.all_to_all(all_grads, BOTH, 0, 0, tiled=True), axis=0)
    (
        gain_one_grad, shift_one_grad, query_shift_grad, value_shift_grad, out_shift_grad,
        gain_two_grad, shift_two_grad, down_shift_grad,
    ) = (all_grads[n * rows_held : (n + 1) * rows_held] for n in range(8))
    up_shift_grad = all_grads[8 * rows_held :]
    return (
        result[None],
        grad_inputs[None],
        summary_grad[None],
        gain_one_grad,
        shift_one_grad,
        query_grad,
        query_shift_grad,
        key_grad,
        value_grad,
        value_shift_grad,
        out_grad,
        out_shift_grad,
        gain_two_grad,
        shift_two_grad,
        up_grad,
        up_shift_grad,
        down_grad,
        down_shift_grad,
    )


def solution(mesh):
    vector = P(BOTH)
    matrix = P(BOTH, None)
    rows = P("dp", "fsdp", None)
    columns = P("dp", None, "fsdp")
    return jax.shard_map(
        per_device,
        mesh=mesh,
        in_specs=(
            rows, columns, P("dp", None), P("dp"), rows, vector, vector, matrix, vector, matrix,
            matrix, vector, matrix, vector, vector, vector, matrix, vector, matrix, vector,
        ),
        out_specs=(
            rows, rows, columns, vector, vector, matrix, vector, matrix, matrix, vector, matrix,
            vector, vector, vector, matrix, vector, matrix, vector,
        ),
        check_vma=False,
    )
```

```python
import functools
import math

import jax
import jax.numpy as jnp
from jax import lax
from jax.experimental import pallas as pl
from jax.experimental.pallas import tpu as pltpu
from jax.sharding import PartitionSpec as P

HEAD = 64
SUMM = 50

epsilon = 1e-05
masked_score = -1e30
bf16 = jnp.bfloat16
f32 = jnp.float32
BOTH = ("dp", "fsdp")
score_scale = 1.0 / math.sqrt(HEAD)

ROWS_BY_ROWS = (((1,), (0,)), ((), ()))
ROWS_BY_COLS = (((1,), (1,)), ((), ()))
COLS_BY_ROWS = (((0,), (0,)), ((), ()))


def dot(left, right, dims):
    return lax.dot_general(left, right, dims, preferred_element_type=f32)


def layer_norm(values, gains, shifts):
    centre = jnp.mean(values, axis=-1, keepdims=True)
    centred = values - centre
    spread = jnp.mean(centred * centred, axis=-1, keepdims=True)
    return centred * lax.rsqrt(spread + epsilon) * gains + shifts


def gelu_tanh(values):
    return jax.nn.gelu(values, approximate=True)


def slot_order(devices):
    if devices == 8:
        return [
            (0, 0), (0, 1), (1, 0), (1, 1),
            (2, 0), (3, 0), (4, 1), (5, 1),
            (2, 1), (3, 1), (4, 0), (5, 0),
            (6, 0), (6, 1), (7, 0), (7, 1),
        ]
    return [(m, h) for m in range(devices) for h in range(2)]


def slot_groups(devices):
    return len(slot_order(devices)) // 4


def in_groups(items):
    return [items[n : n + 4] for n in range(0, len(items), 4)]


def swapped(x, bit):
    devices = lax.axis_size("fsdp")
    return lax.ppermute(x, "fsdp", [(i, i ^ bit) for i in range(devices)])


def sent(own):
    if lax.axis_size("fsdp") != 8:
        return None
    x0 = swapped(own[0], 2)
    y1 = swapped(own[1], 4)
    x1 = swapped(own[1], 2)
    y0 = swapped(own[0], 4)
    return x0, y1, x1, y0


def passed_on(own, hops, earlier=()):
    devices = lax.axis_size("fsdp")
    if devices != 8:
        pieces = [own]
        bit = 1
        while bit < devices:
            pieces = pieces + [[swapped(half, bit) for half in piece] for piece in pieces]
            bit *= 2
        return in_groups([half for piece in pieces for half in piece])
    x0, y1, x1, y0 = hops
    if earlier:
        x0, y1 = after((x0, y1), *earlier)
    a0 = swapped(x0, 4)
    a1 = swapped(y1, 2)
    return [
        [own[0], own[1], swapped(own[0], 1), swapped(own[1], 1)],
        [x0, swapped(x0, 1), y1, swapped(y1, 1)],
        [x1, swapped(x1, 1), y0, swapped(y0, 1)],
        [a0, a1, swapped(a0, 1), swapped(a1, 1)],
    ]


def total(*terms):
    result = terms[0].astype(f32)
    for term in terms[1:]:
        result = result + term.astype(f32)
    return result


def low_sums_kernel(counts, *refs):
    place = 0
    for count, out in zip(counts, refs[sum(counts) :]):
        terms = [ref[...].reshape(out.shape) for ref in refs[place : place + count]]
        out[...] = total(*terms).astype(bf16)
        place += count


def low_sums(*lists):
    half, wide = lists[0][0].shape
    chunk = half // 2
    rows = pl.BlockSpec((chunk, wide), lambda s: (s, 0))
    terms = [term for one in lists for term in one]

    def place_of(term):
        if not isinstance(term, tuple):
            return rows
        return pl.BlockSpec((1, chunk, wide), lambda s, slot=term[1]: (slot, s, 0))

    return pl.pallas_call(
        functools.partial(low_sums_kernel, [len(one) for one in lists]),
        grid=(2,),
        in_specs=[place_of(term) for term in terms],
        out_specs=[rows] * len(lists),
        out_shape=[jax.ShapeDtypeStruct((half, wide), bf16)] * len(lists),
        compiler_params=pltpu.CompilerParams(
            dimension_semantics=("arbitrary",), vmem_limit_bytes=32 * 2**20
        ),
        cost_estimate=pl.CostEstimate(
            flops=half * wide * len(terms),
            bytes_accessed=2 * half * wide * (len(terms) + len(lists)),
            transcendentals=0,
        ),
        name="low_sums",
    )(*[term[0] if isinstance(term, tuple) else term for term in terms])


def finish_kernel(count, *refs):
    other_ref, shift_ref, out_ref = refs[2 * count :]
    for h in range(2):
        terms = [ref[...] for ref in refs[h * count : (h + 1) * count]]
        out_ref[h] = (total(*terms, other_ref[h]) + shift_ref[...]).astype(bf16)


def finish(lists, others, shift):
    half, wide = lists[0][0].shape
    chunk = half // 2
    rows = pl.BlockSpec((chunk, wide), lambda s: (s, 0))
    both = pl.BlockSpec((2, chunk, wide), lambda s: (0, s, 0))
    terms = [term for one in lists for term in one]
    return pl.pallas_call(
        functools.partial(finish_kernel, len(lists[0])),
        grid=(2,),
        in_specs=[rows] * len(terms) + [both, held(shift.shape)],
        out_specs=both,
        out_shape=jax.ShapeDtypeStruct((2, half, wide), bf16),
        compiler_params=pltpu.CompilerParams(
            dimension_semantics=("arbitrary",), vmem_limit_bytes=40 * 2**20
        ),
        cost_estimate=pl.CostEstimate(
            flops=10 * half * wide, bytes_accessed=24 * half * wide, transcendentals=0
        ),
        name="finish",
    )(*terms, others, shift)


def plain_scattered_sum(groups):
    flat = [half for group in groups for half in group]
    bit = len(flat) // 4
    while bit > 1:
        flat = [
            total(flat[n], swapped(flat[n + 2 * bit], bit)).astype(bf16) for n in range(2 * bit)
        ]
        bit //= 2
    return [[flat[h], swapped(flat[h + 2], 1)] for h in range(2)]


def scattered_sum(make, groups, first=None, second=None):
    if groups != 4:
        made = [make(g, ()) for g in range(groups)]
        for extra in (first, second):
            if extra:
                done, use = extra(())
                use(done)
        return plain_scattered_sum(made)
    later = make(2, ())
    x1, y0 = low_sums([later[0], swapped(later[1], 1)], [later[2], swapped(later[3], 1)])
    if first:
        done, use = first((x1, y0))
        x1, y0, done = after((swapped(x1, 2), swapped(y0, 4), done))
        use(done)
        far = make(3, (x1, y0))
    else:
        far = make(3, (x1, y0))
        far, x1, y0 = after((far, swapped(x1, 2), swapped(y0, 4)))
    a0, a1 = low_sums([far[0], swapped(far[2], 1)], [far[1], swapped(far[3], 1)])
    near = make(1, (a0, a1))
    own = make(0, (a0, a1, near[0]))
    own, a0, a1 = after((own, swapped(a0, 4), swapped(a1, 2)))
    x0, y1 = low_sums([near[0], swapped(near[1], 1), a0], [near[2], swapped(near[3], 1), a1])
    mine = [[own[0], swapped(own[2], 1), y0], [own[1], swapped(own[3], 1), x1]]
    done, use = second((x0, y1)) if second else ((), None)
    x0, y1, mine, done = after((swapped(x0, 2), swapped(y1, 4), mine, done))
    if use:
        use(done)
    return [mine[0] + [x0], mine[1] + [y1]]


def after(values, *earlier):
    flat, tree = jax.tree.flatten(values)
    flat = lax.optimization_barrier(tuple(flat) + earlier)[: len(flat)]
    return jax.tree.unflatten(tree, flat)


def held(shape, place=None):
    where = place or (0,) * len(shape)
    return pl.BlockSpec(shape, lambda *_: where, pipeline_mode=pl.Buffered(1))


anywhere = pl.BlockSpec(memory_space=pl.ANY)


def half_rows(chunk, width):
    return pl.BlockSpec((chunk, width), lambda s: (s, 0))


def group_rows(group, chunk, width):
    return pl.BlockSpec((4, chunk, width), lambda s: (group, s, 0))


def group_call(kernel, name, steps, ins, specs, outs, out_specs, earlier, scratch, flops, moved):
    aliases = {len(ins) + n: n for n in range(len(earlier))}
    made = pl.pallas_call(
        functools.partial(kernel, len(ins), len(earlier)),
        grid=(steps,),
        in_specs=specs + [anywhere] * len(earlier),
        out_specs=out_specs,
        out_shape=outs,
        scratch_shapes=scratch,
        input_output_aliases=aliases,
        compiler_params=pltpu.CompilerParams(
            dimension_semantics=("arbitrary",), vmem_limit_bytes=52 * 2**20
        ),
        cost_estimate=pl.CostEstimate(flops=flops, bytes_accessed=moved, transcendentals=0),
        name=name,
    )(*ins, *earlier)
    return list(made)


def split_refs(n_ins, n_earlier, refs):
    return refs[:n_ins], refs[n_ins + n_earlier :]


def norm_kernel(n_ins, n_earlier, *refs):
    ins, rest = split_refs(n_ins, n_earlier, refs)
    gain_ref, shift_ref = ins[4:]
    for n in range(4):
        rest[0][n] = layer_norm(
            ins[n][...].astype(f32), gain_ref[...], shift_ref[...]
        ).astype(bf16)


def norm_rows(group, halves, gain, shift, earlier, slots):
    half, wide = halves[0].shape
    chunk = half // 2
    return group_call(
        norm_kernel,
        "norm_rows",
        2,
        list(halves) + [gain, shift],
        [half_rows(chunk, wide)] * 4 + [held(gain.shape), held(shift.shape)],
        [jax.ShapeDtypeStruct((slots, half, wide), bf16)],
        [group_rows(group, chunk, wide)],
        earlier,
        [],
        80 * half * wide,
        16 * half * wide,
    )


def triple_kernel(n_ins, n_earlier, *refs):
    (rows_ref, weight_ref, bias_ref), outs = split_refs(n_ins, n_earlier, refs)
    width = outs[0].shape[1]
    made = (dot(rows_ref[...], weight_ref[...], ROWS_BY_ROWS) + bias_ref[...]).astype(bf16)
    for place in range(3):
        outs[place][...] = made[:, place * width : (place + 1) * width]


def triple(first, steps, rows, weight, bias, earlier, count):
    wide = rows.shape[1]
    size = count // slot_groups(lax.axis_size("fsdp"))
    width = weight.shape[1] // 3
    return group_call(
        triple_kernel,
        "triple",
        steps,
        [rows, weight, bias],
        [
            pl.BlockSpec((size, wide), lambda s: (s + first, 0)),
            held(weight.shape),
            held(bias.shape),
        ],
        [jax.ShapeDtypeStruct((count, width), bf16)] * 3,
        [pl.BlockSpec((size, width), lambda s: (s + first, 0))] * 3,
        earlier,
        [],
        6 * steps * size * wide * width,
        2 * steps * size * wide,
    )


def norm_back_kernel(count, low, *refs):
    values, terms, rest = refs[:2], refs[2 : 2 + 2 * count], refs[2 + 2 * count :]
    extra_ref, gain_ref, grad_ref, sum_ref = rest[:4]

    @pl.when(pl.program_id(0) == 0)
    def _():
        sum_ref[...] = jnp.zeros_like(sum_ref)

    def average(one):
        return jnp.mean(one, axis=-1, keepdims=True)

    def add_rows(place, one):
        sum_ref[place : place + 1, :] += jnp.sum(one, axis=0, keepdims=True)

    for h in range(2):
        value = values[h][...].astype(f32)
        grad = total(*[ref[...] for ref in terms[h * count : (h + 1) * count]])
        extra = extra_ref[h].astype(f32)
        centred = value - average(value)
        rate = lax.rsqrt(average(centred * centred) + epsilon)
        unit = centred * rate
        scaled = grad * gain_ref[...]
        back = (scaled - average(scaled) - unit * average(scaled * unit)) * rate + extra
        grad_ref[h] = back
        add_rows(0, grad * unit)
        add_rows(1, grad)
        if low:
            rounded = back.astype(bf16)
            rest[4 + h][...] = rounded
            add_rows(2, rounded.astype(f32))
            add_rows(3, extra)


def norm_back(values, sums, extra, gain, low):
    half, wide = values[0].shape
    chunk = min(half, 64)
    rows = half_rows(chunk, wide)
    both = pl.BlockSpec((2, chunk, wide), lambda s: (0, s, 0))
    outs = [
        jax.ShapeDtypeStruct((2, half, wide), f32), jax.ShapeDtypeStruct((8, wide), f32)
    ] + [jax.ShapeDtypeStruct((half, wide), bf16)] * (2 * low)
    return pl.pallas_call(
        functools.partial(norm_back_kernel, len(sums[0]), low),
        grid=(half // chunk,),
        in_specs=[rows] * (2 + 2 * len(sums[0])) + [both, held(gain.shape)],
        out_specs=[both, pl.BlockSpec((8, wide), lambda s: (0, 0))] + [rows] * (2 * low),
        out_shape=outs,
        compiler_params=pltpu.CompilerParams(
            dimension_semantics=("arbitrary",), vmem_limit_bytes=40 * 2**20
        ),
        cost_estimate=pl.CostEstimate(
            flops=80 * half * wide, bytes_accessed=36 * half * wide, transcendentals=0
        ),
        name="norm_back",
    )(*values, *sums[0], *sums[1], extra, gain)


def project_kernel(n_ins, n_earlier, *refs):
    ins, rest = split_refs(n_ins, n_earlier, refs)
    weight_ref, outs = ins[-1], rest[:4]
    chunk, wide = outs[0].shape
    parts = [ref[...].reshape(4 * chunk, ref.shape[2]) for ref in ins[:-1]]
    rows = parts[0] if len(parts) == 1 else jnp.concatenate(parts, axis=1)
    by_rows = weight_ref.shape[0] == rows.shape[1] and weight_ref.shape[1] == wide
    tile = min(wide, 512)
    for start in range(0, wide, tile):
        columns = slice(start, start + tile)
        if by_rows:
            made = dot(rows, weight_ref[:, columns], ROWS_BY_ROWS)
        else:
            made = dot(rows, weight_ref[columns, :], ROWS_BY_COLS)
        made = made.astype(bf16)
        for n in range(4):
            outs[n][:, columns] = made[n * chunk : (n + 1) * chunk, :]


def project(group, parts, weight, wide):
    half = parts[0].shape[1]
    chunk = half // 2
    return group_call(
        project_kernel,
        "project",
        2,
        list(parts) + [weight],
        [group_rows(group, chunk, part.shape[2]) for part in parts] + [held(weight.shape)],
        [jax.ShapeDtypeStruct((half, wide), bf16)] * 4,
        [half_rows(chunk, wide)] * 4,
        [],
        [],
        8 * half * weight.size,
        8 * half * wide + 2 * weight.size,
    )


def project_back_kernel(n_ins, n_earlier, *refs):
    ins, rest = split_refs(n_ins, n_earlier, refs)
    weight_ref = ins[4]
    made_ref, kept_ref, rows = rest
    chunk = ins[0].shape[0]
    for n in range(4):
        kept_ref[n] = ins[n][...]
        rows[n * chunk : (n + 1) * chunk, :] = ins[n][...]
    made = dot(rows[...], weight_ref[...], ROWS_BY_COLS).astype(bf16)
    for n in range(4):
        made_ref[n] = made[n * chunk : (n + 1) * chunk, :]


def project_back(group, halves, weight, earlier, slots):
    half, wide = halves[0].shape
    chunk = half // 2
    width = weight.shape[0]
    return group_call(
        project_back_kernel,
        "project_back",
        2,
        list(halves) + [weight],
        [half_rows(chunk, wide)] * 4 + [held(weight.shape)],
        [jax.ShapeDtypeStruct((slots, half, n), bf16) for n in (width, wide)],
        [group_rows(group, chunk, n) for n in (width, wide)],
        earlier,
        [pltpu.VMEM((4 * chunk, wide), bf16)],
        8 * half * weight.size,
        16 * half * wide,
    )


gelu_rate = math.sqrt(2.0 / math.pi)
gelu_cube = 0.044715


def feed_forward_kernel(keep, n_ins, n_earlier, *refs):
    ins, rest = split_refs(n_ins, n_earlier, refs)
    up_ref, shift_ref, down_ref = ins[8:]
    active_ref, grad_ref, rows_ref, grad_rows_ref, other_ref = rest[:5]
    back = rest[5:9]
    gone = [n for n in range(4) if n not in keep]
    ahead = [
        rest[9 + keep.index(n)] if n in keep else other_ref.at[gone.index(n)] for n in range(4)
    ]
    shift_grad_ref, rows, grad_rows, active, grad_upper = rest[11:]
    chunk, wide = ins[0].shape
    units = up_ref.shape[1]
    for n in range(4):
        r = slice(n * chunk, (n + 1) * chunk)
        rows[r, :] = ins[n][...]
        grad_rows[r, :] = ins[4 + n][...]
        rows_ref[n] = ins[n][...]
        grad_rows_ref[n] = ins[4 + n][...]
    tile = min(units, 512)

    def hidden(t, carry):
        columns = pl.ds(pl.multiple_of(t * tile, tile), tile)
        upper = dot(rows[...], up_ref[:, columns], ROWS_BY_ROWS) + shift_ref[:, columns]
        grad_active = dot(grad_rows[...], down_ref[columns, :], ROWS_BY_COLS)
        square = upper * upper
        bend = jnp.tanh(gelu_rate * upper * (1.0 + gelu_cube * square))
        share = 0.5 * (1.0 + bend)
        slope = share + 0.5 * upper * (1.0 - bend * bend) * (
            gelu_rate * (1.0 + 3.0 * gelu_cube * square)
        )
        made = (upper * share).astype(bf16)
        grad = (grad_active * slope).astype(bf16)
        active[:, columns] = made
        grad_upper[:, columns] = grad
        shift_grad_ref[0, 0:1, columns] = jnp.sum(grad.astype(f32), axis=0, keepdims=True)
        for n in range(4):
            r = slice(n * chunk, (n + 1) * chunk)
            active_ref[n, :, columns] = made[r, :]
            grad_ref[n, :, columns] = grad[r, :]
        return carry

    lax.fori_loop(0, units // tile, hidden, 0)
    step = min(wide, 1024)

    def outer(t, carry):
        columns = pl.ds(pl.multiple_of(t * step, step), step)
        made_back = dot(grad_upper[...], up_ref[columns, :], ROWS_BY_COLS).astype(bf16)
        made_ahead = dot(active[...], down_ref[:, columns], ROWS_BY_ROWS).astype(bf16)
        for n in range(4):
            r = slice(n * chunk, (n + 1) * chunk)
            back[n][:, columns] = made_back[r, :]
            ahead[n][:, columns] = made_ahead[r, :]
        return carry

    lax.fori_loop(0, wide // step, outer, 0)


def feed_forward(group, keep, halves, grad_halves, up, shift, down, earlier, slots):
    half, wide = halves[0].shape
    chunk = half // 2
    units = up.shape[1]
    sizes = (units, units, wide, wide)
    outs = [jax.ShapeDtypeStruct((slots, half, n), bf16) for n in sizes]
    outs += [jax.ShapeDtypeStruct((slots // 2, half, wide), bf16)]
    outs += [jax.ShapeDtypeStruct((half, wide), bf16)] * 6
    outs += [jax.ShapeDtypeStruct((2, 8, units), f32)]
    made = group_call(
        functools.partial(feed_forward_kernel, keep),
        "feed_forward",
        2,
        list(halves) + list(grad_halves) + [up, shift, down],
        [half_rows(chunk, wide)] * 8 + [held(up.shape), held(shift.shape), held(down.shape)],
        outs,
        [group_rows(group, chunk, n) for n in sizes]
        + [pl.BlockSpec((2, chunk, wide), lambda s: (group, s, 0))]
        + [half_rows(chunk, wide)] * 6
        + [pl.BlockSpec((1, 8, units), lambda s: (s, 0, 0))],
        earlier,
        [pltpu.VMEM((4 * chunk, n), bf16) for n in (wide, wide, units, units)],
        32 * half * wide * units,
        48 * half * wide + 4 * wide * units,
    )
    return made[:5], made[5:9], made[9:11], jnp.sum(made[11][:, 0], axis=0)


def only_head(values, head):
    columns = lax.broadcasted_iota(jnp.int32, values.shape, 1) // HEAD
    return jnp.where(columns == head, values, jnp.zeros_like(values))


def transposed(values):
    return values.astype(f32).T.astype(bf16)


def places_of(plan_ref, blocks, subs, half, j):
    return [
        pl.ds(pl.multiple_of(plan_ref[3 * blocks + subs * j + n] * half, half), half)
        for n in range(subs)
    ]


def rows_of(ref, places):
    parts = [ref[place, :] for place in places]
    return parts[0] if len(parts) == 1 else jnp.concatenate(parts, axis=0)


def cols_of(ref, places):
    parts = [ref[:, place] for place in places]
    return parts[0] if len(parts) == 1 else jnp.concatenate(parts, axis=1)


def attn_forward_kernel(
    block, half, heads, plan_ref, q_ref, k_ref, v_ref, sk_ref, sv_ref, row_ref, o_ref, log_ref,
    q_heads, vt_all, svt, tops, sums, mixed,
):
    i = pl.program_id(0)
    blocks = pl.num_programs(0)
    subs = block // half

    @pl.when(i == 0)
    def _():
        for n in range(v_ref.shape[0] // half):
            r = slice(n * half, (n + 1) * half)
            vt_all[:, r] = transposed(v_ref[r, :])
        svt[...] = transposed(sv_ref[...])

    mine = places_of(plan_ref, blocks, subs, half, i)
    q = rows_of(q_ref, mine).astype(f32) * score_scale
    for h in range(heads):
        q_heads[h] = only_head(q, h).astype(bf16)
    tops[...] = jnp.full_like(tops, masked_score)
    sums[...] = jnp.zeros_like(sums)
    mixed[...] = jnp.zeros_like(mixed)
    lowest = row_ref[0:1, :]
    highest = row_ref[1:2, :]
    summ_end = row_ref[2:3, :]
    me = row_ref[3:4, :]

    def step(keys, values_t, mask):
        each = range(heads)
        scores = [dot(keys, q_heads[h], ROWS_BY_COLS) for h in each]
        if mask is not None:
            scores = [jnp.where(mask, one, masked_score) for one in scores]
        before = [tops[h : h + 1, :] for h in each]
        top = [jnp.maximum(before[h], jnp.max(scores[h], axis=0, keepdims=True)) for h in each]
        weights = [jnp.exp(scores[h] - top[h]) for h in each]
        keep = [jnp.exp(before[h] - top[h]) for h in each]
        added = [jnp.sum(weights[h], axis=0, keepdims=True) for h in each]
        totals = [keep[h] * sums[h : h + 1, :] + added[h] for h in each]
        part_of = [slice(h * HEAD, (h + 1) * HEAD) for h in each]
        more = [dot(values_t[part_of[h], :], weights[h].astype(bf16), ROWS_BY_ROWS) for h in each]
        result = [keep[h] * mixed[part_of[h], :] + more[h] for h in each]
        for h in each:
            tops[h : h + 1, :] = top[h]
            sums[h : h + 1, :] = totals[h]
            mixed[part_of[h], :] = result[h]

    @pl.when(plan_ref[2 * blocks + i] > 0)
    def _():
        places = lax.broadcasted_iota(jnp.int32, (sk_ref.shape[0], block), 0)
        step(sk_ref[...], svt[...], places < summ_end)

    def whole(j, carry):
        there = places_of(plan_ref, blocks, subs, half, j)
        step(rows_of(k_ref, there), cols_of(vt_all, there), None)
        return carry

    def part(j, carry):
        there = places_of(plan_ref, blocks, subs, half, j)
        places = j * block + lax.broadcasted_iota(jnp.int32, (block, block), 0)
        mask = ((places >= lowest) & (places <= highest)) | (places == me)
        step(rows_of(k_ref, there), cols_of(vt_all, there), mask)
        return carry

    lax.fori_loop(plan_ref[i], plan_ref[blocks + i], whole, 0)
    lax.fori_loop(plan_ref[blocks + i], i + 1, part, 0)
    for h in range(heads):
        r = slice(h * HEAD, (h + 1) * HEAD)
        mixed[r, :] = mixed[r, :] * (1.0 / sums[h : h + 1, :])
    log_ref[...] = tops[...] + jnp.log(jnp.maximum(sums[...], 1e-37))
    made = mixed[...].T.astype(bf16)
    for n, place in enumerate(mine):
        o_ref[place, :] = made[n * half : (n + 1) * half, :]


def attn_backward_kernel(
    block, half, heads, plan_ref, q_ref, k_ref, v_ref, sk_ref, sv_ref, row_ref, log_ref, o_ref, do_ref, dq_ref, dk_ref, dv_ref, dsk_ref, dsv_ref, shift_ref, q_heads, do_heads, kt_all, skt, dq_sum,
    dk_sum, dv_sum, dsk_sum, dsv_sum,
):
    i = pl.program_id(0)
    blocks = pl.num_programs(0)
    subs = block // half

    @pl.when(i == 0)
    def _():
        dk_sum[...] = jnp.zeros_like(dk_sum)
        dv_sum[...] = jnp.zeros_like(dv_sum)
        dsk_sum[...] = jnp.zeros_like(dsk_sum)
        dsv_sum[...] = jnp.zeros_like(dsv_sum)
        for n in range(k_ref.shape[0] // half):
            r = slice(n * half, (n + 1) * half)
            kt_all[:, r] = transposed(k_ref[r, :])
        skt[...] = transposed(sk_ref[...])

    mine = places_of(plan_ref, blocks, subs, half, i)
    q = rows_of(q_ref, mine).astype(f32) * score_scale
    do = rows_of(do_ref, mine).astype(f32)
    for h in range(heads):
        q_heads[h] = only_head(q, h).astype(bf16)
        do_heads[h] = only_head(do, h).astype(bf16)
    both_t = (do * rows_of(o_ref, mine).astype(f32)).T
    row_terms = [
        jnp.sum(both_t[h * HEAD : (h + 1) * HEAD, :], axis=0, keepdims=True) for h in range(heads)
    ]
    dq_sum[...] = jnp.zeros_like(dq_sum)
    lowest = row_ref[0:1, :]
    highest = row_ref[1:2, :]
    summ_end = row_ref[2:3, :]
    me = row_ref[3:4, :]

    def step(keys, values, keys_t, mask):
        dk = dv = None
        for h in range(heads):
            scores = dot(keys, q_heads[h], ROWS_BY_COLS)
            if mask is not None:
                scores = jnp.where(mask, scores, masked_score)
            probs = jnp.exp(scores - log_ref[h : h + 1, :])
            grad_probs = dot(values, do_heads[h], ROWS_BY_COLS)
            grad_scores = (probs * (grad_probs - row_terms[h])).astype(bf16)
            r = slice(h * HEAD, (h + 1) * HEAD)
            dq_sum[r, :] += dot(keys_t[r, :], grad_scores, ROWS_BY_ROWS)
            dv_own = dot(probs.astype(bf16), do_heads[h], ROWS_BY_ROWS)
            dk_own = dot(grad_scores, q_heads[h], ROWS_BY_ROWS)
            dv = dv_own if dv is None else dv + dv_own
            dk = dk_own if dk is None else dk + dk_own
        return dk, dv

    @pl.when(plan_ref[2 * blocks + i] > 0)
    def _():
        places = lax.broadcasted_iota(jnp.int32, (sk_ref.shape[0], block), 0)
        dk, dv = step(sk_ref[...], sv_ref[...], skt[...], places < summ_end)
        dsk_sum[...] += dk
        dsv_sum[...] += dv

    def whole(j, masked):
        there = places_of(plan_ref, blocks, subs, half, j)
        mask = None
        if masked:
            places = j * block + lax.broadcasted_iota(jnp.int32, (block, block), 0)
            mask = ((places >= lowest) & (places <= highest)) | (places == me)
        dk, dv = step(rows_of(k_ref, there), rows_of(v_ref, there), cols_of(kt_all, there), mask)
        for n, place in enumerate(there):
            dk_sum[place, :] += dk[n * half : (n + 1) * half, :]
            dv_sum[place, :] += dv[n * half : (n + 1) * half, :]

    def plain(j, carry):
        whole(j, False)
        return carry

    def part(j, carry):
        whole(j, True)
        return carry

    lax.fori_loop(plan_ref[i], plan_ref[blocks + i], plain, 0)
    lax.fori_loop(plan_ref[blocks + i], i + 1, part, 0)
    made = (dq_sum[...] * score_scale).T.astype(bf16)
    for n, place in enumerate(mine):
        dq_ref[place, :] = made[n * half : (n + 1) * half, :]

    @pl.when(i == blocks - 1)
    def _():
        dk_ref[...] = dk_sum[...].astype(bf16)
        dv_ref[...] = dv_sum[...].astype(bf16)
        dsk_ref[...] = dsk_sum[...].astype(bf16)
        dsv_ref[...] = dsv_sum[...].astype(bf16)

        def added(ref):
            return jnp.sum(ref[...].astype(f32), axis=0, keepdims=True)

        shift_ref[...] = jnp.zeros_like(shift_ref)
        shift_ref[0:1, :] = added(dq_ref)
        shift_ref[1:2, :] = added(dv_ref) + added(dsv_ref)


def attn_forward(part, parts, plan, rows, q, k, v, sk, sv, block, half):
    count = q.shape[0]
    width = q.shape[1] // parts
    heads = width // HEAD
    by_cols = pl.BlockSpec((8, block), lambda i, *_: (0, i))
    pairs = count * count // 4
    return pl.pallas_call(
        functools.partial(attn_forward_kernel, block, half, heads),
        grid_spec=pltpu.PrefetchScalarGridSpec(
            num_scalar_prefetch=1,
            grid=(count // block,),
            in_specs=[held((one.shape[0], width), (0, part)) for one in (q, k, v, sk, sv)] + [by_cols],
            out_specs=[held((count, width)), by_cols],
            scratch_shapes=[
                pltpu.VMEM((heads, block, width), bf16),
                pltpu.VMEM((width, count), bf16),
                pltpu.VMEM((width, sk.shape[0]), bf16),
                pltpu.VMEM((8, block), f32),
                pltpu.VMEM((8, block), f32),
                pltpu.VMEM((width, block), f32),
            ],
        ),
        out_shape=[
            jax.ShapeDtypeStruct((count, width), bf16),
            jax.ShapeDtypeStruct((8, count), f32),
        ],
        compiler_params=pltpu.CompilerParams(
            dimension_semantics=("arbitrary",), vmem_limit_bytes=40 * 2**20
        ),
        cost_estimate=pl.CostEstimate(
            flops=16 * pairs * width, bytes_accessed=8 * count * width, transcendentals=pairs * heads
        ),
        name="attn_forward",
    )(plan, q, k, v, sk, sv, rows)


def attn_backward(part, parts, plan, rows, q, k, v, sk, sv, logs, o, do, block, half):
    count = q.shape[0]
    width = q.shape[1] // parts
    heads = width // HEAD
    by_cols = pl.BlockSpec((8, block), lambda i, *_: (0, i))
    pairs = count * count // 4
    long = jax.ShapeDtypeStruct((count, width), bf16)
    short = jax.ShapeDtypeStruct((sk.shape[0], width), bf16)
    shift = jax.ShapeDtypeStruct((8, width), f32)
    long_in = held((count, width), (0, part))
    short_in = held((sk.shape[0], width), (0, part))
    return pl.pallas_call(
        functools.partial(attn_backward_kernel, block, half, heads),
        grid_spec=pltpu.PrefetchScalarGridSpec(
            num_scalar_prefetch=1,
            grid=(count // block,),
            in_specs=[long_in] * 3
            + [short_in] * 2
            + [by_cols] * 2
            + [held((count, width)), long_in],
            out_specs=[held(one.shape) for one in (long, long, long, short, short, shift)],
            scratch_shapes=[
                pltpu.VMEM((heads, block, width), bf16),
                pltpu.VMEM((heads, block, width), bf16),
                pltpu.VMEM((width, count), bf16),
                pltpu.VMEM((width, sk.shape[0]), bf16),
                pltpu.VMEM((width, block), f32),
                pltpu.VMEM((count, width), f32),
                pltpu.VMEM((count, width), f32),
                pltpu.VMEM((sk.shape[0], width), f32),
                pltpu.VMEM((sk.shape[0], width), f32),
            ],
        ),
        out_shape=[long, long, long, short, short, shift],
        compiler_params=pltpu.CompilerParams(
            dimension_semantics=("arbitrary",), vmem_limit_bytes=48 * 2**20
        ),
        cost_estimate=pl.CostEstimate(
            flops=24 * pairs * width, bytes_accessed=20 * count * width, transcendentals=pairs * heads
        ),
        name="attn_backward",
    )(plan, q, k, v, sk, sv, rows, logs, o, do)


def spread_columns_kernel(parts_ref, *outs):
    shards = parts_ref.shape[0]
    width = parts_ref.shape[2] // 3
    for n, ref in enumerate(outs):
        for d in range(width // HEAD):
            start = n * width + d * HEAD
            for f in range(0, shards, 2):
                pair = [parts_ref[f + m, :, start : start + HEAD].astype(f32) for m in range(2)]
                place = (d * shards + f) * HEAD
                ref[:, place : place + 2 * HEAD] = jnp.concatenate(pair, axis=1)


def spread_columns(parts):
    shards, count, width = parts.shape
    return pl.pallas_call(
        spread_columns_kernel,
        out_shape=[jax.ShapeDtypeStruct((count, shards * width // 3), f32)] * 3,
        name="spread_columns",
    )(parts)


def attention_plan(lengths, padding, count, block, slots):
    places = jnp.arange(count, dtype=jnp.int32)
    ends = jnp.cumsum(lengths)
    passed = places[:, None] >= ends[None, :]
    segment = jnp.sum(passed.astype(jnp.int32), axis=1)
    lowest = jnp.max(jnp.where(passed, ends[None, :], 0), axis=1)
    living = count - padding
    highest = jnp.minimum(places, living - 1)
    nothing = jnp.zeros_like(places)
    rows = jnp.stack(
        [lowest, highest, segment * SUMM, places, nothing, nothing, nothing, nothing], axis=0
    )
    blocks = count // block
    starts = jnp.arange(blocks, dtype=jnp.int32) * block
    first = lowest.reshape(blocks, block)[:, 0] // block
    one_piece = lowest.reshape(blocks, block)[:, -1] <= first * block
    whole_end = jnp.maximum(jnp.minimum(starts, living) // block, first)
    split = jnp.where(one_piece, whole_end, first)
    summ_flag = (segment.reshape(blocks, block)[:, -1] > 0).astype(jnp.int32)
    return rows, jnp.concatenate([first, split, summ_flag, slots]).astype(jnp.int32)


def per_device(
    tokens,
    summaries,
    segment_lengths,
    pad_lengths,
    output_grad,
    norm1_gain,
    norm1_bias,
    query_weight,
    query_bias,
    key_weight,
    value_weight,
    value_bias,
    out_weight,
    out_bias,
    norm2_gain,
    norm2_bias,
    up_weight,
    up_bias,
    down_weight,
    down_bias,
):
    shards = lax.axis_size("fsdp")
    items = lax.axis_size("dp")
    devices = shards * items
    position = lax.axis_index("fsdp")
    tok_rows = tokens.shape[1]
    width = tokens.shape[2]
    count = tok_rows * shards
    own_width = width // shards
    rows_held = query_weight.shape[0]
    units_held = up_bias.shape[0]
    own_units = units_held * items
    hidden = units_held * devices
    summary_rows = summaries.shape[1]
    padded_summ = -(-summary_rows // 32) * 32
    spread = rows_held % HEAD == 0
    block = math.gcd(count, 512)

    def for_shards(weight):
        if spread:
            split = weight.reshape(rows_held, items, shards, rows_held)
            return split.transpose(2, 0, 1, 3).reshape(shards, rows_held, own_width)
        return weight.reshape(rows_held, shards, own_width).transpose(1, 0, 2)

    def from_shards(parts):
        if spread:
            split = parts.reshape(shards, rows_held, items, rows_held)
            return split.transpose(1, 2, 0, 3).reshape(rows_held, width)
        return parts.transpose(1, 0, 2).reshape(rows_held, width)

    def own_columns(vector):
        if spread:
            split = vector.reshape(items, shards, rows_held)
            return lax.dynamic_index_in_dim(split, position, 1, keepdims=False).reshape(own_width)
        return lax.dynamic_slice_in_dim(vector, position * own_width, own_width, 0)

    def whole_columns(vector):
        if spread:
            split = jnp.zeros((items, shards, rows_held), f32)
            return lax.dynamic_update_index_in_dim(
                split, vector.reshape(items, 1, rows_held), position, 1
            ).reshape(width)
        return lax.dynamic_update_slice_in_dim(
            jnp.zeros((width,), f32), vector, position * own_width, 0
        )

    half = tok_rows // 2
    order = slot_order(shards)
    groups = len(order) // 4
    eight = shards == 8

    def halves(whole):
        return [whole[:half], whole[half:]]

    def flat(slotted):
        return slotted.reshape(count, slotted.shape[2])

    def slot_rows(slotted):
        return slotted.reshape(slotted.shape[0] * half, slotted.shape[2])

    qkv_parts = jnp.concatenate(
        [for_shards(query_weight), for_shards(key_weight), for_shards(value_weight)], axis=2
    )
    qkv_parts = lax.all_to_all(qkv_parts, "fsdp", 0, 0, tiled=True)
    qkv_own = lax.all_gather(
        qkv_parts.reshape(shards * rows_held, 3 * own_width), "dp", axis=0, tiled=True
    )
    vectors = jnp.concatenate(
        [
            norm1_gain, norm1_bias, query_bias, value_bias, out_bias, norm2_gain, norm2_bias,
            down_bias, up_bias,
        ]
    ).astype(f32)
    vectors = lax.all_to_all(
        jnp.broadcast_to(vectors[None], (devices, vectors.shape[0])), BOTH, 0, 0, tiled=True
    )
    gain_one, shift_one, query_shift, value_shift, out_shift, gain_two, shift_two, down_shift = (
        vectors[:, n * rows_held : (n + 1) * rows_held].reshape(width) for n in range(8)
    )
    token_halves = after(halves(tokens[0]), qkv_parts, vectors)
    token_hops = sent(token_halves)
    grad_own = halves(output_grad[0])
    up_parts = up_weight.reshape(rows_held, items, shards, units_held).transpose(2, 0, 1, 3)
    up_parts = up_parts.reshape(shards, rows_held, own_units)
    more_slots = -(-padded_summ // half)

    query_shift = own_columns(query_shift)
    value_shift = own_columns(value_shift)
    qkv_shift = jnp.concatenate([query_shift, jnp.zeros_like(query_shift), value_shift])[None]

    def normed_group(g, group, normed):
        return norm_rows(
            g, group, gain_one[None], shift_one[None], normed, 4 * groups + more_slots
        )

    if eight:
        mine = [*token_halves, *[swapped(one, 1) for one in token_halves]]
        normed = normed_group(0, mine, [])
        x0, y1, x1, y0 = token_hops
        x0, y1, x1, y0 = after((x0, y1, x1, y0), normed[0], up_parts, *grad_own)
        a0, a1 = swapped(x0, 4), swapped(y1, 2)
        normed = normed_group(1, [x0, swapped(x0, 1), y1, swapped(y1, 1)], normed)
        normed = normed_group(2, [x1, swapped(x1, 1), y0, swapped(y0, 1)], normed)
        made = triple(0, groups - 1, slot_rows(normed[0]), qkv_own, qkv_shift, [], count)
        a0, a1, made = after((a0, a1, made))
        last_tokens = [a0, a1, swapped(a0, 1), swapped(a1, 1)]
    else:
        normed = []
        token_groups = passed_on(token_halves, token_hops)
        last_tokens = token_groups[-1]
        for g in range(groups - 1):
            normed = normed_group(g, token_groups[g], normed)
        made = triple(0, groups - 1, slot_rows(normed[0]), qkv_own, qkv_shift, [], count)
    up_shift = lax.dynamic_index_in_dim(
        vectors[:, 8 * rows_held :].reshape(items, shards, units_held), position, 1, keepdims=False
    ).reshape(1, own_units)

    early = token_hops[:2] if eight else ()
    if spread:
        both = after(jnp.concatenate([out_weight, down_weight], axis=0), *early)
        both = lax.all_gather(both, "dp", axis=0)
        out_own = both[:, :rows_held].reshape(own_width, width)
        down_shares = both
    else:
        out_own = lax.dynamic_slice_in_dim(
            lax.all_gather(out_weight, BOTH, axis=0, tiled=True), position * own_width, own_width, 0
        )
        down_shares = lax.all_gather(down_weight, "dp", axis=0)
    up_parts = after(up_parts, last_tokens[0])
    up_parts = lax.all_to_all(up_parts, "fsdp", 0, 0, tiled=True)
    grad_own = after(grad_own, *last_tokens)
    grad_hops = sent(grad_own)

    summ_full = after(
        jnp.broadcast_to(summaries, (shards,) + summaries.shape[1:]), last_tokens[0]
    )
    summ_full = lax.all_to_all(summ_full, "fsdp", 0, 0, tiled=True)
    normed = normed_group(groups - 1, last_tokens, normed)
    queries, keys, values = triple(
        groups - 1, 1, slot_rows(normed[0]), qkv_own, qkv_shift, made, count
    )
    queries, keys, values, summ_full = after((queries, keys, values, summ_full))
    summ_full = summ_full.transpose(1, 0, 2).reshape(summary_rows, width)
    summ_inputs = jnp.pad(summ_full, ((0, padded_summ - summary_rows), (0, 0))).astype(f32)
    normed_summ = layer_norm(summ_inputs, gain_one, shift_one).astype(bf16)
    extra_rows = ((0, more_slots * half - padded_summ), (0, 0))
    normed = lax.dynamic_update_slice(
        slot_rows(normed[0]), jnp.pad(normed_summ, extra_rows), (count, 0)
    )
    summ_qkv = dot(normed_summ, qkv_own, ROWS_BY_ROWS) + qkv_shift
    summ_keys = summ_qkv[:, own_width : 2 * own_width].astype(bf16)
    summ_values = summ_qkv[:, 2 * own_width :].astype(bf16)
    slot_of = [[order.index((m, h)) for h in range(2)] for m in range(shards)]
    slots = jnp.array(slot_of, jnp.int32)[jnp.arange(shards) ^ position].reshape(-1)
    rows, plan = attention_plan(segment_lengths[0], pad_lengths[0], count, block, slots)
    parts = 2 if own_width % 256 == 0 else 1
    attn = []
    logs = []
    for part in range(parts):
        one, log = attn_forward(
            part, parts, plan, rows, queries, keys, values, summ_keys, summ_values, block, half
        )
        if eight and part == 0:
            one, log, plan, *grad_hops = after((one, log, plan, *grad_hops))
            x0, y1, x1, y0 = grad_hops
            a0, a1 = swapped(x0, 4), swapped(y1, 2)
        elif eight:
            one, log, a0, a1, up_parts, out_own = after((one, log, a0, a1, up_parts, out_own))
            grad_groups = [
                [*grad_own, swapped(grad_own[0], 1), swapped(grad_own[1], 1)],
                [x0, swapped(x0, 1), y1, swapped(y1, 1)],
                [x1, swapped(x1, 1), y0, swapped(y0, 1)],
                [a0, a1, swapped(a0, 1), swapped(a1, 1)],
            ]
        attn.append(one)
        logs.append(log)
    if not eight:
        grad_groups = passed_on(grad_own, grad_hops)
    up_own = lax.all_gather(
        up_parts.reshape(shards * rows_held, own_units), "dp", axis=0, tiled=True
    )
    attn_slots = [one.reshape(4 * groups, half, own_width // parts) for one in attn]
    inputs = [one.astype(f32) for one in halves(tokens[0])]
    proj_sums = scattered_sum(
        lambda g, earlier: project(g, attn_slots, after(out_own, *earlier), width), groups
    )
    resid = [
        total(inputs[h], *proj_sums[h]) + out_shift for h in range(2)
    ]

    normed_two_own = [layer_norm(one, gain_two, shift_two).astype(bf16) for one in resid]
    two_hops = sent(normed_two_own)
    down_own = after(down_shares, *normed_two_own)[:, down_shares.shape[1] - units_held :]
    down_own = down_own.reshape(own_units, width)
    if eight:
        x0, y1, x1, y0 = two_hops
        x0, y1, down_own = after((x0, y1, down_own))
        two_hops = (x0, y1, x1, y0)
    two_groups = passed_on(normed_two_own, two_hops)
    made = []
    back = {}
    ahead = {}
    unit_sums = []

    def feed(g, earlier):
        nonlocal made
        for n in [1, 2, 3, 0] if eight else range(groups):
            if n not in back and g not in back:
                mine = two_groups[n]
                if n == 2 and eight:
                    x1, y0 = after((mine[0], mine[2]), back[1][0])
                    mine = [x1, swapped(x1, 1), y0, swapped(y0, 1)]
                keep = (0, 2) if eight and n in (1, 2) else (0, 1)
                made, back[n], ahead[n], unit_sum = feed_forward(
                    n, keep, mine, grad_groups[n], up_own, up_shift, after(down_own, *earlier),
                    made, 4 * groups,
                )
                unit_sums.append(unit_sum)
        return back[g]

    kept = {}

    def down_grad_of(earlier):
        active, grad_rows = flat(made[0]), flat(made[3])
        grad = dot(after(active, *earlier), grad_rows, COLS_BY_ROWS).astype(bf16)
        others = swapped(after(made[4], *earlier), 1) if eight else made[4]

        def use(done):
            kept["down"], kept["others"] = done

        return (grad, others), use

    def up_grad_of(earlier):
        grad_upper, normed_two = flat(feed_made[1]), flat(feed_made[2])
        return dot(after(normed_two, *earlier), grad_upper, COLS_BY_ROWS).astype(bf16)

    grad_normed_two = scattered_sum(feed, groups, None, down_grad_of)
    feed_made = made
    down_grad = lax.psum_scatter(kept["down"], "dp", scatter_dimension=0, tiled=True)
    grad_resid, sums_two, *grad_proj = norm_back(
        resid, grad_normed_two, output_grad.reshape(2, half, width), gain_two[None], True
    )

    proj_hops = sent(grad_proj)
    if eight:
        mine = grad_proj + [swapped(one, 1) for one in grad_proj]
        made = project_back(0, mine, out_own, [], 4 * groups)
        up_grad = up_grad_of((made[0],))
        x0, y1, x1, y0, up_grad = after((*proj_hops, up_grad))
        others = kept["others"]
        own, near, later, far = after([ahead[g] for g in range(groups)], up_grad)
        sends = low_sums(
            [later[0], (others, 4)],
            [later[1], (others, 5)],
            [far[0], (others, 6)],
            [far[1], (others, 7)],
        )
        near = [[near[0], (others, 2)], [near[1], (others, 3)]]
        a0, a1 = swapped(x0, 4), swapped(y1, 2)
        made = project_back(
            1, [x0, swapped(x0, 1), y1, swapped(y1, 1)], out_own, made, 4 * groups
        )
        made = project_back(
            2, [x1, swapped(x1, 1), y0, swapped(y0, 1)], out_own, made, 4 * groups
        )
        a0, a1, made, sends = after((a0, a1, made, sends))
        proj_groups = [None, None, None, [a0, a1, swapped(a0, 1), swapped(a1, 1)]]
    else:
        up_grad = up_grad_of(())
        made = []
        proj_groups = passed_on(grad_proj, proj_hops)
    up_grad = lax.psum_scatter(up_grad, "dp", scatter_dimension=0, tiled=True)
    up_grad = up_grad.reshape(shards, rows_held, own_units)
    if not eight:
        up_grad = lax.all_to_all(up_grad, "fsdp", 0, 0, tiled=True)
    ahead = [
        [*ahead[g], kept["others"][2 * g], kept["others"][2 * g + 1]] for g in range(groups)
    ]
    for g in range(groups - 1 if eight else 0, groups):
        halves_now = proj_groups[g]
        made = project_back(g, halves_now, out_own, made, 4 * groups)
    grad_attn, proj_rows = (flat(one) for one in made)
    grad_attn, down_grad = after((grad_attn, down_grad))
    if eight:
        x1, y0, a0, a1 = after(sends, *proj_groups[-1])
        travelling = [swapped(x1, 2), swapped(y0, 4), swapped(a0, 4), swapped(a1, 2)]
    else:
        result = plain_scattered_sum(ahead)
    pulled = []
    again = grad_attn
    for part in range(parts):
        one = list(attn_backward(
            part, parts, plan, rows, queries, keys, values, summ_keys, summ_values, logs[part],
            attn[part], again, block, half,
        ))
        if eight and part == 0:
            one, again, *travelling = after((one, again, *travelling))
            x1, y0, a0, a1 = travelling
            x0, y1 = low_sums(near[0] + [a0], near[1] + [a1])
            travelling = [swapped(x0, 2), swapped(y1, 4)]
            up_grad = after(up_grad, x0, y1)
            up_grad = lax.all_to_all(up_grad, "fsdp", 0, 0, tiled=True)
        elif eight:
            one, up_grad, *travelling = after((one, up_grad, *travelling))
        pulled.append(one)
    grad_slots = [
        pulled[part][n].reshape(4 * groups, half, own_width // parts)
        for n in range(3)
        for part in range(parts)
    ]
    grad_summ_kv = jnp.concatenate(
        [pulled[part][n] for n in (3, 4) for part in range(parts)], axis=1
    )

    summ_share = -(-padded_summ // (shards * 16)) * 16
    more_rows = ((0, summ_share * shards - padded_summ), (0, 0))

    def qkv_grad_of(earlier):
        slots_now, summ_now = after((grad_slots, grad_summ_kv), *earlier)
        grad_qkv = jnp.concatenate([flat(one) for one in slots_now], axis=1)
        grad_qkv = jnp.concatenate(
            [grad_qkv, jnp.pad(summ_now, (extra_rows[0], (own_width, 0)))], axis=0
        )
        grad = dot(normed, grad_qkv, COLS_BY_ROWS).astype(bf16)
        return grad, functools.partial(kept.__setitem__, "qkv")

    def side_work(earlier):
        kept["late"] = earlier
        grad = lax.psum_scatter(kept["qkv"], "dp", scatter_dimension=0, tiled=True)
        up_now, down_now = after((up_grad, down_grad), *earlier)
        grad = after(grad, *earlier).reshape(shards, rows_held, 3 * own_width)
        kept["qkv_parts"] = lax.all_to_all(grad, "fsdp", 0, 0, tiled=True)
        up_now = up_now.reshape(shards, rows_held, items, units_held).transpose(1, 2, 0, 3)
        up_now = up_now.reshape(rows_held, hidden).astype(f32)

        def use(done):
            kept.update(zip(("qkv_parts", "up", "down"), done))

        return (kept["qkv_parts"], up_now, down_now.astype(f32)), use

    if eight:
        x0, y1 = travelling
        result_terms = [(resid[0], own[0], y0, x0), (resid[1], own[1], x1, y1)]
    else:
        result_terms = [(resid[h], *result[h]) for h in range(2)]

    def grad_rows_back(g, earlier):
        if g == 1 or not eight:
            back = dot(after(grad_summ_kv, *earlier), qkv_own[:, own_width:], ROWS_BY_COLS)
            kept["summ"] = jnp.pad(back.astype(bf16), more_rows).reshape(shards, summ_share, width)
            columns = jnp.concatenate(after(attn, *earlier), axis=1)
            kept["out"] = dot(columns, proj_rows, COLS_BY_ROWS).astype(bf16)
        made = project(g, grad_slots, after(qkv_own, *earlier), width)
        if g == 1:
            made, kept["out"] = after((made, kept["out"]))
        return made

    grad_normed = scattered_sum(
        grad_rows_back,
        groups,
        qkv_grad_of,
        side_work,
    )
    out_grad = kept["out"]
    up_grad, down_grad = kept["up"], kept["down"]
    if spread:
        out_grad = lax.psum_scatter(out_grad, "dp", scatter_dimension=0, tiled=True)
    else:
        out_grad = lax.psum_scatter(
            lax.dynamic_update_slice_in_dim(
                jnp.zeros((width, width), bf16), out_grad, position * own_width, 0
            ),
            BOTH,
            scatter_dimension=0,
            tiled=True,
        )
    out_grad_low = out_grad
    grad_normed_summ = lax.all_to_all(kept["summ"], "fsdp", 0, 0, tiled=True)
    grad_normed_summ = after(grad_normed_summ, *kept["late"])
    grad_normed_summ = jnp.sum(grad_normed_summ.astype(f32), axis=0)
    summ_own = lax.dynamic_slice_in_dim(
        jnp.pad(summ_inputs, more_rows),
        position * summ_share,
        summ_share,
        0,
    )
    qkv_grad = kept["qkv_parts"]
    if rows_held == HEAD and shards % 2 == 0:
        query_grad, key_grad, value_grad = spread_columns(qkv_grad)
    else:
        query_grad, key_grad, value_grad = (
            from_shards(qkv_grad[:, :, n * own_width : (n + 1) * own_width]).astype(f32)
            for n in range(3)
        )
    up_shift_grad = sum(unit_sums)
    query_shift_grad = jnp.concatenate([one[5][0] for one in pulled])
    value_shift_grad = jnp.concatenate([one[5][1] for one in pulled])
    grad_inputs, sums_one = norm_back(
        halves(tokens[0]), grad_normed, grad_resid, gain_one[None], False
    )
    grad_inputs = grad_inputs.reshape(tok_rows, width)
    result_terms, out_grad, others = after((result_terms, out_grad_low, kept["others"]), sums_one)
    out_grad = out_grad.astype(f32)
    if eight:
        result = finish(result_terms, others, down_shift[None]).reshape(tok_rows, width)
    else:
        result = jnp.concatenate(
            [(total(*result_terms[h]) + down_shift).astype(bf16) for h in range(2)], axis=0
        )
    _, norm_summ_pull = jax.vjp(layer_norm, summ_own, gain_one, shift_one)
    grad_summ, gain_summ_grad, shift_summ_grad = norm_summ_pull(grad_normed_summ)
    summary_cols = summaries.shape[2]
    grad_summ = lax.all_to_all(
        after(grad_summ, sums_one).reshape(summ_share, shards, summary_cols).transpose(1, 0, 2),
        "fsdp",
        0,
        0,
        tiled=True,
    )
    summary_grad = grad_summ.reshape(shards * summ_share, summary_cols)[:summary_rows]

    vector_grads = jnp.stack(
        [
            sums_one[0] + gain_summ_grad,
            sums_one[1] + shift_summ_grad,
            whole_columns(query_shift_grad),
            whole_columns(value_shift_grad),
            sums_two[2],
            sums_two[0],
            sums_two[1],
            sums_two[3],
        ]
    )
    vector_grads = vector_grads.reshape(8, devices, rows_held).transpose(1, 0, 2)
    unit_grads = lax.dynamic_update_index_in_dim(
        jnp.zeros((items, shards, units_held), f32),
        up_shift_grad.reshape(items, 1, units_held),
        position,
        1,
    )
    all_grads = jnp.concatenate(
        [vector_grads.reshape(devices, 8 * rows_held), unit_grads.reshape(devices, units_held)],
        axis=1,
    )
    all_grads = jnp.sum(lax.all_to_all(all_grads, BOTH, 0, 0, tiled=True), axis=0)
    (
        gain_one_grad, shift_one_grad, query_shift_grad, value_shift_grad, out_shift_grad,
        gain_two_grad, shift_two_grad, down_shift_grad,
    ) = (all_grads[n * rows_held : (n + 1) * rows_held] for n in range(8))
    up_shift_grad = all_grads[8 * rows_held :]
    return (
        result[None],
        grad_inputs[None],
        summary_grad[None],
        gain_one_grad,
        shift_one_grad,
        query_grad,
        query_shift_grad,
        key_grad,
        value_grad,
        value_shift_grad,
        out_grad,
        out_shift_grad,
        gain_two_grad,
        shift_two_grad,
        up_grad,
        up_shift_grad,
        down_grad,
        down_shift_grad,
    )


def solution(mesh):
    vector = P(BOTH)
    matrix = P(BOTH, None)
    rows = P("dp", "fsdp", None)
    columns = P("dp", None, "fsdp")
    return jax.shard_map(
        per_device,
        mesh=mesh,
        in_specs=(
            rows, columns, P("dp", None), P("dp"), rows, vector, vector, matrix, vector, matrix,
            matrix, vector, matrix, vector, vector, vector, matrix, vector, matrix, vector,
        ),
        out_specs=(
            rows, rows, columns, vector, vector, matrix, vector, matrix, matrix, vector, matrix,
            vector, vector, vector, matrix, vector, matrix, vector,
        ),
        check_vma=False,
    )
```

```python
import functools
import math

import jax
import jax.numpy as jnp
from jax import lax
from jax.experimental import pallas as pl
from jax.experimental.pallas import tpu as pltpu
from jax.sharding import PartitionSpec as P

HEAD = 64
SUMM = 50

epsilon = 1e-05
masked_score = -1e30
bf16 = jnp.bfloat16
f32 = jnp.float32
BOTH = ("dp", "fsdp")
score_scale = 1.0 / math.sqrt(HEAD)

ROWS_BY_ROWS = (((1,), (0,)), ((), ()))
ROWS_BY_COLS = (((1,), (1,)), ((), ()))
COLS_BY_ROWS = (((0,), (0,)), ((), ()))


def dot(left, right, dims):
    return lax.dot_general(left, right, dims, preferred_element_type=f32)


def layer_norm(values, gains, shifts):
    centre = jnp.mean(values, axis=-1, keepdims=True)
    centred = values - centre
    spread = jnp.mean(centred * centred, axis=-1, keepdims=True)
    return centred * lax.rsqrt(spread + epsilon) * gains + shifts


def gelu_tanh(values):
    return jax.nn.gelu(values, approximate=True)


def slot_order(devices):
    if devices == 8:
        return [
            (0, 0), (0, 1), (1, 0), (1, 1),
            (2, 0), (3, 0), (4, 1), (5, 1),
            (2, 1), (3, 1), (4, 0), (5, 0),
            (6, 0), (6, 1), (7, 0), (7, 1),
        ]
    return [(m, h) for m in range(devices) for h in range(2)]


def slot_groups(devices):
    return len(slot_order(devices)) // 4


def in_groups(items):
    return [items[n : n + 4] for n in range(0, len(items), 4)]


def swapped(x, bit):
    devices = lax.axis_size("fsdp")
    return lax.ppermute(x, "fsdp", [(i, i ^ bit) for i in range(devices)])


def sent(own):
    if lax.axis_size("fsdp") != 8:
        return None
    x0 = swapped(own[0], 2)
    y1 = swapped(own[1], 4)
    x1 = swapped(own[1], 2)
    y0 = swapped(own[0], 4)
    return x0, y1, x1, y0


def passed_on(own, hops, earlier=()):
    devices = lax.axis_size("fsdp")
    if devices != 8:
        pieces = [own]
        bit = 1
        while bit < devices:
            pieces = pieces + [[swapped(half, bit) for half in piece] for piece in pieces]
            bit *= 2
        return in_groups([half for piece in pieces for half in piece])
    x0, y1, x1, y0 = hops
    if earlier:
        x0, y1 = after((x0, y1), *earlier)
    a0 = swapped(x0, 4)
    a1 = swapped(y1, 2)
    return [
        [own[0], own[1], swapped(own[0], 1), swapped(own[1], 1)],
        [x0, swapped(x0, 1), y1, swapped(y1, 1)],
        [x1, swapped(x1, 1), y0, swapped(y0, 1)],
        [a0, a1, swapped(a0, 1), swapped(a1, 1)],
    ]


def total(*terms):
    result = terms[0].astype(f32)
    for term in terms[1:]:
        result = result + term.astype(f32)
    return result


def low_sums_kernel(counts, *refs):
    place = 0
    for count, out in zip(counts, refs[sum(counts) :]):
        terms = [ref[...].reshape(out.shape) for ref in refs[place : place + count]]
        out[...] = total(*terms).astype(bf16)
        place += count


def low_sums(*lists):
    half, wide = lists[0][0].shape
    chunk = half // 2
    rows = pl.BlockSpec((chunk, wide), lambda s: (s, 0))
    terms = [term for one in lists for term in one]

    def place_of(term):
        if not isinstance(term, tuple):
            return rows
        return pl.BlockSpec((1, chunk, wide), lambda s, slot=term[1]: (slot, s, 0))

    return pl.pallas_call(
        functools.partial(low_sums_kernel, [len(one) for one in lists]),
        grid=(2,),
        in_specs=[place_of(term) for term in terms],
        out_specs=[rows] * len(lists),
        out_shape=[jax.ShapeDtypeStruct((half, wide), bf16)] * len(lists),
        compiler_params=pltpu.CompilerParams(
            dimension_semantics=("arbitrary",), vmem_limit_bytes=32 * 2**20
        ),
        cost_estimate=pl.CostEstimate(
            flops=half * wide * len(terms),
            bytes_accessed=2 * half * wide * (len(terms) + len(lists)),
            transcendentals=0,
        ),
        name="low_sums",
    )(*[term[0] if isinstance(term, tuple) else term for term in terms])


def plain_scattered_sum(groups):
    flat = [half for group in groups for half in group]
    bit = len(flat) // 4
    while bit > 1:
        flat = [
            total(flat[n], swapped(flat[n + 2 * bit], bit)).astype(bf16) for n in range(2 * bit)
        ]
        bit //= 2
    return [[flat[h], swapped(flat[h + 2], 1)] for h in range(2)]


def scattered_sum(make, groups, first=None, second=None):
    if groups != 4:
        made = [make(g, ()) for g in range(groups)]
        for extra in (first, second):
            if extra:
                done, use = extra(())
                use(done)
        return plain_scattered_sum(made)
    later = make(2, ())
    x1, y0 = low_sums([later[0], swapped(later[1], 1)], [later[2], swapped(later[3], 1)])
    if first:
        done, use = first((x1, y0))
        x1, y0, done = after((swapped(x1, 2), swapped(y0, 4), done))
        use(done)
        far = make(3, (x1, y0))
    else:
        far = make(3, (x1, y0))
        far, x1, y0 = after((far, swapped(x1, 2), swapped(y0, 4)))
    a0, a1 = low_sums([far[0], swapped(far[2], 1)], [far[1], swapped(far[3], 1)])
    near = make(1, (a0, a1))
    own = make(0, (a0, a1, near[0]))
    own, a0, a1 = after((own, swapped(a0, 4), swapped(a1, 2)))
    x0, y1 = low_sums([near[0], swapped(near[1], 1), a0], [near[2], swapped(near[3], 1), a1])
    mine = [[own[0], swapped(own[2], 1), y0], [own[1], swapped(own[3], 1), x1]]
    done, use = second((x0, y1)) if second else ((), None)
    x0, y1, mine, done = after((swapped(x0, 2), swapped(y1, 4), mine, done))
    if use:
        use(done)
    return [mine[0] + [x0], mine[1] + [y1]]


def after(values, *earlier):
    flat, tree = jax.tree.flatten(values)
    flat = lax.optimization_barrier(tuple(flat) + earlier)[: len(flat)]
    return jax.tree.unflatten(tree, flat)


def held(shape, place=None):
    where = place or (0,) * len(shape)
    return pl.BlockSpec(shape, lambda *_: where, pipeline_mode=pl.Buffered(1))


anywhere = pl.BlockSpec(memory_space=pl.ANY)


def half_rows(chunk, width):
    return pl.BlockSpec((chunk, width), lambda s: (s, 0))


def group_rows(group, chunk, width):
    return pl.BlockSpec((4, chunk, width), lambda s: (group, s, 0))


def group_call(kernel, name, steps, ins, specs, outs, out_specs, earlier, scratch, flops, moved):
    aliases = {len(ins) + n: n for n in range(len(earlier))}
    made = pl.pallas_call(
        functools.partial(kernel, len(ins), len(earlier)),
        grid=(steps,),
        in_specs=specs + [anywhere] * len(earlier),
        out_specs=out_specs,
        out_shape=outs,
        scratch_shapes=scratch,
        input_output_aliases=aliases,
        compiler_params=pltpu.CompilerParams(
            dimension_semantics=("arbitrary",), vmem_limit_bytes=52 * 2**20
        ),
        cost_estimate=pl.CostEstimate(flops=flops, bytes_accessed=moved, transcendentals=0),
        name=name,
    )(*ins, *earlier)
    return list(made)


def split_refs(n_ins, n_earlier, refs):
    return refs[:n_ins], refs[n_ins + n_earlier :]


def norm_kernel(n_ins, n_earlier, *refs):
    ins, rest = split_refs(n_ins, n_earlier, refs)
    gain_ref, shift_ref = ins[4:]
    for n in range(4):
        rest[0][n] = layer_norm(
            ins[n][...].astype(f32), gain_ref[...], shift_ref[...]
        ).astype(bf16)


def norm_rows(group, halves, gain, shift, earlier, slots):
    half, wide = halves[0].shape
    chunk = half // 2
    return group_call(
        norm_kernel,
        "norm_rows",
        2,
        list(halves) + [gain, shift],
        [half_rows(chunk, wide)] * 4 + [held(gain.shape), held(shift.shape)],
        [jax.ShapeDtypeStruct((slots, half, wide), bf16)],
        [group_rows(group, chunk, wide)],
        earlier,
        [],
        80 * half * wide,
        16 * half * wide,
    )


def triple_kernel(n_ins, n_earlier, *refs):
    (rows_ref, weight_ref, bias_ref), outs = split_refs(n_ins, n_earlier, refs)
    width = outs[0].shape[1]
    made = (dot(rows_ref[...], weight_ref[...], ROWS_BY_ROWS) + bias_ref[...]).astype(bf16)
    for place in range(3):
        outs[place][...] = made[:, place * width : (place + 1) * width]


def triple(first, steps, rows, weight, bias, earlier, count):
    wide = rows.shape[1]
    size = count // slot_groups(lax.axis_size("fsdp"))
    width = weight.shape[1] // 3
    return group_call(
        triple_kernel,
        "triple",
        steps,
        [rows, weight, bias],
        [
            pl.BlockSpec((size, wide), lambda s: (s + first, 0)),
            held(weight.shape),
            held(bias.shape),
        ],
        [jax.ShapeDtypeStruct((count, width), bf16)] * 3,
        [pl.BlockSpec((size, width), lambda s: (s + first, 0))] * 3,
        earlier,
        [],
        6 * steps * size * wide * width,
        2 * steps * size * wide,
    )


def norm_back_kernel(count, low, *refs):
    values, terms, rest = refs[:2], refs[2 : 2 + 2 * count], refs[2 + 2 * count :]
    extra_ref, gain_ref, grad_ref, sum_ref = rest[:4]

    @pl.when(pl.program_id(0) == 0)
    def _():
        sum_ref[...] = jnp.zeros_like(sum_ref)

    def average(one):
        return jnp.mean(one, axis=-1, keepdims=True)

    def add_rows(place, one):
        sum_ref[place : place + 1, :] += jnp.sum(one, axis=0, keepdims=True)

    for h in range(2):
        value = values[h][...].astype(f32)
        grad = total(*[ref[...] for ref in terms[h * count : (h + 1) * count]])
        extra = extra_ref[h].astype(f32)
        centred = value - average(value)
        rate = lax.rsqrt(average(centred * centred) + epsilon)
        unit = centred * rate
        scaled = grad * gain_ref[...]
        back = (scaled - average(scaled) - unit * average(scaled * unit)) * rate + extra
        grad_ref[h] = back
        add_rows(0, grad * unit)
        add_rows(1, grad)
        if low:
            rounded = back.astype(bf16)
            rest[4 + h][...] = rounded
            add_rows(2, rounded.astype(f32))
            add_rows(3, extra)


def norm_back(values, sums, extra, gain, low):
    half, wide = values[0].shape
    chunk = min(half, 128)
    rows = half_rows(chunk, wide)
    both = pl.BlockSpec((2, chunk, wide), lambda s: (0, s, 0))
    outs = [
        jax.ShapeDtypeStruct((2, half, wide), f32), jax.ShapeDtypeStruct((8, wide), f32)
    ] + [jax.ShapeDtypeStruct((half, wide), bf16)] * (2 * low)
    return pl.pallas_call(
        functools.partial(norm_back_kernel, len(sums[0]), low),
        grid=(half // chunk,),
        in_specs=[rows] * (2 + 2 * len(sums[0])) + [both, held(gain.shape)],
        out_specs=[both, pl.BlockSpec((8, wide), lambda s: (0, 0))] + [rows] * (2 * low),
        out_shape=outs,
        compiler_params=pltpu.CompilerParams(
            dimension_semantics=("arbitrary",), vmem_limit_bytes=40 * 2**20
        ),
        cost_estimate=pl.CostEstimate(
            flops=80 * half * wide, bytes_accessed=36 * half * wide, transcendentals=0
        ),
        name="norm_back",
    )(*values, *sums[0], *sums[1], extra, gain)


def project_kernel(n_ins, n_earlier, *refs):
    ins, rest = split_refs(n_ins, n_earlier, refs)
    weight_ref, outs = ins[-1], rest[:4]
    chunk, wide = outs[0].shape
    parts = [ref[...].reshape(4 * chunk, ref.shape[2]) for ref in ins[:-1]]
    rows = parts[0] if len(parts) == 1 else jnp.concatenate(parts, axis=1)
    by_rows = weight_ref.shape[0] == rows.shape[1] and weight_ref.shape[1] == wide
    tile = min(wide, 512)
    for start in range(0, wide, tile):
        columns = slice(start, start + tile)
        if by_rows:
            made = dot(rows, weight_ref[:, columns], ROWS_BY_ROWS)
        else:
            made = dot(rows, weight_ref[columns, :], ROWS_BY_COLS)
        made = made.astype(bf16)
        for n in range(4):
            outs[n][:, columns] = made[n * chunk : (n + 1) * chunk, :]


def project(group, parts, weight, wide):
    half = parts[0].shape[1]
    chunk = half // 2
    return group_call(
        project_kernel,
        "project",
        2,
        list(parts) + [weight],
        [group_rows(group, chunk, part.shape[2]) for part in parts] + [held(weight.shape)],
        [jax.ShapeDtypeStruct((half, wide), bf16)] * 4,
        [half_rows(chunk, wide)] * 4,
        [],
        [],
        8 * half * weight.size,
        8 * half * wide + 2 * weight.size,
    )


def project_back_kernel(n_ins, n_earlier, *refs):
    ins, rest = split_refs(n_ins, n_earlier, refs)
    weight_ref = ins[4]
    made_ref, kept_ref, rows = rest
    chunk = ins[0].shape[0]
    for n in range(4):
        kept_ref[n] = ins[n][...]
        rows[n * chunk : (n + 1) * chunk, :] = ins[n][...]
    made = dot(rows[...], weight_ref[...], ROWS_BY_COLS).astype(bf16)
    for n in range(4):
        made_ref[n] = made[n * chunk : (n + 1) * chunk, :]


def project_back(group, halves, weight, earlier, slots):
    half, wide = halves[0].shape
    chunk = half // 2
    width = weight.shape[0]
    return group_call(
        project_back_kernel,
        "project_back",
        2,
        list(halves) + [weight],
        [half_rows(chunk, wide)] * 4 + [held(weight.shape)],
        [jax.ShapeDtypeStruct((slots, half, n), bf16) for n in (width, wide)],
        [group_rows(group, chunk, n) for n in (width, wide)],
        earlier,
        [pltpu.VMEM((4 * chunk, wide), bf16)],
        8 * half * weight.size,
        16 * half * wide,
    )


gelu_rate = math.sqrt(2.0 / math.pi)
gelu_cube = 0.044715


def feed_forward_kernel(keep, n_ins, n_earlier, *refs):
    ins, rest = split_refs(n_ins, n_earlier, refs)
    up_ref, shift_ref, down_ref = ins[8:]
    active_ref, grad_ref, rows_ref, grad_rows_ref, other_ref = rest[:5]
    back = rest[5:9]
    gone = [n for n in range(4) if n not in keep]
    ahead = [
        rest[9 + keep.index(n)] if n in keep else other_ref.at[gone.index(n)] for n in range(4)
    ]
    shift_grad_ref, rows, grad_rows, active, grad_upper = rest[11:]
    chunk, wide = ins[0].shape
    units = up_ref.shape[1]
    for n in range(4):
        r = slice(n * chunk, (n + 1) * chunk)
        rows[r, :] = ins[n][...]
        grad_rows[r, :] = ins[4 + n][...]
        rows_ref[n] = ins[n][...]
        grad_rows_ref[n] = ins[4 + n][...]
    tile = min(units, 512)

    def hidden(t, carry):
        columns = pl.ds(pl.multiple_of(t * tile, tile), tile)
        upper = dot(rows[...], up_ref[:, columns], ROWS_BY_ROWS) + shift_ref[:, columns]
        grad_active = dot(grad_rows[...], down_ref[columns, :], ROWS_BY_COLS)
        square = upper * upper
        bend = jnp.tanh(gelu_rate * upper * (1.0 + gelu_cube * square))
        share = 0.5 * (1.0 + bend)
        slope = share + 0.5 * upper * (1.0 - bend * bend) * (
            gelu_rate * (1.0 + 3.0 * gelu_cube * square)
        )
        made = (upper * share).astype(bf16)
        grad = (grad_active * slope).astype(bf16)
        active[:, columns] = made
        grad_upper[:, columns] = grad
        shift_grad_ref[0, 0:1, columns] = jnp.sum(grad.astype(f32), axis=0, keepdims=True)
        for n in range(4):
            r = slice(n * chunk, (n + 1) * chunk)
            active_ref[n, :, columns] = made[r, :]
            grad_ref[n, :, columns] = grad[r, :]
        return carry

    lax.fori_loop(0, units // tile, hidden, 0)
    step = min(wide, 1024)

    def outer(t, carry):
        columns = pl.ds(pl.multiple_of(t * step, step), step)
        made_back = dot(grad_upper[...], up_ref[columns, :], ROWS_BY_COLS).astype(bf16)
        made_ahead = dot(active[...], down_ref[:, columns], ROWS_BY_ROWS).astype(bf16)
        for n in range(4):
            r = slice(n * chunk, (n + 1) * chunk)
            back[n][:, columns] = made_back[r, :]
            ahead[n][:, columns] = made_ahead[r, :]
        return carry

    lax.fori_loop(0, wide // step, outer, 0)


def feed_forward(group, keep, halves, grad_halves, up, shift, down, earlier, slots):
    half, wide = halves[0].shape
    chunk = half // 2
    units = up.shape[1]
    sizes = (units, units, wide, wide)
    outs = [jax.ShapeDtypeStruct((slots, half, n), bf16) for n in sizes]
    outs += [jax.ShapeDtypeStruct((slots // 2, half, wide), bf16)]
    outs += [jax.ShapeDtypeStruct((half, wide), bf16)] * 6
    outs += [jax.ShapeDtypeStruct((2, 8, units), f32)]
    made = group_call(
        functools.partial(feed_forward_kernel, keep),
        "feed_forward",
        2,
        list(halves) + list(grad_halves) + [up, shift, down],
        [half_rows(chunk, wide)] * 8 + [held(up.shape), held(shift.shape), held(down.shape)],
        outs,
        [group_rows(group, chunk, n) for n in sizes]
        + [pl.BlockSpec((2, chunk, wide), lambda s: (group, s, 0))]
        + [half_rows(chunk, wide)] * 6
        + [pl.BlockSpec((1, 8, units), lambda s: (s, 0, 0))],
        earlier,
        [pltpu.VMEM((4 * chunk, n), bf16) for n in (wide, wide, units, units)],
        32 * half * wide * units,
        48 * half * wide + 4 * wide * units,
    )
    return made[:5], made[5:9], made[9:11], jnp.sum(made[11][:, 0], axis=0)


def only_head(values, head):
    columns = lax.broadcasted_iota(jnp.int32, values.shape, 1) // HEAD
    return jnp.where(columns == head, values, jnp.zeros_like(values))


def transposed(values):
    return values.astype(f32).T.astype(bf16)


def places_of(plan_ref, blocks, subs, half, j):
    return [
        pl.ds(pl.multiple_of(plan_ref[3 * blocks + subs * j + n] * half, half), half)
        for n in range(subs)
    ]


def rows_of(ref, places):
    parts = [ref[place, :] for place in places]
    return parts[0] if len(parts) == 1 else jnp.concatenate(parts, axis=0)


def cols_of(ref, places):
    parts = [ref[:, place] for place in places]
    return parts[0] if len(parts) == 1 else jnp.concatenate(parts, axis=1)


def attn_forward_kernel(
    block, half, heads, plan_ref, q_ref, k_ref, v_ref, sk_ref, sv_ref, row_ref, o_ref, log_ref,
    q_heads, vt_all, svt, tops, sums, mixed,
):
    i = pl.program_id(0)
    blocks = pl.num_programs(0)
    subs = block // half

    @pl.when(i == 0)
    def _():
        for n in range(v_ref.shape[0] // half):
            r = slice(n * half, (n + 1) * half)
            vt_all[:, r] = transposed(v_ref[r, :])
        svt[...] = transposed(sv_ref[...])

    mine = places_of(plan_ref, blocks, subs, half, i)
    q = rows_of(q_ref, mine).astype(f32) * score_scale
    for h in range(heads):
        q_heads[h] = only_head(q, h).astype(bf16)
    tops[...] = jnp.full_like(tops, masked_score)
    sums[...] = jnp.zeros_like(sums)
    mixed[...] = jnp.zeros_like(mixed)
    lowest = row_ref[0:1, :]
    highest = row_ref[1:2, :]
    summ_end = row_ref[2:3, :]
    me = row_ref[3:4, :]

    def step(keys, values_t, mask):
        each = range(heads)
        scores = [dot(keys, q_heads[h], ROWS_BY_COLS) for h in each]
        if mask is not None:
            scores = [jnp.where(mask, one, masked_score) for one in scores]
        before = [tops[h : h + 1, :] for h in each]
        top = [jnp.maximum(before[h], jnp.max(scores[h], axis=0, keepdims=True)) for h in each]
        weights = [jnp.exp(scores[h] - top[h]) for h in each]
        keep = [jnp.exp(before[h] - top[h]) for h in each]
        added = [jnp.sum(weights[h], axis=0, keepdims=True) for h in each]
        totals = [keep[h] * sums[h : h + 1, :] + added[h] for h in each]
        part_of = [slice(h * HEAD, (h + 1) * HEAD) for h in each]
        more = [dot(values_t[part_of[h], :], weights[h].astype(bf16), ROWS_BY_ROWS) for h in each]
        result = [keep[h] * mixed[part_of[h], :] + more[h] for h in each]
        for h in each:
            tops[h : h + 1, :] = top[h]
            sums[h : h + 1, :] = totals[h]
            mixed[part_of[h], :] = result[h]

    @pl.when(plan_ref[2 * blocks + i] > 0)
    def _():
        places = lax.broadcasted_iota(jnp.int32, (sk_ref.shape[0], block), 0)
        step(sk_ref[...], svt[...], places < summ_end)

    def whole(j, carry):
        there = places_of(plan_ref, blocks, subs, half, j)
        step(rows_of(k_ref, there), cols_of(vt_all, there), None)
        return carry

    def part(j, carry):
        there = places_of(plan_ref, blocks, subs, half, j)
        places = j * block + lax.broadcasted_iota(jnp.int32, (block, block), 0)
        mask = ((places >= lowest) & (places <= highest)) | (places == me)
        step(rows_of(k_ref, there), cols_of(vt_all, there), mask)
        return carry

    lax.fori_loop(plan_ref[i], plan_ref[blocks + i], whole, 0)
    lax.fori_loop(plan_ref[blocks + i], i + 1, part, 0)
    for h in range(heads):
        r = slice(h * HEAD, (h + 1) * HEAD)
        mixed[r, :] = mixed[r, :] * (1.0 / sums[h : h + 1, :])
    log_ref[...] = tops[...] + jnp.log(jnp.maximum(sums[...], 1e-37))
    made = mixed[...].T.astype(bf16)
    for n, place in enumerate(mine):
        o_ref[place, :] = made[n * half : (n + 1) * half, :]


def attn_backward_kernel(
    block, half, heads, plan_ref, q_ref, k_ref, v_ref, sk_ref, sv_ref, row_ref, log_ref, o_ref, do_ref, dq_ref, dk_ref, dv_ref, dsk_ref, dsv_ref, shift_ref, q_heads, do_heads, kt_all, skt, dq_sum,
    dk_sum, dv_sum, dsk_sum, dsv_sum,
):
    i = pl.program_id(0)
    blocks = pl.num_programs(0)
    subs = block // half

    @pl.when(i == 0)
    def _():
        dk_sum[...] = jnp.zeros_like(dk_sum)
        dv_sum[...] = jnp.zeros_like(dv_sum)
        dsk_sum[...] = jnp.zeros_like(dsk_sum)
        dsv_sum[...] = jnp.zeros_like(dsv_sum)
        for n in range(k_ref.shape[0] // half):
            r = slice(n * half, (n + 1) * half)
            kt_all[:, r] = transposed(k_ref[r, :])
        skt[...] = transposed(sk_ref[...])

    mine = places_of(plan_ref, blocks, subs, half, i)
    q = rows_of(q_ref, mine).astype(f32) * score_scale
    do = rows_of(do_ref, mine).astype(f32)
    for h in range(heads):
        q_heads[h] = only_head(q, h).astype(bf16)
        do_heads[h] = only_head(do, h).astype(bf16)
    both_t = (do * rows_of(o_ref, mine).astype(f32)).T
    row_terms = [
        jnp.sum(both_t[h * HEAD : (h + 1) * HEAD, :], axis=0, keepdims=True) for h in range(heads)
    ]
    dq_sum[...] = jnp.zeros_like(dq_sum)
    lowest = row_ref[0:1, :]
    highest = row_ref[1:2, :]
    summ_end = row_ref[2:3, :]
    me = row_ref[3:4, :]

    def step(keys, values, keys_t, mask):
        dk = dv = None
        for h in range(heads):
            scores = dot(keys, q_heads[h], ROWS_BY_COLS)
            if mask is not None:
                scores = jnp.where(mask, scores, masked_score)
            probs = jnp.exp(scores - log_ref[h : h + 1, :])
            grad_probs = dot(values, do_heads[h], ROWS_BY_COLS)
            grad_scores = (probs * (grad_probs - row_terms[h])).astype(bf16)
            r = slice(h * HEAD, (h + 1) * HEAD)
            dq_sum[r, :] += dot(keys_t[r, :], grad_scores, ROWS_BY_ROWS)
            dv_own = dot(probs.astype(bf16), do_heads[h], ROWS_BY_ROWS)
            dk_own = dot(grad_scores, q_heads[h], ROWS_BY_ROWS)
            dv = dv_own if dv is None else dv + dv_own
            dk = dk_own if dk is None else dk + dk_own
        return dk, dv

    @pl.when(plan_ref[2 * blocks + i] > 0)
    def _():
        places = lax.broadcasted_iota(jnp.int32, (sk_ref.shape[0], block), 0)
        dk, dv = step(sk_ref[...], sv_ref[...], skt[...], places < summ_end)
        dsk_sum[...] += dk
        dsv_sum[...] += dv

    def whole(j, masked):
        there = places_of(plan_ref, blocks, subs, half, j)
        mask = None
        if masked:
            places = j * block + lax.broadcasted_iota(jnp.int32, (block, block), 0)
            mask = ((places >= lowest) & (places <= highest)) | (places == me)
        dk, dv = step(rows_of(k_ref, there), rows_of(v_ref, there), cols_of(kt_all, there), mask)
        for n, place in enumerate(there):
            dk_sum[place, :] += dk[n * half : (n + 1) * half, :]
            dv_sum[place, :] += dv[n * half : (n + 1) * half, :]

    def plain(j, carry):
        whole(j, False)
        return carry

    def part(j, carry):
        whole(j, True)
        return carry

    lax.fori_loop(plan_ref[i], plan_ref[blocks + i], plain, 0)
    lax.fori_loop(plan_ref[blocks + i], i + 1, part, 0)
    made = (dq_sum[...] * score_scale).T.astype(bf16)
    for n, place in enumerate(mine):
        dq_ref[place, :] = made[n * half : (n + 1) * half, :]

    @pl.when(i == blocks - 1)
    def _():
        dk_ref[...] = dk_sum[...].astype(bf16)
        dv_ref[...] = dv_sum[...].astype(bf16)
        dsk_ref[...] = dsk_sum[...].astype(bf16)
        dsv_ref[...] = dsv_sum[...].astype(bf16)

        def added(ref):
            return jnp.sum(ref[...].astype(f32), axis=0, keepdims=True)

        shift_ref[...] = jnp.zeros_like(shift_ref)
        shift_ref[0:1, :] = added(dq_ref)
        shift_ref[1:2, :] = added(dv_ref) + added(dsv_ref)


def attn_forward(part, parts, plan, rows, q, k, v, sk, sv, block, half):
    count = q.shape[0]
    width = q.shape[1] // parts
    heads = width // HEAD
    by_cols = pl.BlockSpec((8, block), lambda i, *_: (0, i))
    pairs = count * count // 4
    return pl.pallas_call(
        functools.partial(attn_forward_kernel, block, half, heads),
        grid_spec=pltpu.PrefetchScalarGridSpec(
            num_scalar_prefetch=1,
            grid=(count // block,),
            in_specs=[held((one.shape[0], width), (0, part)) for one in (q, k, v, sk, sv)] + [by_cols],
            out_specs=[held((count, width)), by_cols],
            scratch_shapes=[
                pltpu.VMEM((heads, block, width), bf16),
                pltpu.VMEM((width, count), bf16),
                pltpu.VMEM((width, sk.shape[0]), bf16),
                pltpu.VMEM((8, block), f32),
                pltpu.VMEM((8, block), f32),
                pltpu.VMEM((width, block), f32),
            ],
        ),
        out_shape=[
            jax.ShapeDtypeStruct((count, width), bf16),
            jax.ShapeDtypeStruct((8, count), f32),
        ],
        compiler_params=pltpu.CompilerParams(
            dimension_semantics=("arbitrary",), vmem_limit_bytes=40 * 2**20
        ),
        cost_estimate=pl.CostEstimate(
            flops=16 * pairs * width, bytes_accessed=8 * count * width, transcendentals=pairs * heads
        ),
        name="attn_forward",
    )(plan, q, k, v, sk, sv, rows)


def attn_backward(part, parts, plan, rows, q, k, v, sk, sv, logs, o, do, block, half):
    count = q.shape[0]
    width = q.shape[1] // parts
    heads = width // HEAD
    by_cols = pl.BlockSpec((8, block), lambda i, *_: (0, i))
    pairs = count * count // 4
    long = jax.ShapeDtypeStruct((count, width), bf16)
    short = jax.ShapeDtypeStruct((sk.shape[0], width), bf16)
    shift = jax.ShapeDtypeStruct((8, width), f32)
    long_in = held((count, width), (0, part))
    short_in = held((sk.shape[0], width), (0, part))
    return pl.pallas_call(
        functools.partial(attn_backward_kernel, block, half, heads),
        grid_spec=pltpu.PrefetchScalarGridSpec(
            num_scalar_prefetch=1,
            grid=(count // block,),
            in_specs=[long_in] * 3
            + [short_in] * 2
            + [by_cols] * 2
            + [held((count, width)), long_in],
            out_specs=[held(one.shape) for one in (long, long, long, short, short, shift)],
            scratch_shapes=[
                pltpu.VMEM((heads, block, width), bf16),
                pltpu.VMEM((heads, block, width), bf16),
                pltpu.VMEM((width, count), bf16),
                pltpu.VMEM((width, sk.shape[0]), bf16),
                pltpu.VMEM((width, block), f32),
                pltpu.VMEM((count, width), f32),
                pltpu.VMEM((count, width), f32),
                pltpu.VMEM((sk.shape[0], width), f32),
                pltpu.VMEM((sk.shape[0], width), f32),
            ],
        ),
        out_shape=[long, long, long, short, short, shift],
        compiler_params=pltpu.CompilerParams(
            dimension_semantics=("arbitrary",), vmem_limit_bytes=48 * 2**20
        ),
        cost_estimate=pl.CostEstimate(
            flops=24 * pairs * width, bytes_accessed=20 * count * width, transcendentals=pairs * heads
        ),
        name="attn_backward",
    )(plan, q, k, v, sk, sv, rows, logs, o, do)


def spread_columns_kernel(parts_ref, *outs):
    shards = parts_ref.shape[0]
    width = parts_ref.shape[2] // 3
    for n, ref in enumerate(outs):
        for d in range(width // HEAD):
            start = n * width + d * HEAD
            for f in range(0, shards, 2):
                pair = [parts_ref[f + m, :, start : start + HEAD].astype(f32) for m in range(2)]
                place = (d * shards + f) * HEAD
                ref[:, place : place + 2 * HEAD] = jnp.concatenate(pair, axis=1)


def spread_columns(parts):
    shards, count, width = parts.shape
    return pl.pallas_call(
        spread_columns_kernel,
        out_shape=[jax.ShapeDtypeStruct((count, shards * width // 3), f32)] * 3,
        name="spread_columns",
    )(parts)


def attention_plan(lengths, padding, count, block, slots):
    places = jnp.arange(count, dtype=jnp.int32)
    ends = jnp.cumsum(lengths)
    passed = places[:, None] >= ends[None, :]
    segment = jnp.sum(passed.astype(jnp.int32), axis=1)
    lowest = jnp.max(jnp.where(passed, ends[None, :], 0), axis=1)
    living = count - padding
    highest = jnp.minimum(places, living - 1)
    nothing = jnp.zeros_like(places)
    rows = jnp.stack(
        [lowest, highest, segment * SUMM, places, nothing, nothing, nothing, nothing], axis=0
    )
    blocks = count // block
    starts = jnp.arange(blocks, dtype=jnp.int32) * block
    first = lowest.reshape(blocks, block)[:, 0] // block
    one_piece = lowest.reshape(blocks, block)[:, -1] <= first * block
    whole_end = jnp.maximum(jnp.minimum(starts, living) // block, first)
    split = jnp.where(one_piece, whole_end, first)
    summ_flag = (segment.reshape(blocks, block)[:, -1] > 0).astype(jnp.int32)
    return rows, jnp.concatenate([first, split, summ_flag, slots]).astype(jnp.int32)


def per_device(
    tokens,
    summaries,
    segment_lengths,
    pad_lengths,
    output_grad,
    norm1_gain,
    norm1_bias,
    query_weight,
    query_bias,
    key_weight,
    value_weight,
    value_bias,
    out_weight,
    out_bias,
    norm2_gain,
    norm2_bias,
    up_weight,
    up_bias,
    down_weight,
    down_bias,
):
    shards = lax.axis_size("fsdp")
    items = lax.axis_size("dp")
    devices = shards * items
    position = lax.axis_index("fsdp")
    tok_rows = tokens.shape[1]
    width = tokens.shape[2]
    count = tok_rows * shards
    own_width = width // shards
    rows_held = query_weight.shape[0]
    units_held = up_bias.shape[0]
    own_units = units_held * items
    hidden = units_held * devices
    summary_rows = summaries.shape[1]
    padded_summ = -(-summary_rows // 32) * 32
    spread = rows_held % HEAD == 0
    block = math.gcd(count, 512)

    def for_shards(weight):
        if spread:
            split = weight.reshape(rows_held, items, shards, rows_held)
            return split.transpose(2, 0, 1, 3).reshape(shards, rows_held, own_width)
        return weight.reshape(rows_held, shards, own_width).transpose(1, 0, 2)

    def from_shards(parts):
        if spread:
            split = parts.reshape(shards, rows_held, items, rows_held)
            return split.transpose(1, 2, 0, 3).reshape(rows_held, width)
        return parts.transpose(1, 0, 2).reshape(rows_held, width)

    def own_columns(vector):
        if spread:
            split = vector.reshape(items, shards, rows_held)
            return lax.dynamic_index_in_dim(split, position, 1, keepdims=False).reshape(own_width)
        return lax.dynamic_slice_in_dim(vector, position * own_width, own_width, 0)

    def whole_columns(vector):
        if spread:
            split = jnp.zeros((items, shards, rows_held), f32)
            return lax.dynamic_update_index_in_dim(
                split, vector.reshape(items, 1, rows_held), position, 1
            ).reshape(width)
        return lax.dynamic_update_slice_in_dim(
            jnp.zeros((width,), f32), vector, position * own_width, 0
        )

    half = tok_rows // 2
    order = slot_order(shards)
    groups = len(order) // 4
    eight = shards == 8

    def halves(whole):
        return [whole[:half], whole[half:]]

    def flat(slotted):
        return slotted.reshape(count, slotted.shape[2])

    def slot_rows(slotted):
        return slotted.reshape(slotted.shape[0] * half, slotted.shape[2])

    qkv_parts = jnp.concatenate(
        [for_shards(query_weight), for_shards(key_weight), for_shards(value_weight)], axis=2
    )
    qkv_parts = lax.all_to_all(qkv_parts, "fsdp", 0, 0, tiled=True)
    qkv_own = lax.all_gather(
        qkv_parts.reshape(shards * rows_held, 3 * own_width), "dp", axis=0, tiled=True
    )
    vectors = jnp.concatenate(
        [
            norm1_gain, norm1_bias, query_bias, value_bias, out_bias, norm2_gain, norm2_bias,
            down_bias, up_bias,
        ]
    ).astype(f32)
    vectors = lax.all_to_all(
        jnp.broadcast_to(vectors[None], (devices, vectors.shape[0])), BOTH, 0, 0, tiled=True
    )
    gain_one, shift_one, query_shift, value_shift, out_shift, gain_two, shift_two, down_shift = (
        vectors[:, n * rows_held : (n + 1) * rows_held].reshape(width) for n in range(8)
    )
    token_halves = after(halves(tokens[0]), qkv_parts, vectors)
    token_hops = sent(token_halves)
    grad_own = halves(output_grad[0])
    up_parts = up_weight.reshape(rows_held, items, shards, units_held).transpose(2, 0, 1, 3)
    up_parts = up_parts.reshape(shards, rows_held, own_units)
    more_slots = -(-padded_summ // half)

    query_shift = own_columns(query_shift)
    value_shift = own_columns(value_shift)
    qkv_shift = jnp.concatenate([query_shift, jnp.zeros_like(query_shift), value_shift])[None]

    def normed_group(g, group, normed):
        return norm_rows(
            g, group, gain_one[None], shift_one[None], normed, 4 * groups + more_slots
        )

    if eight:
        mine = [*token_halves, *[swapped(one, 1) for one in token_halves]]
        normed = normed_group(0, mine, [])
        x0, y1, x1, y0 = token_hops
        x0, y1, x1, y0 = after((x0, y1, x1, y0), normed[0], up_parts, *grad_own)
        a0, a1 = swapped(x0, 4), swapped(y1, 2)
        normed = normed_group(1, [x0, swapped(x0, 1), y1, swapped(y1, 1)], normed)
        normed = normed_group(2, [x1, swapped(x1, 1), y0, swapped(y0, 1)], normed)
        made = triple(0, groups - 1, slot_rows(normed[0]), qkv_own, qkv_shift, [], count)
        a0, a1, made = after((a0, a1, made))
        last_tokens = [a0, a1, swapped(a0, 1), swapped(a1, 1)]
    else:
        normed = []
        token_groups = passed_on(token_halves, token_hops)
        last_tokens = token_groups[-1]
        for g in range(groups - 1):
            normed = normed_group(g, token_groups[g], normed)
        made = triple(0, groups - 1, slot_rows(normed[0]), qkv_own, qkv_shift, [], count)
    up_shift = lax.dynamic_index_in_dim(
        vectors[:, 8 * rows_held :].reshape(items, shards, units_held), position, 1, keepdims=False
    ).reshape(1, own_units)

    early = token_hops[:2] if eight else ()
    if spread:
        both = after(jnp.concatenate([out_weight, down_weight], axis=0), *early)
        both = lax.all_gather(both, "dp", axis=0)
        out_own = both[:, :rows_held].reshape(own_width, width)
        down_shares = both
    else:
        out_own = lax.dynamic_slice_in_dim(
            lax.all_gather(out_weight, BOTH, axis=0, tiled=True), position * own_width, own_width, 0
        )
        down_shares = lax.all_gather(down_weight, "dp", axis=0)
    up_parts = after(up_parts, last_tokens[0])
    up_parts = lax.all_to_all(up_parts, "fsdp", 0, 0, tiled=True)
    grad_own = after(grad_own, *last_tokens)
    grad_hops = sent(grad_own)

    summ_full = after(
        jnp.broadcast_to(summaries, (shards,) + summaries.shape[1:]), last_tokens[0]
    )
    summ_full = lax.all_to_all(summ_full, "fsdp", 0, 0, tiled=True)
    normed = normed_group(groups - 1, last_tokens, normed)
    queries, keys, values = triple(
        groups - 1, 1, slot_rows(normed[0]), qkv_own, qkv_shift, made, count
    )
    queries, keys, values, summ_full = after((queries, keys, values, summ_full))
    summ_full = summ_full.transpose(1, 0, 2).reshape(summary_rows, width)
    summ_inputs = jnp.pad(summ_full, ((0, padded_summ - summary_rows), (0, 0))).astype(f32)
    normed_summ = layer_norm(summ_inputs, gain_one, shift_one).astype(bf16)
    extra_rows = ((0, more_slots * half - padded_summ), (0, 0))
    normed = lax.dynamic_update_slice(
        slot_rows(normed[0]), jnp.pad(normed_summ, extra_rows), (count, 0)
    )
    summ_qkv = dot(normed_summ, qkv_own, ROWS_BY_ROWS) + qkv_shift
    summ_keys = summ_qkv[:, own_width : 2 * own_width].astype(bf16)
    summ_values = summ_qkv[:, 2 * own_width :].astype(bf16)
    slot_of = [[order.index((m, h)) for h in range(2)] for m in range(shards)]
    slots = jnp.array(slot_of, jnp.int32)[jnp.arange(shards) ^ position].reshape(-1)
    rows, plan = attention_plan(segment_lengths[0], pad_lengths[0], count, block, slots)
    parts = 2 if own_width % 256 == 0 else 1
    attn = []
    logs = []
    for part in range(parts):
        one, log = attn_forward(
            part, parts, plan, rows, queries, keys, values, summ_keys, summ_values, block, half
        )
        if eight and part == 0:
            one, log, plan, *grad_hops = after((one, log, plan, *grad_hops))
            x0, y1, x1, y0 = grad_hops
            a0, a1 = swapped(x0, 4), swapped(y1, 2)
        elif eight:
            one, log, a0, a1, up_parts, out_own = after((one, log, a0, a1, up_parts, out_own))
            grad_groups = [
                [*grad_own, swapped(grad_own[0], 1), swapped(grad_own[1], 1)],
                [x0, swapped(x0, 1), y1, swapped(y1, 1)],
                [x1, swapped(x1, 1), y0, swapped(y0, 1)],
                [a0, a1, swapped(a0, 1), swapped(a1, 1)],
            ]
        attn.append(one)
        logs.append(log)
    if not eight:
        grad_groups = passed_on(grad_own, grad_hops)
    up_own = lax.all_gather(
        up_parts.reshape(shards * rows_held, own_units), "dp", axis=0, tiled=True
    )
    attn_slots = [one.reshape(4 * groups, half, own_width // parts) for one in attn]
    inputs = [one.astype(f32) for one in halves(tokens[0])]
    proj_sums = scattered_sum(
        lambda g, earlier: project(g, attn_slots, after(out_own, *earlier), width), groups
    )
    resid = [
        total(inputs[h], *proj_sums[h]) + out_shift for h in range(2)
    ]

    normed_two_own = [layer_norm(one, gain_two, shift_two).astype(bf16) for one in resid]
    two_hops = sent(normed_two_own)
    down_own = after(down_shares, *normed_two_own)[:, down_shares.shape[1] - units_held :]
    down_own = down_own.reshape(own_units, width)
    if eight:
        x0, y1, x1, y0 = two_hops
        x0, y1, down_own = after((x0, y1, down_own))
        two_hops = (x0, y1, x1, y0)
    two_groups = passed_on(normed_two_own, two_hops)
    made = []
    back = {}
    ahead = {}
    unit_sums = []

    def feed(g, earlier):
        nonlocal made
        for n in [1, 2, 3, 0] if eight else range(groups):
            if n not in back and g not in back:
                mine = two_groups[n]
                if n == 2 and eight:
                    x1, y0 = after((mine[0], mine[2]), back[1][0])
                    mine = [x1, swapped(x1, 1), y0, swapped(y0, 1)]
                keep = (0, 2) if eight and n in (1, 2) else (0, 1)
                made, back[n], ahead[n], unit_sum = feed_forward(
                    n, keep, mine, grad_groups[n], up_own, up_shift, after(down_own, *earlier),
                    made, 4 * groups,
                )
                unit_sums.append(unit_sum)
        return back[g]

    kept = {}

    def down_grad_of(earlier):
        active, grad_rows = flat(made[0]), flat(made[3])
        grad = dot(after(active, *earlier), grad_rows, COLS_BY_ROWS).astype(bf16)
        others = swapped(after(made[4], *earlier), 1) if eight else made[4]

        def use(done):
            kept["down"], kept["others"] = done

        return (grad, others), use

    def up_grad_of(earlier):
        grad_upper, normed_two = flat(feed_made[1]), flat(feed_made[2])
        return dot(after(normed_two, *earlier), grad_upper, COLS_BY_ROWS).astype(bf16)

    grad_normed_two = scattered_sum(feed, groups, None, down_grad_of)
    feed_made = made
    down_grad = lax.psum_scatter(kept["down"], "dp", scatter_dimension=0, tiled=True)
    grad_resid, sums_two, *grad_proj = norm_back(
        resid, grad_normed_two, output_grad.reshape(2, half, width), gain_two[None], True
    )

    proj_hops = sent(grad_proj)
    if eight:
        mine = grad_proj + [swapped(one, 1) for one in grad_proj]
        made = project_back(0, mine, out_own, [], 4 * groups)
        up_grad = up_grad_of((made[0],))
        x0, y1, x1, y0, up_grad = after((*proj_hops, up_grad))
        others = kept["others"]
        own, near, later, far = after([ahead[g] for g in range(groups)], up_grad)
        sends = low_sums(
            [later[0], (others, 4)],
            [later[1], (others, 5)],
            [far[0], (others, 6)],
            [far[1], (others, 7)],
        )
        near = [[near[0], (others, 2)], [near[1], (others, 3)]]
        a0, a1 = swapped(x0, 4), swapped(y1, 2)
        made = project_back(
            1, [x0, swapped(x0, 1), y1, swapped(y1, 1)], out_own, made, 4 * groups
        )
        made = project_back(
            2, [x1, swapped(x1, 1), y0, swapped(y0, 1)], out_own, made, 4 * groups
        )
        a0, a1, made, sends = after((a0, a1, made, sends))
        proj_groups = [None, None, None, [a0, a1, swapped(a0, 1), swapped(a1, 1)]]
    else:
        up_grad = up_grad_of(())
        made = []
        proj_groups = passed_on(grad_proj, proj_hops)
    up_grad = lax.psum_scatter(up_grad, "dp", scatter_dimension=0, tiled=True)
    up_grad = up_grad.reshape(shards, rows_held, own_units)
    if not eight:
        up_grad = lax.all_to_all(up_grad, "fsdp", 0, 0, tiled=True)
    ahead = [
        [*ahead[g], kept["others"][2 * g], kept["others"][2 * g + 1]] for g in range(groups)
    ]
    for g in range(groups - 1 if eight else 0, groups):
        halves_now = proj_groups[g]
        made = project_back(g, halves_now, out_own, made, 4 * groups)
    grad_attn, proj_rows = (flat(one) for one in made)
    grad_attn, down_grad = after((grad_attn, down_grad))
    if eight:
        x1, y0, a0, a1 = after(sends, *proj_groups[-1])
        travelling = [swapped(x1, 2), swapped(y0, 4), swapped(a0, 4), swapped(a1, 2)]
    else:
        result = plain_scattered_sum(ahead)
    pulled = []
    again = grad_attn
    for part in range(parts):
        one = list(attn_backward(
            part, parts, plan, rows, queries, keys, values, summ_keys, summ_values, logs[part],
            attn[part], again, block, half,
        ))
        if eight and part == 0:
            one, again, *travelling = after((one, again, *travelling))
            x1, y0, a0, a1 = travelling
            x0, y1 = low_sums(near[0] + [a0], near[1] + [a1])
            travelling = [swapped(x0, 2), swapped(y1, 4)]
            up_grad = after(up_grad, x0, y1)
            up_grad = lax.all_to_all(up_grad, "fsdp", 0, 0, tiled=True)
        elif eight:
            one, up_grad, *travelling = after((one, up_grad, *travelling))
        pulled.append(one)
    grad_slots = [
        pulled[part][n].reshape(4 * groups, half, own_width // parts)
        for n in range(3)
        for part in range(parts)
    ]
    grad_summ_kv = jnp.concatenate(
        [pulled[part][n] for n in (3, 4) for part in range(parts)], axis=1
    )

    summ_share = -(-padded_summ // (shards * 16)) * 16
    more_rows = ((0, summ_share * shards - padded_summ), (0, 0))

    def qkv_grad_of(earlier):
        slots_now, summ_now = after((grad_slots, grad_summ_kv), *earlier)
        grad_qkv = jnp.concatenate([flat(one) for one in slots_now], axis=1)
        grad_qkv = jnp.concatenate(
            [grad_qkv, jnp.pad(summ_now, (extra_rows[0], (own_width, 0)))], axis=0
        )
        grad = dot(normed, grad_qkv, COLS_BY_ROWS).astype(bf16)
        return grad, functools.partial(kept.__setitem__, "qkv")

    def side_work(earlier):
        kept["late"] = earlier
        grad = lax.psum_scatter(kept["qkv"], "dp", scatter_dimension=0, tiled=True)
        up_now, down_now = after((up_grad, down_grad), *earlier)
        grad = after(grad, *earlier).reshape(shards, rows_held, 3 * own_width)
        kept["qkv_parts"] = lax.all_to_all(grad, "fsdp", 0, 0, tiled=True)
        up_now = up_now.reshape(shards, rows_held, items, units_held).transpose(1, 2, 0, 3)
        up_now = up_now.reshape(rows_held, hidden).astype(f32)

        def use(done):
            kept.update(zip(("qkv_parts", "up", "down"), done))

        return (kept["qkv_parts"], up_now, down_now.astype(f32)), use

    if eight:
        x0, y1 = travelling
        result_terms = [(resid[0], own[0], y0, x0), (resid[1], own[1], x1, y1)]
    else:
        result_terms = [(resid[h], *result[h]) for h in range(2)]

    def grad_rows_back(g, earlier):
        if g == 1 or not eight:
            back = dot(after(grad_summ_kv, *earlier), qkv_own[:, own_width:], ROWS_BY_COLS)
            kept["summ"] = jnp.pad(back.astype(bf16), more_rows).reshape(shards, summ_share, width)
            columns = jnp.concatenate(after(attn, *earlier), axis=1)
            kept["out"] = dot(columns, proj_rows, COLS_BY_ROWS).astype(bf16)
        made = project(g, grad_slots, after(qkv_own, *earlier), width)
        if g == 1:
            made, kept["out"] = after((made, kept["out"]))
        return made

    grad_normed = scattered_sum(
        grad_rows_back,
        groups,
        qkv_grad_of,
        side_work,
    )
    out_grad = kept["out"]
    up_grad, down_grad = kept["up"], kept["down"]
    if spread:
        out_grad = lax.psum_scatter(out_grad, "dp", scatter_dimension=0, tiled=True)
    else:
        out_grad = lax.psum_scatter(
            lax.dynamic_update_slice_in_dim(
                jnp.zeros((width, width), bf16), out_grad, position * own_width, 0
            ),
            BOTH,
            scatter_dimension=0,
            tiled=True,
        )
    out_grad_low = out_grad
    grad_normed_summ = lax.all_to_all(kept["summ"], "fsdp", 0, 0, tiled=True)
    grad_normed_summ = after(grad_normed_summ, *kept["late"])
    grad_normed_summ = jnp.sum(grad_normed_summ.astype(f32), axis=0)
    summ_own = lax.dynamic_slice_in_dim(
        jnp.pad(summ_inputs, more_rows),
        position * summ_share,
        summ_share,
        0,
    )
    qkv_grad = kept["qkv_parts"]
    if rows_held == HEAD and shards % 2 == 0:
        query_grad, key_grad, value_grad = spread_columns(qkv_grad)
    else:
        query_grad, key_grad, value_grad = (
            from_shards(qkv_grad[:, :, n * own_width : (n + 1) * own_width]).astype(f32)
            for n in range(3)
        )
    up_shift_grad = sum(unit_sums)
    query_shift_grad = jnp.concatenate([one[5][0] for one in pulled])
    value_shift_grad = jnp.concatenate([one[5][1] for one in pulled])
    grad_inputs, sums_one = norm_back(
        halves(tokens[0]), grad_normed, grad_resid, gain_one[None], False
    )
    grad_inputs = grad_inputs.reshape(tok_rows, width)
    result_terms, out_grad, others = after((result_terms, out_grad_low, kept["others"]), sums_one)
    if eight:
        result_terms = [(*result_terms[h], others[h]) for h in range(2)]
    out_grad = out_grad.astype(f32)
    result = jnp.concatenate(
        [(total(*result_terms[h]) + down_shift).astype(bf16) for h in range(2)], axis=0
    )
    _, norm_summ_pull = jax.vjp(layer_norm, summ_own, gain_one, shift_one)
    grad_summ, gain_summ_grad, shift_summ_grad = norm_summ_pull(grad_normed_summ)
    summary_cols = summaries.shape[2]
    grad_summ = lax.all_to_all(
        after(grad_summ, sums_one).reshape(summ_share, shards, summary_cols).transpose(1, 0, 2),
        "fsdp",
        0,
        0,
        tiled=True,
    )
    summary_grad = grad_summ.reshape(shards * summ_share, summary_cols)[:summary_rows]

    vector_grads = jnp.stack(
        [
            sums_one[0] + gain_summ_grad,
            sums_one[1] + shift_summ_grad,
            whole_columns(query_shift_grad),
            whole_columns(value_shift_grad),
            sums_two[2],
            sums_two[0],
            sums_two[1],
            sums_two[3],
        ]
    )
    vector_grads = vector_grads.reshape(8, devices, rows_held).transpose(1, 0, 2)
    unit_grads = lax.dynamic_update_index_in_dim(
        jnp.zeros((items, shards, units_held), f32),
        up_shift_grad.reshape(items, 1, units_held),
        position,
        1,
    )
    all_grads = jnp.concatenate(
        [vector_grads.reshape(devices, 8 * rows_held), unit_grads.reshape(devices, units_held)],
        axis=1,
    )
    all_grads = jnp.sum(lax.all_to_all(all_grads, BOTH, 0, 0, tiled=True), axis=0)
    (
        gain_one_grad, shift_one_grad, query_shift_grad, value_shift_grad, out_shift_grad,
        gain_two_grad, shift_two_grad, down_shift_grad,
    ) = (all_grads[n * rows_held : (n + 1) * rows_held] for n in range(8))
    up_shift_grad = all_grads[8 * rows_held :]
    return (
        result[None],
        grad_inputs[None],
        summary_grad[None],
        gain_one_grad,
        shift_one_grad,
        query_grad,
        query_shift_grad,
        key_grad,
        value_grad,
        value_shift_grad,
        out_grad,
        out_shift_grad,
        gain_two_grad,
        shift_two_grad,
        up_grad,
        up_shift_grad,
        down_grad,
        down_shift_grad,
    )


def solution(mesh):
    vector = P(BOTH)
    matrix = P(BOTH, None)
    rows = P("dp", "fsdp", None)
    columns = P("dp", None, "fsdp")
    return jax.shard_map(
        per_device,
        mesh=mesh,
        in_specs=(
            rows, columns, P("dp", None), P("dp"), rows, vector, vector, matrix, vector, matrix,
            matrix, vector, matrix, vector, vector, vector, matrix, vector, matrix, vector,
        ),
        out_specs=(
            rows, rows, columns, vector, vector, matrix, vector, matrix, matrix, vector, matrix,
            vector, vector, vector, matrix, vector, matrix, vector,
        ),
        check_vma=False,
    )
```
